32 devices in a mesh: section: 4 (over x, core), dp: 8 (over z, y).
Axes of the slice: x: 2, y: 2, z: 4, core: 2. Of those that a mesh axis runs over, the one named last changes fastest.
Arguments:
- frames_in: bfloat16 [128, 64, 512], P('dp'), may hold values from -6 to 6
- segment_ids: int32 [128, 64], P('dp'), may hold values from 0 to 3, never falling along the last dimension, each value on 1 to 48 neighbouring positions
- cotangent: bfloat16 [128, 64, 512], P('dp'), may hold values from -6 to 6
- w_qkv: float32 [4, 512, 1536], P('section', 'dp'), may hold values from -0.25 to 0.25
- w_out: float32 [4, 512, 512], P('section', 'dp'), may hold values from -0.75 to 0.75
- w_up: float32 [4, 512, 2048], P('section', 'dp'), may hold values from -0.25 to 0.25
- w_down: float32 [4, 2048, 512], P('section', 'dp'), may hold values from -0.1875 to 0.1875
- norm1_gain: float32 [4, 512], P('section', 'dp'), may hold values from 0.1 to 1.9
- norm1_shift: float32 [4, 512], P('section', 'dp'), may hold values from -1.5 to 1.5
- norm2_gain: float32 [4, 512], P('section', 'dp'), may hold values from 0.1 to 1.9
- norm2_shift: float32 [4, 512], P('section', 'dp'), may hold values from -1.5 to 1.5
- up_bias: float32 [4, 2048], P('section', 'dp'), may hold values from -2.5 to 2.5
- down_bias: float32 [4, 512], P('section', 'dp'), may hold values from -1.5 to 1.5
Outputs:
- layer_outputs: float32 [4, 128, 64, 512], P('section', 'dp')
- layer_input_grads: float32 [4, 128, 64, 512], P('section', 'dp')
- grad_qkv: float32 [4, 512, 1536], P('section', 'dp')
- grad_out: float32 [4, 512, 512], P('section', 'dp')
- grad_up: float32 [4, 512, 2048], P('section', 'dp')
- grad_down: float32 [4, 2048, 512], P('section', 'dp')
- grad_norm1_gain: float32 [4, 512], P('section', 'dp')
- grad_norm1_shift: float32 [4, 512], P('section', 'dp')
- grad_norm2_gain: float32 [4, 512], P('section', 'dp')
- grad_norm2_shift: float32 [4, 512], P('section', 'dp')
- grad_up_bias: float32 [4, 2048], P('section', 'dp')
- grad_down_bias: float32 [4, 512], P('section', 'dp')
The draws below stay inside these ranges and needn't reach their ends.
Inputs may be any that keep to these rules, and one draw needn't show every extreme that they name: `segment_ids`: along each row of 64 frames the episode numbers never fall; each episode has 1 to 48 frames.
All inputs are finite; a program needn't handle non-finite values.
Results may differ from the reference program's by a relative error of at most 0.023.
Values may be sent and summed in bfloat16 or wider, within the bound.
No kernel may reach another device: no remote copies, remote signals or barrier semaphores. Data moves between devices by JAX's collectives and lax.ppermute only.
A program may use at most 192 MiB of HBM per device.

```python
import math
import jax
import jax.numpy as jnp
import numpy as np
from jax import lax

D = 512
HEADS = 8
FF = 2048
HEAD_DIM = 64
FRAMES = 64
LAYERS = 4
ROWS_ALL = 128


def raised(entries, rng, source, target, blocks, factor):
    owner, partner = [(jnp.arange(entries.shape[position]) // (entries.shape[position] // blocks)).reshape([-1 if axis == position else 1 for axis in range(entries.ndim)]) for position in (source, target)]
    chosen = jax.random.permutation(rng, blocks)[partner]
    strong = (owner == chosen) | (owner == (partner + blocks // 2) % blocks)
    return jnp.where(strong, factor * entries, entries)


def shard_levels(rng, extent, split, low, high):
    level, own = 1.0, jax.random.fold_in(rng, 6)
    for dim, shards_of in split:
        heights = jnp.exp(jax.random.uniform(jax.random.fold_in(own, dim), (shards_of,), jnp.float32, low / len(split), high / len(split)))
        level = level * jnp.repeat(heights, extent[dim] // shards_of).reshape([-1 if axis == dim else 1 for axis in range(len(extent))])
    return level


def length_profile(number_of, total, most, slope):
    loads = [(1 << 20) // math.isqrt(rank ** slope) + 1 for rank in range(2, number_of + 1)]
    rest, holding = total - most - (number_of - 1), [1] * (number_of - 1)
    while rest > 0:
        free = [i for i in range(number_of - 1) if holding[i] < most]
        mass, remaining = sum([loads[i] for i in free]), rest
        for i in free:
            addition = min(most - holding[i], max(1, remaining * loads[i] // mass), rest)
            holding[i] = holding[i] + addition
            rest = rest - addition
    return np.array([most] + holding)


def ragged_sizes(rng, number_of, total, most, skew):
    if number_of == 2:
        one = jax.random.randint(rng, (), max(1, total - most), min(most, total - 1) + 1)
        return jnp.stack([one, total - one])
    sizes = jnp.asarray(length_profile(number_of, total, most, skew), jnp.int32)
    twos = (number_of - 1) // 2
    giver, receiver = sizes[1:1 + 2 * twos:2], sizes[2:2 + 2 * twos:2]
    room = jnp.minimum(giver - 1, most - receiver)
    shifted = jax.random.randint(jax.random.fold_in(rng, 1), (twos,), 0, 1 << 20) % (room + 1)
    sizes = sizes.at[1:1 + 2 * twos:2].set(giver - shifted).at[2:2 + 2 * twos:2].set(receiver + shifted)
    return sizes[jax.random.permutation(jax.random.fold_in(rng, 2), number_of)]


def centred(rng, dims, deviation, reach, pieces=(), kind=jnp.bfloat16):
    array = deviation * jax.random.normal(rng, dims, jnp.float32)
    if pieces:
        array = array * shard_levels(rng, dims, pieces, -0.22, 0.18)
    return jnp.clip(array, -reach, reach).astype(kind)


def heavy_noise(own_key, extent, scale, bound, pieces, heavy, kind=jnp.bfloat16):
    values = scale * jax.random.normal(own_key, extent, jnp.float32)
    if pieces:
        values = values * shard_levels(own_key, extent, pieces, -0.22, 0.18)
    return jnp.clip(raised(values, jax.random.fold_in(own_key, 3), *heavy), -bound, bound).astype(kind)


def setup_inputs(seed: int = 0) -> dict:
    arg_keys = jax.random.split(jax.random.key(seed), 14)
    return {
        "frames_in": centred(arg_keys[0], (ROWS_ALL, FRAMES, D), 1.0, 6.0, ((0, 8),)),
        "segment_ids": jax.vmap(lambda own: jnp.searchsorted(jnp.cumsum(ragged_sizes(own, 4, FRAMES, 3 * FRAMES // 4, 2)), jnp.arange(FRAMES), side="right"))(jax.random.split(arg_keys[1], ROWS_ALL)).reshape((ROWS_ALL, FRAMES)).astype(jnp.int32),
        "cotangent": heavy_noise(arg_keys[2], (ROWS_ALL, FRAMES, D), 1.0, 6.0, ((0, 8),), (0, 2, 8, 2.0)),
        "w_qkv": centred(arg_keys[3], (LAYERS, D, 3 * D), D ** -0.5, 0.25, ((0, 4), (1, 8)), jnp.float32),
        "w_out": centred(arg_keys[4], (LAYERS, D, D), (D // 8) ** -0.5, 0.75, ((0, 4), (1, 8)), jnp.float32),
        "w_up": centred(arg_keys[5], (LAYERS, D, FF), D ** -0.5, 0.25, ((0, 4), (1, 8)), jnp.float32),
        "w_down": centred(arg_keys[6], (LAYERS, FF, D), (FF // 2) ** -0.5, 0.1875, ((0, 4), (1, 8)), jnp.float32),
        "norm1_gain": jnp.clip(1.0 + 0.18 * jax.random.normal(arg_keys[7], (LAYERS, D), jnp.float32), 0.1, 1.9),
        "norm1_shift": centred(arg_keys[8], (LAYERS, D), 0.3, 1.5, ((0, 4), (1, 8)), jnp.float32),
        "norm2_gain": jnp.clip(1.0 + 0.18 * jax.random.normal(arg_keys[9], (LAYERS, D), jnp.float32), 0.1, 1.9),
        "norm2_shift": centred(arg_keys[10], (LAYERS, D), 0.3, 1.5, ((0, 4), (1, 8)), jnp.float32),
        "up_bias": centred(arg_keys[11], (LAYERS, FF), 0.5, 2.5, ((0, 4), (1, 8)), jnp.float32),
        "down_bias": centred(arg_keys[12], (LAYERS, D), 0.3, 1.5, ((0, 4), (1, 8)), jnp.float32),
    }


@jax.custom_vjp
def low(v):
    return lax.optimization_barrier(v.astype(jnp.bfloat16)).astype(jnp.float32)

@jax.custom_vjp
def low_back(v):
    return v

def low_keep(v):
    return (low(v), None)

def low_pass(kept, grad):
    return (grad,)

def back_keep(v):
    return (v, None)

def back_low(kept, grad):
    return (low(grad),)
low.defvjp(low_keep, low_pass)
low_back.defvjp(back_keep, back_low)

def layer_norm(values, gain, shift):
    center = values - lax.optimization_barrier(jnp.mean(values, axis=-1, keepdims=True))
    spread = lax.optimization_barrier(jnp.mean(center * center, axis=-1, keepdims=True))
    return center * lax.rsqrt(spread + 1e-05) * gain + shift

def allowed_pairs(segments):
    frame_count = segments.shape[1]
    order = jnp.arange(frame_count, dtype=jnp.int32)
    causal = order[None, :] <= order[:, None]
    same = segments[:, :, None] == segments[:, None, :]
    return (causal[None] & same)[:, None]

def transformer_layer(hidden, allowed, layer_params):
    exact = lax.Precision.HIGHEST
    w_qkv, w_out, w_up, w_down, gain_one, shift_one, gain_two, shift_two, up_bias, down_bias = layer_params
    row_count, frame_count, model_width = hidden.shape
    normed = low(layer_norm(hidden, gain_one, shift_one))
    packed = low(low_back(jnp.einsum('rfd,de->rfe', normed, w_qkv, precision=exact)))
    query_heads = packed[..., :model_width].reshape(row_count, frame_count, HEADS, HEAD_DIM)
    key_heads = packed[..., model_width:2 * model_width].reshape(row_count, frame_count, HEADS, HEAD_DIM)
    value_heads = packed[..., 2 * model_width:].reshape(row_count, frame_count, HEADS, HEAD_DIM)
    scores = low_back(jnp.einsum('rqhd,rkhd->rhqk', query_heads, key_heads, precision=exact) * HEAD_DIM ** (-0.5))
    scores = jnp.where(allowed, scores, -1e+30)
    weights_low = low(jax.nn.softmax(scores, axis=-1))
    mixed = low(low_back(jnp.einsum('rhqk,rkhd->rqhd', weights_low, value_heads, precision=exact)))
    mixed = mixed.reshape(row_count, frame_count, model_width)
    middle = hidden + low_back(jnp.einsum('rfd,de->rfe', mixed, w_out, precision=exact))
    normed_two = low(layer_norm(middle, gain_two, shift_two))
    before = low_back(jnp.einsum('rfd,di->rfi', normed_two, w_up, precision=exact) + up_bias)
    activated = low(jax.nn.gelu(before, approximate=True))
    return middle + low_back(jnp.einsum('rfi,id->rfd', activated, w_down, precision=exact) + down_bias)

def reference(frames_in, segment_ids, cotangent, w_qkv, w_out, w_up, w_down, norm1_gain, norm1_shift, norm2_gain, norm2_shift, up_bias, down_bias):
    masters = (w_qkv, w_out, w_up, w_down, norm1_gain, norm1_shift, norm2_gain, norm2_shift, up_bias, down_bias)
    total_rows, frame_count, model_width = frames_in.shape
    group_rows = math.gcd(total_rows, 64)
    group_count = total_rows // group_rows
    layer_count = w_qkv.shape[0]

    def one_group(running, group_index):
        row_start = (group_index * group_rows).astype(jnp.int32)
        inputs = lax.dynamic_slice_in_dim(frames_in, row_start, group_rows, 0).astype(jnp.float32)
        segments = lax.dynamic_slice_in_dim(segment_ids, row_start, group_rows, 0)
        cot_rows = lax.dynamic_slice_in_dim(cotangent, row_start, group_rows, 0).astype(jnp.float32)
        allowed = allowed_pairs(segments)

        def forward(weights, offsets):
            hidden = inputs
            results = []
            for layer_index in range(layer_count):
                if layer_index > 0:
                    hidden = low(low_back(hidden))
                hidden = hidden + offsets[layer_index]
                layer_params = tuple((low(master[layer_index]) for master in weights))
                hidden = transformer_layer(hidden, allowed, layer_params)
                results.append(hidden)
            return (jnp.sum(cot_rows * hidden), jnp.stack(results))
        offsets = jnp.zeros((layer_count, group_rows, frame_count, model_width), jnp.float32)
        loss_value, pullback, stacked = jax.vjp(forward, masters, offsets, has_aux=True)
        weight_grads, input_grads = pullback(jnp.ones_like(loss_value))
        running = tuple((total_item + term_item for total_item, term_item in zip(running, weight_grads)))
        return (running, (stacked, input_grads))
    start_sums = tuple((jnp.zeros_like(master) for master in masters))
    totals, (stacked_all, grads_all) = lax.scan(one_group, start_sums, jnp.arange(group_count, dtype=jnp.int32))
    layer_outputs = jnp.moveaxis(stacked_all, 1, 0).reshape(layer_count, total_rows, frame_count, model_width)
    layer_input_grads = jnp.moveaxis(grads_all, 1, 0).reshape(layer_count, total_rows, frame_count, model_width)
    return (layer_outputs, layer_input_grads, totals[0], totals[1], totals[2], totals[3], totals[4], totals[5], totals[6], totals[7], totals[8], totals[9])
```

```python
import functools

import jax
import jax.numpy as jnp
from jax import lax
from jax.experimental import pallas as pl
from jax.experimental.pallas import tpu as pltpu
from jax.sharding import PartitionSpec as P

HEADS = 8
HEAD_DIM = 64
GROUPS = 8
SMALL_ROWS = 16
BF16 = jnp.bfloat16
F32 = jnp.float32
ANY = pl.BlockSpec(memory_space=pl.ANY)
SMEM = pl.BlockSpec(memory_space=pltpu.SMEM)
MICRO = 2
VMEM_LIMIT = 56 * 1024 * 1024


def dot(left, right):
    return lax.dot_general(left, right, (((1,), (0,)), ((), ())), preferred_element_type=F32)


def dot_rhs_t(left, right):
    return lax.dot_general(left, right, (((1,), (1,)), ((), ())), preferred_element_type=F32)


def dot_lhs_t(left, right):
    return lax.dot_general(left, right, (((0,), (0,)), ((), ())), preferred_element_type=F32)


def copy_weights(meta, own, other, weights, smalls, sems, width):
    part = width // GROUPS
    full = 6 * part

    def spans(piece_index):
        if piece_index < 7:
            return 0, full + SMALL_ROWS
        return (0, 3 * part) if piece_index == 7 else (3 * part, full + SMALL_ROWS)

    def start(ref, low, high, source, block_rows, size, sem):
        a, b = max(source, low), min(source + size, high)
        if a < b:
            target = pl.multiple_of(block_rows + (a - source), 16)
            pltpu.make_async_copy(
                ref.at[pl.ds(a - low, b - a)], weights.at[pl.ds(target, b - a)], sems.at[sem]
            ).start()

    def first_half(refs):
        for index, ref in enumerate(refs):
            low, high = spans(index)
            place = meta[4 + min(index, 7)]
            for block in range(6):
                start(ref, low, high, block * part, block * width + place * part, part, 0 if block < 2 else 3)

    def second_half(refs):
        for index, ref in enumerate(refs):
            low, high = spans(index)
            place = meta[4 + min(index, 7)]
            start(ref, low, high, 0, 6 * width + place * part, part, 1)
            start(ref, low, high, part, 7 * width + place * part, part, 2)
            start(ref, low, high, 2 * part, 8 * width + place * 4 * part, 4 * part, 4)

    for index, ref in enumerate(own):
        low, high = spans(index)
        if high > full:
            slot = min(index, 7)
            pltpu.make_async_copy(ref.at[pl.ds(full - low, SMALL_ROWS)], smalls.at[slot], sems.at[5]).start()

    @pl.when(meta[2] == 0)
    def _():
        first_half(own)
        second_half(other)

    @pl.when(meta[2] != 0)
    def _():
        first_half(other)
        second_half(own)


def wait_rows(weights, sems, sem, low, high):
    pltpu.make_async_copy(weights.at[pl.ds(low, high - low)], weights.at[pl.ds(low, high - low)], sems.at[sem]).wait()


def wait_smalls(smalls, sems):
    pltpu.make_async_copy(smalls, smalls, sems.at[5]).wait()
    total = smalls[0].astype(F32)
    for index in range(1, GROUPS):
        total = total + smalls[index].astype(F32)
    return total


def normalise(values):
    center = values - jnp.mean(values, axis=-1, keepdims=True)
    spread = jnp.mean(center * center, axis=-1, keepdims=True)
    scale = lax.rsqrt(spread + 1e-05)
    return center * scale, scale


def norm_back(grad, gain, unit, scale):
    grad_unit = grad * gain
    mean_grad = jnp.mean(grad_unit, axis=-1, keepdims=True)
    mean_dot = jnp.mean(grad_unit * unit, axis=-1, keepdims=True)
    return scale * (grad_unit - mean_grad - unit * mean_dot)


def stack_heads(pair, low_lanes):
    zero = jnp.zeros_like(pair)
    return jnp.concatenate([jnp.where(low_lanes, pair, zero), jnp.where(low_lanes, zero, pair)], axis=0)


def forward_kernel(n_pieces, source_count, n_saved, *refs):
    meta = refs[0]
    sources = refs[1 : 1 + source_count]
    bias_hbm = refs[1 + source_count]
    at = 2 + source_count
    own, other = refs[at : at + n_pieces], refs[at + n_pieces : at + 2 * n_pieces]
    at += 2 * n_pieces
    at += n_saved
    outs = refs[at : at + 9]
    out_hidden, out_qkv, out_probs, out_mixed, out_middle, out_act, out_slope, out_result, out_low = outs
    (weights, smalls, hidden_v, bias_v, qkv_v, probs_v, mixed_v, middle_v, act_v, slope_v, result_v, low_v,
     sems, in_sems, out_sems) = refs[at + 9 :]
    tokens, width = hidden_v.shape
    hidden_units = act_v.shape[1]
    slot = meta[1]

    @pl.when(meta[0] != 0)
    def _():
        if source_count == 2:

            @pl.when(meta[3] == 0)
            def _():
                pltpu.make_async_copy(sources[0].at[meta[12]], hidden_v, in_sems.at[0]).start()

            @pl.when(meta[3] != 0)
            def _():
                pltpu.make_async_copy(sources[1], hidden_v, in_sems.at[0]).start()

        else:
            pltpu.make_async_copy(sources[0], hidden_v, in_sems.at[0]).start()
        copy_weights(meta, own, other, weights, smalls, sems, width)
        bias_copy = pltpu.make_async_copy(bias_hbm.at[slot], bias_v, in_sems.at[1])
        bias_copy.start()
        pltpu.make_async_copy(hidden_v, hidden_v, in_sems.at[0]).wait()
        saves = []

        def save(index, source, target):
            copy = pltpu.make_async_copy(source, target, out_sems.at[index])
            copy.start()
            saves.append(copy)

        save(0, hidden_v, out_hidden.at[slot])
        small = wait_smalls(smalls, sems)
        gain_one, shift_one, gain_two, shift_two, down_bias = (small[i : i + 1] for i in range(5))
        hidden = hidden_v[...].astype(F32)
        unit, _ = normalise(hidden)
        normed = (unit * gain_one + shift_one).astype(BF16)
        wait_rows(weights, sems, 0, 0, 2 * width)
        qkv_v[:, :width] = (dot(normed, weights[:width]) * HEAD_DIM**-0.5).astype(BF16)
        qkv_v[:, width : 2 * width] = dot(normed, weights[width : 2 * width]).astype(BF16)
        wait_rows(weights, sems, 1, 6 * width, 7 * width)
        qkv_v[:, 2 * width :] = dot(normed, weights[6 * width : 7 * width]).astype(BF16)
        save(1, qkv_v, out_qkv.at[slot])
        bias_copy.wait()
        low_lanes = lax.broadcasted_iota(jnp.int32, (128, 128), 1) < HEAD_DIM
        for group in range(tokens // 128):
            rows = slice(group * 128, group * 128 + 128)
            bias = bias_v[rows]
            bias = jnp.concatenate([bias, bias], axis=0)
            for pair in range(width // 128):
                lanes = pair * 128
                query = stack_heads(qkv_v[rows, lanes : lanes + 128], low_lanes)
                key = qkv_v[rows, width + lanes : width + lanes + 128]
                value = qkv_v[rows, 2 * width + lanes : 2 * width + lanes + 128]
                scores = dot_rhs_t(query, key) + bias
                raised = jnp.exp(scores - jnp.max(scores, axis=-1, keepdims=True))
                probs = (raised * (1.0 / jnp.sum(raised, axis=-1, keepdims=True))).astype(BF16)
                at_row = (group * (width // 128) + pair) * 256
                probs_v[at_row : at_row + 256] = probs
                mixed = dot(probs, value)
                mixed_v[rows, lanes : lanes + 128] = jnp.where(low_lanes, mixed[:128], mixed[128:]).astype(BF16)
        save(2, probs_v, out_probs.at[slot])
        save(3, mixed_v, out_mixed.at[slot])
        wait_rows(weights, sems, 2, 7 * width, 8 * width)
        middle = hidden + dot(mixed_v[...], weights[7 * width : 8 * width])
        middle_v[...] = middle
        save(4, middle_v, out_middle.at[slot])
        unit, _ = normalise(middle)
        normed = (unit * gain_two + shift_two).astype(BF16)
        wait_rows(weights, sems, 3, 2 * width, 6 * width)
        total = middle + down_bias
        for block in range(hidden_units // width):
            lanes = slice(block * width, (block + 1) * width)
            before = dot(normed, weights[(2 + block) * width : (3 + block) * width]) + small[5 + block : 6 + block]
            square = before * before
            tanh = jnp.tanh(before * (0.7978845608028654 + 0.035677408136300125 * square))
            half = 0.5 * tanh + 0.5
            act_v[:, lanes] = (before * half).astype(BF16)
            slope = half + before * (0.5 - 0.5 * (tanh * tanh)) * (0.7978845608028654 + 0.10703222440890037 * square)
            slope_v[:, lanes] = slope.astype(BF16)
            if block == 0:
                wait_rows(weights, sems, 4, 8 * width, 12 * width)
            total = total + dot(act_v[:, lanes], weights[(8 + block) * width : (9 + block) * width])
        result_v[...] = total
        low_v[...] = total.astype(BF16)
        save(8, low_v, out_low)
        save(5, act_v, out_act.at[slot])
        save(6, slope_v, out_slope.at[slot])
        save(7, result_v, out_result.at[slot])
        for copy in saves:
            copy.wait()


def forward_call(meta, sources, bias, own, other, saved, micros, tokens, width, hidden_units):
    wide = 3 * width
    shapes = (
        ((micros, tokens, width), BF16),
        ((micros, tokens, wide), BF16),
        ((micros, tokens * HEADS, 128), BF16),
        ((micros, tokens, width), BF16),
        ((micros, tokens, width), F32),
        ((micros, tokens, hidden_units), BF16),
        ((micros, tokens, hidden_units), BF16),
        ((micros, tokens, width), F32),
        ((tokens, width), BF16),
    )
    saved = () if saved is None else saved
    n_pieces = len(own)
    first_saved = 1 + len(sources) + 1 + 2 * n_pieces
    pieces = (*own, *other)
    flops = 2 * tokens * (4 * width * width + 2 * width * hidden_units) + 4 * tokens * width * 128 * 2
    return pl.pallas_call(
        functools.partial(forward_kernel, n_pieces, len(sources), len(saved)),
        out_shape=tuple(jax.ShapeDtypeStruct(shape, kind) for shape, kind in shapes),
        in_specs=[SMEM] + [ANY] * (len(sources) + 1 + 2 * n_pieces + len(saved)),
        out_specs=tuple([ANY] * 9),
        input_output_aliases={first_saved + i: i for i in range(len(saved))},
        scratch_shapes=[
            pltpu.VMEM((12 * width, width), BF16),
            pltpu.VMEM((GROUPS, SMALL_ROWS, width), BF16),
            pltpu.VMEM((tokens, width), BF16),
            pltpu.VMEM((tokens, 128), F32),
            pltpu.VMEM((tokens, wide), BF16),
            pltpu.VMEM((tokens * HEADS, 128), BF16),
            pltpu.VMEM((tokens, width), BF16),
            pltpu.VMEM((tokens, width), F32),
            pltpu.VMEM((tokens, hidden_units), BF16),
            pltpu.VMEM((tokens, hidden_units), BF16),
            pltpu.VMEM((tokens, width), F32),
            pltpu.VMEM((tokens, width), BF16),
            pltpu.SemaphoreType.DMA((6,)),
            pltpu.SemaphoreType.DMA((2,)),
            pltpu.SemaphoreType.DMA((9,)),
        ],
        compiler_params=pltpu.CompilerParams(vmem_limit_bytes=VMEM_LIMIT),
        cost_estimate=pl.CostEstimate(flops=flops, bytes_accessed=12 * width * width * 2 + tokens * 9000, transcendentals=0),
        name="layer_forward",
    )(meta, *sources, bias, *pieces, *saved)


def backward_kernel(n_pieces, source_count, n_saved, stages, *refs):
    meta = refs[0]
    sources = refs[1 : 1 + source_count]
    at = 1 + source_count
    hidden_hbm, qkv_hbm, probs_hbm, middle_hbm, slope_hbm = refs[at : at + 5]
    at += 5
    own, other = refs[at : at + n_pieces], refs[at + n_pieces : at + 2 * n_pieces]
    at += 2 * n_pieces
    at += n_saved
    outs = refs[at : at + 9]
    (out_upstream, out_du, out_normed_two, out_r1, out_dqkv, out_normed_one, out_sums, out_grad, out_low) = outs
    (weights, smalls, upstream_v, hidden_v, qkv_v, probs_v, middle_v, slope_v, du_v, normed_two_v, r1_v, dqkv_v,
     normed_one_v, sums_v, grad_v, low_v, do_v, sems, in_sems, out_sems) = refs[at + 9 :]
    tokens, width = hidden_v.shape
    hidden_units = slope_v.shape[1]
    slot = meta[1]

    @pl.when(meta[0] != 0)
    def _():
        if source_count == 2:

            @pl.when(meta[3] == stages - 1)
            def _():
                pltpu.make_async_copy(sources[0].at[meta[12]], upstream_v, in_sems.at[0]).start()

            @pl.when(meta[3] != stages - 1)
            def _():
                pltpu.make_async_copy(sources[1], upstream_v, in_sems.at[0]).start()

        else:
            pltpu.make_async_copy(sources[0], upstream_v, in_sems.at[0]).start()
        loads = [
            pltpu.make_async_copy(source.at[slot], target, in_sems.at[1 + i])
            for i, (source, target) in enumerate(
                ((slope_hbm, slope_v), (middle_hbm, middle_v), (qkv_hbm, qkv_v), (probs_hbm, probs_v), (hidden_hbm, hidden_v))
            )
        ]
        loads[0].start()
        copy_weights(meta, own, other, weights, smalls, sems, width)
        for copy in loads[1:]:
            copy.start()
        saves = []

        def save(index, source, target):
            copy = pltpu.make_async_copy(source, target, out_sems.at[index])
            copy.start()
            saves.append(copy)

        pltpu.make_async_copy(upstream_v, upstream_v, in_sems.at[0]).wait()
        save(0, upstream_v, out_upstream.at[slot])
        small = wait_smalls(smalls, sems)
        gain_one, shift_one, gain_two, shift_two = (small[i : i + 1] for i in range(4))
        upstream_low = upstream_v[...]
        upstream = upstream_low.astype(F32)
        sums_v[...] = jnp.zeros_like(sums_v)
        sums_v[4:5] = jnp.sum(upstream, axis=0, keepdims=True)
        loads[0].wait()
        wait_rows(weights, sems, 4, 8 * width, 12 * width)
        wait_rows(weights, sems, 3, 2 * width, 6 * width)
        da = jnp.zeros((tokens, width), F32)
        for block in range(hidden_units // width):
            lanes = slice(block * width, (block + 1) * width)
            dz = dot_rhs_t(upstream_low, weights[(8 + block) * width : (9 + block) * width])
            du = (dz * slope_v[:, lanes].astype(F32)).astype(BF16)
            du_v[:, lanes] = du
            sums_v[5 + block : 6 + block] = jnp.sum(du.astype(F32), axis=0, keepdims=True)
            da = da + dot_rhs_t(du, weights[(2 + block) * width : (3 + block) * width])
        save(1, du_v, out_du.at[slot])
        loads[1].wait()
        unit, scale = normalise(middle_v[...])
        normed_two_v[...] = (unit * gain_two + shift_two).astype(BF16)
        save(2, normed_two_v, out_normed_two.at[slot])
        sums_v[2:3] = jnp.sum(da * unit, axis=0, keepdims=True)
        sums_v[3:4] = jnp.sum(da, axis=0, keepdims=True)
        grad_middle = upstream + norm_back(da, gain_two, unit, scale)
        grad_v[...] = grad_middle
        r1 = grad_middle.astype(BF16)
        r1_v[...] = r1
        save(3, r1_v, out_r1.at[slot])
        wait_rows(weights, sems, 2, 7 * width, 8 * width)
        do_v[...] = dot_rhs_t(r1, weights[7 * width : 8 * width]).astype(BF16)
        loads[2].wait()
        loads[3].wait()
        low_lanes = lax.broadcasted_iota(jnp.int32, (128, 128), 1) < HEAD_DIM
        for group in range(tokens // 128):
            rows = slice(group * 128, group * 128 + 128)
            for pair in range(width // 128):
                lanes = pair * 128
                query = stack_heads(qkv_v[rows, lanes : lanes + 128], low_lanes)
                key = qkv_v[rows, width + lanes : width + lanes + 128]
                value = qkv_v[rows, 2 * width + lanes : 2 * width + lanes + 128]
                grad_mixed = stack_heads(do_v[rows, lanes : lanes + 128], low_lanes)
                at_row = (group * (width // 128) + pair) * 256
                probs = probs_v[at_row : at_row + 256]
                dqkv_v[rows, 2 * width + lanes : 2 * width + lanes + 128] = dot_lhs_t(probs, grad_mixed).astype(BF16)
                grad_probs = dot_rhs_t(grad_mixed, value)
                probs = probs.astype(F32)
                weighted = grad_probs * probs
                grad_scores = (weighted - probs * jnp.sum(weighted, axis=-1, keepdims=True)).astype(BF16)
                dq = dot(grad_scores, key) * HEAD_DIM**-0.5
                dqkv_v[rows, lanes : lanes + 128] = jnp.where(low_lanes, dq[:128], dq[128:]).astype(BF16)
                dqkv_v[rows, width + lanes : width + lanes + 128] = dot_lhs_t(grad_scores, query).astype(BF16)
        save(4, dqkv_v, out_dqkv.at[slot])
        loads[4].wait()
        unit, scale = normalise(hidden_v[...].astype(F32))
        normed_one_v[...] = (unit * gain_one + shift_one).astype(BF16)
        save(5, normed_one_v, out_normed_one.at[slot])
        wait_rows(weights, sems, 0, 0, 2 * width)
        wait_rows(weights, sems, 1, 6 * width, 7 * width)
        da = dot_rhs_t(dqkv_v[:, :width], weights[:width])
        da = da + dot_rhs_t(dqkv_v[:, width : 2 * width], weights[width : 2 * width])
        da = da + dot_rhs_t(dqkv_v[:, 2 * width :], weights[6 * width : 7 * width])
        sums_v[0:1] = jnp.sum(da * unit, axis=0, keepdims=True)
        sums_v[1:2] = jnp.sum(da, axis=0, keepdims=True)
        grad = grad_v[...] + norm_back(da, gain_one, unit, scale)
        grad_v[...] = grad
        low_v[...] = grad.astype(BF16)
        save(8, low_v, out_low)
        save(6, sums_v, out_sums.at[slot])
        save(7, grad_v, out_grad.at[slot])
        for copy in saves:
            copy.wait()


def backward_call(meta, sources, forward_saved, own, other, saved, stages, micros, tokens, width, hidden_units):
    wide = 3 * width
    hidden, qkv, probs, _, middle, _, slope, _, _ = forward_saved
    shapes = (
        ((micros, tokens, width), BF16),
        ((micros, tokens, hidden_units), BF16),
        ((micros, tokens, width), BF16),
        ((micros, tokens, width), BF16),
        ((micros, tokens, wide), BF16),
        ((micros, tokens, width), BF16),
        ((micros, SMALL_ROWS, width), F32),
        ((micros, tokens, width), F32),
        ((tokens, width), BF16),
    )
    saved = () if saved is None else saved
    n_pieces = len(own)
    first_saved = 1 + len(sources) + 5 + 2 * n_pieces
    flops = 2 * tokens * (4 * width * width + 2 * width * hidden_units) + 10 * tokens * width * 128 * 2
    return pl.pallas_call(
        functools.partial(backward_kernel, n_pieces, len(sources), len(saved), stages),
        out_shape=tuple(jax.ShapeDtypeStruct(shape, kind) for shape, kind in shapes),
        in_specs=[SMEM] + [ANY] * (len(sources) + 5 + 2 * n_pieces + len(saved)),
        out_specs=tuple([ANY] * 9),
        input_output_aliases={first_saved + i: i for i in range(len(saved))},
        scratch_shapes=[
            pltpu.VMEM((12 * width, width), BF16),
            pltpu.VMEM((GROUPS, SMALL_ROWS, width), BF16),
            pltpu.VMEM((tokens, width), BF16),
            pltpu.VMEM((tokens, width), BF16),
            pltpu.VMEM((tokens, wide), BF16),
            pltpu.VMEM((tokens * HEADS, 128), BF16),
            pltpu.VMEM((tokens, width), F32),
            pltpu.VMEM((tokens, hidden_units), BF16),
            pltpu.VMEM((tokens, hidden_units), BF16),
            pltpu.VMEM((tokens, width), BF16),
            pltpu.VMEM((tokens, width), BF16),
            pltpu.VMEM((tokens, wide), BF16),
            pltpu.VMEM((tokens, width), BF16),
            pltpu.VMEM((SMALL_ROWS, width), F32),
            pltpu.VMEM((tokens, width), F32),
            pltpu.VMEM((tokens, width), BF16),
            pltpu.VMEM((tokens, width), BF16),
            pltpu.SemaphoreType.DMA((6,)),
            pltpu.SemaphoreType.DMA((6,)),
            pltpu.SemaphoreType.DMA((9,)),
        ],
        compiler_params=pltpu.CompilerParams(vmem_limit_bytes=VMEM_LIMIT),
        cost_estimate=pl.CostEstimate(flops=flops, bytes_accessed=12 * width * width * 2 + tokens * 16000, transcendentals=0),
        name="layer_backward",
    )(meta, *sources, hidden, qkv, probs, middle, slope, *own, *other, *saved)


def weight_kernel(meta, normed_one, mixed, normed_two, act, dqkv, r1, du, upstream, sums, keep, give, first, second, sems):
    micros = normed_one.shape[0]
    width = normed_one.shape[2]
    part = width // GROUPS
    hidden_units = act.shape[2]
    fold = lambda ref: ref[...].reshape(micros * ref.shape[1], ref.shape[2])
    small = sums[0]
    for micro in range(1, micros):
        small = small + sums[micro]
    small = jnp.broadcast_to(small.astype(BF16)[None], (GROUPS, SMALL_ROWS, width))
    first[:, 6 * part :, :] = small
    second[:, 6 * part :, :] = small
    left = fold(normed_one).T
    grads = fold(dqkv)
    for block, (target, row) in enumerate(((first, 0), (first, part), (second, 0))):
        grad = dot(left, grads[:, block * width : (block + 1) * width]).astype(BF16)
        target[:, row : row + part, :] = grad.reshape(GROUPS, part, width)
    grad = dot(fold(mixed).T, fold(r1)).astype(BF16)
    second[:, part : 2 * part, :] = grad.reshape(GROUPS, part, width)
    left = fold(normed_two).T
    for block in range(hidden_units // width):
        right = du[:, :, block * width : (block + 1) * width].reshape(micros * du.shape[1], width)
        grad = dot(left, right).astype(BF16)
        first[:, (2 + block) * part : (3 + block) * part, :] = grad.reshape(GROUPS, part, width)
    right = fold(upstream)
    groups_a_block = GROUPS * width // hidden_units
    for block in range(hidden_units // width):
        piece = act[:, :, block * width : (block + 1) * width].reshape(micros * act.shape[1], width)
        grad = dot(piece.T, right).astype(BF16)
        second[block * groups_a_block : (block + 1) * groups_a_block, 2 * part : 6 * part, :] = grad.reshape(
            groups_a_block, 4 * part, width
        )

    def send(one, two):
        copies = [pltpu.make_async_copy(one, keep, sems.at[0]), pltpu.make_async_copy(two, give, sems.at[1])]
        for copy in copies:
            copy.start()
        for copy in copies:
            copy.wait()

    @pl.when(meta[2] == 0)
    def _():
        send(first, second)

    @pl.when(meta[2] != 0)
    def _():
        send(second, first)


def weight_call(meta, forward_saved, backward_saved, width, hidden_units):
    _, _, _, mixed, _, act, _, _, _ = forward_saved
    upstream, du, normed_two, r1, dqkv, normed_one, sums, _, _ = backward_saved
    part = width // GROUPS
    shape = jax.ShapeDtypeStruct((GROUPS, 6 * part + SMALL_ROWS, width), BF16)
    tokens = mixed.shape[0] * mixed.shape[1]
    whole = pl.BlockSpec(memory_space=pltpu.VMEM)
    return pl.pallas_call(
        weight_kernel,
        out_shape=(shape, shape),
        in_specs=[SMEM] + [whole] * 9,
        out_specs=(ANY, ANY),
        scratch_shapes=[
            pltpu.VMEM(shape.shape, BF16),
            pltpu.VMEM(shape.shape, BF16),
            pltpu.SemaphoreType.DMA((2,)),
        ],
        compiler_params=pltpu.CompilerParams(vmem_limit_bytes=VMEM_LIMIT),
        cost_estimate=pl.CostEstimate(
            flops=24 * tokens * width * width, bytes_accessed=12 * width * width * 2 + tokens * 16000, transcendentals=0
        ),
        name="weight_grads",
    )(meta, normed_one, mixed, normed_two, act, dqkv, r1, du, upstream, sums)


CYCLE = (0, 2, 4, 6, 7, 5, 3, 1)
OFFSETS = (0, -1, 1, -2, 2, -3, 3, 4)


def to_core(value):
    count = lax.axis_size("section")
    return lax.ppermute(value, "section", [(i, i ^ 1) for i in range(count)])


def to_stage(value, by):
    count = lax.axis_size("section")
    return lax.ppermute(value, "section", [(i, i + 2 * by) for i in range(count) if 0 <= i + 2 * by < count])


def along(value, by):
    size = len(CYCLE)
    return lax.ppermute(value, "dp", [(CYCLE[i], CYCLE[(i + by) % size]) for i in range(size)])


def ring_gather(piece, cut):
    ahead, behind, pieces = piece, piece, [piece]
    for _ in range(3):
        ahead, behind = along(ahead, 1), along(behind, -1)
        pieces += [ahead, behind]
    return pieces + [along(ahead[:cut], 1), along(behind[cut:], -1)]


def ring_scatter(keep, got, order, cut):
    def own(offset):
        place = order[OFFSETS.index(offset)]
        mine, theirs = (lax.dynamic_index_in_dim(part, place, 0, keepdims=False) for part in (keep, got))
        return mine.astype(F32) + theirs.astype(F32)

    far = own(4).astype(BF16)
    ahead, behind = along(far[:cut], 1), along(far[cut:], -1)
    for step in (3, 2, 1):
        front, back = own(step), own(-step)
        if step == 3:
            front = jnp.concatenate([front[:cut] + ahead.astype(F32), front[cut:]])
            back = jnp.concatenate([back[:cut], back[cut:] + behind.astype(F32)])
        else:
            front, back = front + ahead.astype(F32), back + behind.astype(F32)
        ahead, behind = along(front.astype(BF16), 1), along(back.astype(BF16), -1)
    return own(0) + ahead.astype(F32) + behind.astype(F32)


def placed_row(shard, dp_index, dp_count):
    full = jnp.zeros((shard.shape[0] * dp_count,), BF16)
    return lax.dynamic_update_slice(full, shard, (dp_index * shard.shape[0],))


def on_device(
    frames_in,
    segment_ids,
    cotangent,
    w_qkv,
    w_out,
    w_up,
    w_down,
    norm1_gain,
    norm1_shift,
    norm2_gain,
    norm2_shift,
    up_bias,
    down_bias,
):
    section = lax.axis_index("section")
    stages = lax.axis_size("section") // 2
    core, stage = section % 2, section // 2
    dp_index, dp_count = lax.axis_index("dp"), lax.axis_size("dp")
    rows, frame_count, width = frames_in.shape
    hidden_units = w_up.shape[2]
    own_rows = rows // 2
    tokens = own_rows * frame_count // MICRO
    ring = dp_count == len(CYCLE)
    part = w_qkv.shape[1]
    cut = 3 * width // GROUPS

    shard_qkv, shard_out, shard_up, shard_down = (w[0].astype(BF16) for w in (w_qkv, w_out, w_up, w_down))
    rows_of = [
        placed_row(vector[0].astype(BF16), dp_index, dp_count).reshape(-1, width)
        for vector in (norm1_gain, norm1_shift, norm2_gain, norm2_shift, down_bias, up_bias)
    ]
    small = jnp.concatenate(rows_of + [jnp.zeros((SMALL_ROWS - 5 - hidden_units // width, width), BF16)])
    first_half = [shard_qkv[:, :width], shard_qkv[:, width : 2 * width]]
    first_half += [shard_up[:, i * width : (i + 1) * width] for i in range(hidden_units // width)]
    second_half = [shard_qkv[:, 2 * width :], shard_out, shard_down]
    is_first = core == 0
    if ring:
        first_half = jnp.concatenate(first_half + [small])
        second_half = jnp.concatenate(second_half + [small])
        swapped = to_core(jnp.where(is_first, second_half, first_half))
        layers = []
        for start in (jnp.where(is_first, first_half, swapped), jnp.where(is_first, swapped, second_half)):
            own = ring_gather(start, cut)
            layers.append((tuple(own), tuple(to_core(piece) for piece in own)))
        place = jnp.asarray([CYCLE.index(i) for i in range(dp_count)], jnp.int32)[dp_index]
        order = [jnp.asarray(CYCLE, jnp.int32)[(place + offset) % dp_count] for offset in OFFSETS]
        holder = core
    else:
        gathered = [lax.all_gather(block, "dp", axis=0, tiled=True) for block in first_half + second_half]
        small = lax.psum(small.astype(F32), "dp").astype(BF16)

        def split(blocks):
            pieces = []
            for i in range(GROUPS):
                cuts = [block[i * block.shape[0] // GROUPS : (i + 1) * block.shape[0] // GROUPS] for block in blocks]
                pieces.append(jnp.concatenate(cuts + [small if i == 0 else jnp.zeros_like(small)]))
            return pieces[:-1] + [pieces[-1][:cut], pieces[-1][cut:]]

        mine = (split(gathered[: len(first_half)]), split(gathered[len(first_half) :]))
        theirs = jax.tree.map(to_core, mine)
        pick = lambda one, two: jax.tree.map(lambda a, b: jnp.where(is_first, a, b), one, two)
        layers = [pick(mine, theirs), pick(theirs, mine)]
        order = [jnp.int32(i) for i in range(GROUPS)]
        holder = jnp.int32(0)

    pair_rows = 128 // frame_count
    segments = lax.dynamic_slice_in_dim(segment_ids, core * own_rows, own_rows, 0).reshape(-1, 128)
    spot = jnp.arange(128, dtype=jnp.int32)
    allowed = (spot[None, :] <= spot[:, None]) & (spot[None, :] // frame_count == spot[:, None] // frame_count)
    allowed = allowed[None] & (segments[:, :, None] == segments[:, None, :])
    bias = jnp.where(allowed, 0.0, -1e30).astype(F32).reshape(MICRO, tokens, 128)
    frames = frames_in.reshape(2 * MICRO, tokens, width)
    last_grads = cotangent.reshape(2 * MICRO, tokens, width)

    def meta(micro):
        active = ((micro >= 0) & (micro < MICRO)).astype(jnp.int32)
        slot = jnp.clip(micro, 0, MICRO - 1)
        return jnp.stack([active, slot, holder, stage, *order, core * MICRO + slot]).astype(jnp.int32)

    sizes = (MICRO, tokens, width, hidden_units)
    first_saved = second_saved = None
    incoming = jnp.zeros((tokens, width), BF16)
    for tick in range(MICRO + stages - 1):
        facts = meta(tick - stage)
        first_saved = forward_call(facts, (frames, incoming), bias, *layers[0], first_saved, *sizes)
        second_saved = forward_call(facts, (first_saved[8],), bias, *layers[1], second_saved, *sizes)
        if tick + 1 < MICRO + stages - 1:
            incoming = to_stage(second_saved[8], 1)
    first_back = second_back = None
    incoming = jnp.zeros((tokens, width), BF16)
    for tick in range(MICRO + stages - 1):
        facts = meta(tick - (stages - 1 - stage))
        second_back = backward_call(facts, (last_grads, incoming), second_saved, *layers[1], second_back, stages, *sizes)
        first_back = backward_call(facts, (second_back[8],), first_saved, *layers[0], first_back, stages, *sizes)
        if tick + 1 < MICRO + stages - 1:
            incoming = to_stage(first_back[8], -1)

    facts = meta(jnp.int32(0))
    totals = []
    for forward_saved, backward_saved in ((second_saved, second_back), (first_saved, first_back)):
        keep, give = weight_call(facts, forward_saved, backward_saved, width, hidden_units)
        if ring:
            totals.append(ring_scatter(keep, to_core(give), order, cut))
        else:
            totals.append((keep, give))
    total_second, total_first = totals
    if ring:
        theirs = to_core(jnp.where(is_first, total_second, total_first))
        mine = jnp.where(is_first, total_first, total_second)
        one = jnp.where(is_first, mine, theirs)
        two = jnp.where(is_first, theirs, mine)
        small = mine[6 * part :]
        first_grads = [one[i * part : (i + 1) * part] for i in range(6)]
        second_grads = [two[:part], two[part : 2 * part], two[2 * part : 6 * part]]
    else:
        theirs = jax.tree.map(lambda a, b: to_core(jnp.where(is_first, a, b)), total_second, total_first)
        one, two = jax.tree.map(
            lambda a, b, c: jnp.where(is_first, b, a).astype(F32) + c.astype(F32), total_second, total_first, theirs
        )
        small = lax.psum(one[0, 6 * width // GROUPS :], "dp")
        block = width // GROUPS
        natural = lambda half, low, high: lax.psum_scatter(
            half[:, low * block : high * block].reshape(-1, width), "dp", scatter_dimension=0, tiled=True
        )
        first_grads = [natural(one, i, i + 1) for i in range(6)]
        second_grads = [natural(two, 0, 1), natural(two, 1, 2), natural(two, 2, 6)]
    vectors = [
        lax.dynamic_slice_in_dim(small[i : i + 1].reshape(-1), dp_index * part, part) for i in range(5)
    ]
    grad_up_bias = lax.dynamic_slice_in_dim(
        small[5 : 5 + hidden_units // width].reshape(-1), dp_index * up_bias.shape[1], up_bias.shape[1]
    )

    def whole(first_rows, second_rows):
        theirs = to_core(jnp.where(is_first, second_rows, first_rows))
        mine = jnp.where(is_first, first_rows, second_rows)
        both = jnp.where(is_first, jnp.stack([mine, theirs]), jnp.stack([theirs, mine]))
        return both.reshape(1, rows, frame_count, width)

    return (
        whole(first_saved[7], second_saved[7]),
        whole(first_back[7], second_back[7]),
        jnp.concatenate([first_grads[0], first_grads[1], second_grads[0]], axis=1)[None],
        second_grads[1][None],
        jnp.concatenate(first_grads[2:], axis=1)[None],
        second_grads[2][None],
        *(vector[None] for vector in vectors[:4]),
        grad_up_bias[None],
        vectors[4][None],
    )


def solution(mesh):
    rows = P("dp", None, None)
    matrix, vector = P("section", "dp", None), P("section", "dp")
    result = P("section", "dp", None, None)
    return jax.shard_map(
        on_device,
        mesh=mesh,
        in_specs=(rows, P("dp", None), rows) + (matrix,) * 4 + (vector,) * 6,
        out_specs=(result, result) + (matrix,) * 4 + (vector,) * 6,
        check_vma=False,
    )
```

```python
import functools

import jax
import jax.numpy as jnp
import numpy as np
from jax import lax
from jax.experimental import pallas as pl
from jax.experimental.pallas import tpu as pltpu
from jax.sharding import PartitionSpec as P

HEADS = 8
HEAD_DIM = 64
GROUPS = 8
SMALL_ROWS = 16
MICRO = 2
BF16 = jnp.bfloat16
F32 = jnp.float32
ANY = pl.BlockSpec(memory_space=pltpu.HBM)
SMEM = pl.BlockSpec(memory_space=pltpu.SMEM)
VMEM = pl.BlockSpec(memory_space=pltpu.VMEM)
VMEM_LIMIT = 16 * 1024 * 1024
RUNS, SLOT, CORE, STAGE, ORDER, ROWS = 0, 1, 2, 3, 4, 12
PLACE = 13
FACTS = 16


def layout(width, hidden_units):
    sizes = dict(hidden=1, qkv=3, probs=HEADS * 128 // width, mixed=1, middle=2, act=hidden_units // width,
                 slope=hidden_units // width, result=1, upstream=1, normed_two=1, r1=1, normed_one=1, grad=1)
    spans, at = {}, 0
    for name, size in sizes.items():
        spans[name] = slice(at, at + size * width)
        at += size * width
    return spans, at


def columns(state, slot, spans, name):
    return state.at[slot, :, spans[name]]


def dot(left, right):
    return lax.dot_general(left, right, (((1,), (0,)), ((), ())), preferred_element_type=F32)


def dot_rhs_t(left, right):
    return lax.dot_general(left, right, (((1,), (1,)), ((), ())), preferred_element_type=F32)


def dot_lhs_t(left, right):
    return lax.dot_general(left, right, (((0,), (0,)), ((), ())), preferred_element_type=F32)


def params():
    return pltpu.CompilerParams(vmem_limit_bytes=VMEM_LIMIT)


def gather_kernel(places, has_weights, *refs):
    facts = refs[0]
    count = len(places)
    own, other = refs[1 : 1 + count], refs[1 + count : 1 + 2 * count]
    at = 1 + 2 * count + (2 if has_weights else 0)
    weights, small, arrived, sems = refs[at : at + 4]
    width = weights.shape[1]
    part = width // GROUPS
    full = 6 * part

    def move(refs, is_first):
        for ref, (place, low, high) in zip(refs, places):
            source = facts[0, ORDER + place]
            if is_first:
                spans = [(i * part, part, i * width, part) for i in range(6)]
            else:
                spans = [(0, part, 6 * width, part), (part, part, 7 * width, part), (2 * part, 4 * part, 8 * width, 4 * part)]
            for start, size, block, step in spans:
                a, b = max(start, low), min(start + size, high)
                if a < b:
                    target = pl.multiple_of(block + source * step + (a - start), 16)
                    pltpu.make_async_copy(
                        ref.at[pl.ds(a - low, b - a)], weights.at[pl.ds(target, b - a)], sems.at[0]
                    ).start()

    moved = sum(min(high, full) - low for _, low, high in places)
    copies = []
    for ref, (place, low, high) in zip(own, places):
        if high > full:
            copies.append(pltpu.make_async_copy(ref.at[pl.ds(full - low, SMALL_ROWS)], arrived.at[len(copies)], sems.at[1]))
            copies[-1].start()

    @pl.when(facts[0, CORE] == 0)
    def _():
        move(own, True)
        move(other, False)

    @pl.when(facts[0, CORE] != 0)
    def _():
        move(other, True)
        move(own, False)

    for copy in copies:
        copy.wait()
    total = small[...] if has_weights else jnp.zeros(small.shape, F32)
    for index in range(len(copies)):
        total = total + arrived[index].astype(F32)
    small[...] = total
    whole = weights.at[pl.ds(0, moved)]
    for _ in range(2):
        pltpu.make_async_copy(whole, whole, sems.at[0]).wait()


def gather_call(facts, places, own, other, held, width):
    held = () if held is None else held
    count = 2 * len(own)
    return pl.pallas_call(
        functools.partial(gather_kernel, places, bool(held)),
        out_shape=(pltpu.VMEM((12 * width, width), BF16), pltpu.VMEM((SMALL_ROWS, width), F32)),
        in_specs=[SMEM] + [ANY] * count + [VMEM] * len(held),
        out_specs=(VMEM, VMEM),
        input_output_aliases={1 + count + i: i for i in range(len(held))},
        scratch_shapes=[pltpu.VMEM((GROUPS, SMALL_ROWS, width), BF16), pltpu.SemaphoreType.DMA((2,))],
        compiler_params=params(),
        name="lay_out_weights",
    )(facts, *own, *other, *held)


def normalise(values):
    center = values - jnp.mean(values, axis=-1, keepdims=True)
    spread = jnp.mean(center * center, axis=-1, keepdims=True)
    scale = lax.rsqrt(spread + 1e-05)
    return center * scale, scale


def norm_back(grad, gain, unit, scale):
    grad_unit = grad * gain
    mean_grad = jnp.mean(grad_unit, axis=-1, keepdims=True)
    mean_dot = jnp.mean(grad_unit * unit, axis=-1, keepdims=True)
    return scale * (grad_unit - mean_grad - unit * mean_dot)


def stack_heads(pair, low_lanes):
    zero = jnp.zeros_like(pair)
    return jnp.concatenate([jnp.where(low_lanes, pair, zero), jnp.where(low_lanes, zero, pair)], axis=0)


def load_source(facts, call, sources, sliced, target, sem):
    for stage, (source, is_sliced) in enumerate(zip(sources, sliced)):
        if source is None:
            continue

        @pl.when(facts[call, STAGE] == stage)
        def _():
            ref = source.at[facts[call, ROWS]] if is_sliced else source
            pltpu.make_async_copy(ref, target, sem).start()


def forward_kernel(call, sliced, present, has_state, hidden_units, *refs):
    facts = refs[0]
    at = 1
    sources = []
    for is_present in present:
        sources.append(refs[at] if is_present else None)
        at += int(is_present)
    bias_v, weights, small = refs[at : at + 3]
    state, low_o, sem = refs[at + 3 + int(has_state) :]
    width = weights.shape[1]
    tokens = state.shape[1]
    spans, _ = layout(width, hidden_units)
    slot = facts[call, SLOT]

    @pl.when(facts[call, RUNS] != 0)
    def _():
        hidden_v, qkv_v, probs_v, mixed_v, middle_v, act_v, slope_v, result_v = (
            columns(state, slot, spans, name)
            for name in ("hidden", "qkv", "probs", "mixed", "middle", "act", "slope", "result")
        )
        load_source(facts, call, sources, sliced, hidden_v, sem)
        gain_one, shift_one, gain_two, shift_two, down_bias = (small[i : i + 1] for i in range(5))
        pltpu.make_async_copy(hidden_v, hidden_v, sem).wait()
        hidden = hidden_v[...].astype(F32)
        unit, _ = normalise(hidden)
        normed = (unit * gain_one + shift_one).astype(BF16)
        qkv_v[:, :width] = (dot(normed, weights[:width]) * HEAD_DIM**-0.5).astype(BF16)
        qkv_v[:, width : 2 * width] = dot(normed, weights[width : 2 * width]).astype(BF16)
        qkv_v[:, 2 * width :] = dot(normed, weights[6 * width : 7 * width]).astype(BF16)
        low_lanes = lax.broadcasted_iota(jnp.int32, (128, 128), 1) < HEAD_DIM
        for group in range(tokens // 128):
            rows = slice(group * 128, group * 128 + 128)
            bias = bias_v[slot, rows]
            bias = jnp.concatenate([bias, bias], axis=0)
            for pair in range(width // 128):
                lanes = pair * 128
                query = stack_heads(qkv_v[rows, lanes : lanes + 128], low_lanes)
                key = qkv_v[rows, width + lanes : width + lanes + 128]
                value = qkv_v[rows, 2 * width + lanes : 2 * width + lanes + 128]
                scores = dot_rhs_t(query, key) + bias
                raised = jnp.exp(scores - jnp.max(scores, axis=-1, keepdims=True))
                probs = (raised * (1.0 / jnp.sum(raised, axis=-1, keepdims=True))).astype(BF16)
                probs_v[rows, 2 * lanes : 2 * lanes + 128] = probs[:128]
                probs_v[rows, 2 * lanes + 128 : 2 * lanes + 256] = probs[128:]
                mixed = dot(probs, value)
                mixed_v[rows, lanes : lanes + 128] = jnp.where(low_lanes, mixed[:128], mixed[128:]).astype(BF16)
        middle = hidden + dot(mixed_v[...], weights[7 * width : 8 * width])
        high = middle.astype(BF16)
        middle_v[:, :width] = high
        middle_v[:, width:] = (middle - high.astype(F32)).astype(BF16)
        unit, _ = normalise(middle)
        normed = (unit * gain_two + shift_two).astype(BF16)
        total = middle + down_bias
        for block in range(hidden_units // width):
            lanes = slice(block * width, (block + 1) * width)
            before = dot(normed, weights[(2 + block) * width : (3 + block) * width]) + small[5 + block : 6 + block]
            square = before * before
            tanh = jnp.tanh(before * (0.7978845608028654 + 0.035677408136300125 * square))
            half = 0.5 * tanh + 0.5
            act_v[:, lanes] = (before * half).astype(BF16)
            slope = half + before * (0.5 - 0.5 * (tanh * tanh)) * (0.7978845608028654 + 0.10703222440890037 * square)
            slope_v[:, lanes] = slope.astype(BF16)
            total = total + dot(act_v[:, lanes], weights[(8 + block) * width : (9 + block) * width])
        low = total.astype(BF16)
        low_o[...] = low
        result_v[...] = low


def forward_call(call, facts, sources, sliced, bias, held, state, micros, tokens, width, hidden_units):
    given = [source for source in sources if source is not None]
    state = [] if state is None else [state]
    flops = 2 * tokens * (4 * width * width + 2 * width * hidden_units) + 4 * tokens * width * 128 * 2
    return pl.pallas_call(
        functools.partial(forward_kernel, call, sliced, tuple(s is not None for s in sources), bool(state), hidden_units),
        out_shape=(
            pltpu.VMEM((micros, tokens, layout(width, hidden_units)[1]), BF16),
            jax.ShapeDtypeStruct((tokens, width), BF16),
        ),
        in_specs=[SMEM] + [ANY] * len(given) + [VMEM] * (3 + len(state)),
        out_specs=(VMEM, VMEM),
        input_output_aliases={4 + len(given): 0} if state else {},
        scratch_shapes=[pltpu.SemaphoreType.DMA],
        compiler_params=params(),
        cost_estimate=pl.CostEstimate(flops=flops, bytes_accessed=tokens * 4 * width, transcendentals=0),
        name="layer_forward",
    )(facts, *given, bias, *held, *state)


def backward_kernel(call, sliced, present, has_sums, hidden_units, *refs):
    facts = refs[0]
    at = 1
    sources = []
    for is_present in present:
        sources.append(refs[at] if is_present else None)
        at += int(is_present)
    weights, small = refs[at : at + 2]
    state, sums_o, low_o, grad_v, do_v, sem = refs[at + 3 + int(has_sums) :]
    width = weights.shape[1]
    tokens = state.shape[1]
    spans, _ = layout(width, hidden_units)
    slot = facts[call, SLOT]

    @pl.when(facts[call, RUNS] != 0)
    def _():
        hidden_v, qkv_v, probs_v, middle_v, du_v, upstream_v, normed_two_v, r1_v, normed_one_v, out_v = (
            columns(state, slot, spans, name)
            for name in (
                "hidden", "qkv", "probs", "middle", "slope", "upstream", "normed_two", "r1", "normed_one", "grad"
            )
        )
        sums_v = sums_o.at[slot]
        load_source(facts, call, sources, sliced, upstream_v, sem)
        gain_one, shift_one, gain_two, shift_two = (small[i : i + 1] for i in range(4))
        sums_v[...] = jnp.zeros(sums_v.shape, F32)
        pltpu.make_async_copy(upstream_v, upstream_v, sem).wait()
        upstream_low = upstream_v[...]
        upstream = upstream_low.astype(F32)
        sums_v[4:5] = jnp.sum(upstream, axis=0, keepdims=True)
        da = jnp.zeros((tokens, width), F32)
        for block in range(hidden_units // width):
            lanes = slice(block * width, (block + 1) * width)
            dz = dot_rhs_t(upstream_low, weights[(8 + block) * width : (9 + block) * width])
            du = (dz * du_v[:, lanes].astype(F32)).astype(BF16)
            du_v[:, lanes] = du
            sums_v[5 + block : 6 + block] = jnp.sum(du.astype(F32), axis=0, keepdims=True)
            da = da + dot_rhs_t(du, weights[(2 + block) * width : (3 + block) * width])
        unit, scale = normalise(middle_v[:, :width].astype(F32) + middle_v[:, width:].astype(F32))
        normed_two_v[...] = (unit * gain_two + shift_two).astype(BF16)
        sums_v[2:3] = jnp.sum(da * unit, axis=0, keepdims=True)
        sums_v[3:4] = jnp.sum(da, axis=0, keepdims=True)
        grad_middle = upstream + norm_back(da, gain_two, unit, scale)
        grad_v[...] = grad_middle
        r1 = grad_middle.astype(BF16)
        r1_v[...] = r1
        do_v[...] = dot_rhs_t(r1, weights[7 * width : 8 * width]).astype(BF16)
        low_lanes = lax.broadcasted_iota(jnp.int32, (128, 128), 1) < HEAD_DIM
        for group in range(tokens // 128):
            rows = slice(group * 128, group * 128 + 128)
            for pair in range(width // 128):
                lanes = slice(pair * 128, pair * 128 + 128)
                key_lanes = slice(width + pair * 128, width + pair * 128 + 128)
                value_lanes = slice(2 * width + pair * 128, 2 * width + pair * 128 + 128)
                query = stack_heads(qkv_v[rows, lanes], low_lanes)
                key = qkv_v[rows, key_lanes]
                value = qkv_v[rows, value_lanes]
                grad_mixed = stack_heads(do_v[rows, lanes], low_lanes)
                probs = jnp.concatenate(
                    [probs_v[rows, pair * 256 : pair * 256 + 128], probs_v[rows, pair * 256 + 128 : pair * 256 + 256]], axis=0
                )
                qkv_v[rows, value_lanes] = dot_lhs_t(probs, grad_mixed).astype(BF16)
                grad_probs = dot_rhs_t(grad_mixed, value)
                probs = probs.astype(F32)
                weighted = grad_probs * probs
                grad_scores = (weighted - probs * jnp.sum(weighted, axis=-1, keepdims=True)).astype(BF16)
                dq = dot(grad_scores, key) * HEAD_DIM**-0.5
                qkv_v[rows, lanes] = jnp.where(low_lanes, dq[:128], dq[128:]).astype(BF16)
                qkv_v[rows, key_lanes] = dot_lhs_t(grad_scores, query).astype(BF16)
        unit, scale = normalise(hidden_v[...].astype(F32))
        normed_one_v[...] = (unit * gain_one + shift_one).astype(BF16)
        da = dot_rhs_t(qkv_v[:, :width], weights[:width])
        da = da + dot_rhs_t(qkv_v[:, width : 2 * width], weights[width : 2 * width])
        da = da + dot_rhs_t(qkv_v[:, 2 * width :], weights[6 * width : 7 * width])
        sums_v[0:1] = jnp.sum(da * unit, axis=0, keepdims=True)
        sums_v[1:2] = jnp.sum(da, axis=0, keepdims=True)
        low = (grad_v[...] + norm_back(da, gain_one, unit, scale)).astype(BF16)
        low_o[...] = low
        out_v[...] = low


def backward_call(call, facts, sources, sliced, held, state, sums, micros, tokens, width, hidden_units):
    given = [source for source in sources if source is not None]
    at = 3 + len(given)
    sums = [] if sums is None else [sums]
    flops = 2 * tokens * (4 * width * width + 2 * width * hidden_units) + 10 * tokens * width * 128 * 2
    return pl.pallas_call(
        functools.partial(backward_kernel, call, sliced, tuple(s is not None for s in sources), bool(sums), hidden_units),
        out_shape=(
            pltpu.VMEM(state.shape, BF16),
            pltpu.VMEM((micros, SMALL_ROWS, width), F32),
            jax.ShapeDtypeStruct((tokens, width), BF16),
        ),
        in_specs=[SMEM] + [ANY] * len(given) + [VMEM] * (3 + len(sums)),
        out_specs=(VMEM, VMEM, VMEM),
        input_output_aliases={at + i: i for i in range(1 + len(sums))},
        scratch_shapes=[pltpu.VMEM((tokens, width), F32), pltpu.VMEM((tokens, width), BF16), pltpu.SemaphoreType.DMA],
        compiler_params=params(),
        cost_estimate=pl.CostEstimate(flops=flops, bytes_accessed=tokens * 4 * width, transcendentals=0),
        name="layer_backward",
    )(facts, *given, *held, state, *sums)


def weight_kernel(hidden_units, facts, state, sums, keep, give, first, second, sems):
    micros, tokens, _ = state.shape
    width = sums.shape[2]
    part = width // GROUPS
    spans, _ = layout(width, hidden_units)

    def fold(name, block=0):
        at = spans[name].start + block * width
        return state[:, :, at : at + width].reshape(micros * tokens, width)

    small = sums[0]
    for micro in range(1, micros):
        small = small + sums[micro]
    small = jnp.broadcast_to(small.astype(BF16)[None], (GROUPS, SMALL_ROWS, width))
    first[:, 6 * part :, :] = small
    second[:, 6 * part :, :] = small
    left = fold("normed_one").T
    for block, (target, row) in enumerate(((first, 0), (first, part), (second, 0))):
        target[:, row : row + part, :] = dot(left, fold("qkv", block)).astype(BF16).reshape(GROUPS, part, width)
    second[:, part : 2 * part, :] = dot(fold("mixed").T, fold("r1")).astype(BF16).reshape(GROUPS, part, width)
    left = fold("normed_two").T
    for block in range(hidden_units // width):
        grad = dot(left, fold("slope", block)).astype(BF16)
        first[:, (2 + block) * part : (3 + block) * part, :] = grad.reshape(GROUPS, part, width)
    right = fold("upstream")
    of_block = GROUPS * width // hidden_units
    for block in range(hidden_units // width):
        grad = dot(fold("act", block).T, right).astype(BF16)
        second[block * of_block : (block + 1) * of_block, 2 * part : 6 * part, :] = grad.reshape(of_block, 4 * part, width)

    def send(one, two):
        copies = [pltpu.make_async_copy(one, keep, sems.at[0]), pltpu.make_async_copy(two, give, sems.at[1])]
        for copy in copies:
            copy.start()
        for copy in copies:
            copy.wait()

    @pl.when(facts[0, CORE] == 0)
    def _():
        send(first, second)

    @pl.when(facts[0, CORE] != 0)
    def _():
        send(second, first)


def weight_call(facts, state, sums, width, hidden_units):
    part = width // GROUPS
    shape = (GROUPS, 6 * part + SMALL_ROWS, width)
    tokens = state.shape[0] * state.shape[1]
    return pl.pallas_call(
        functools.partial(weight_kernel, hidden_units),
        out_shape=(jax.ShapeDtypeStruct(shape, BF16),) * 2,
        in_specs=[SMEM, VMEM, VMEM],
        out_specs=(ANY, ANY),
        scratch_shapes=[pltpu.VMEM(shape, BF16), pltpu.VMEM(shape, BF16), pltpu.SemaphoreType.DMA((2,))],
        compiler_params=params(),
        cost_estimate=pl.CostEstimate(flops=24 * tokens * width * width, bytes_accessed=24 * width * width, transcendentals=0),
        name="weight_grads",
    )(facts, state, sums)


def halves_kernel(facts, w_qkv, w_out, w_up, w_down, *refs):
    vectors, (first, second) = refs[:6], refs[6:]
    part, width = w_out.shape[1:]
    for i in range(2):
        first[i * part : (i + 1) * part] = w_qkv[0, :, i * width : (i + 1) * width].astype(BF16)
    for i in range(w_up.shape[2] // width):
        first[(2 + i) * part : (3 + i) * part] = w_up[0, :, i * width : (i + 1) * width].astype(BF16)
    second[:part] = w_qkv[0, :, 2 * width :].astype(BF16)
    second[part : 2 * part] = w_out[0].astype(BF16)
    second[2 * part : 6 * part] = w_down[0].astype(BF16)
    lane = lax.broadcasted_iota(jnp.int32, (1, width), 1)
    rows = []
    for vector in vectors:
        size = vector.shape[1]
        spread = jnp.concatenate([vector[...]] * (width // size), axis=1)
        for row in range(size * GROUPS // width):
            rows.append(jnp.where((lane + row * width) // size == facts[0, PLACE], spread, 0.0))
    rows.append(jnp.zeros((SMALL_ROWS - len(rows), width), F32))
    small = jnp.concatenate(rows, axis=0).astype(BF16)
    first[6 * part :] = small
    second[6 * part :] = small


def halves_call(facts, matrices, vectors):
    _, part, width = matrices[1].shape
    shape = jax.ShapeDtypeStruct((6 * part + SMALL_ROWS, width), BF16)
    return pl.pallas_call(
        halves_kernel,
        out_shape=(shape, shape),
        in_specs=[SMEM] + [VMEM] * (len(matrices) + len(vectors)),
        out_specs=(VMEM, VMEM),
        compiler_params=params(),
        name="round_shard",
    )(facts, *matrices, *vectors)


CYCLE = (0, 2, 4, 6, 7, 5, 3, 1)
OFFSETS = (0, -1, 1, -2, 2, -3, 3, 4)


def send(value, pairs):
    return lax.ppermute(value, "section", pairs)


def to_core(value):
    return send(value, [(i, i ^ 1) for i in range(4)])


def to_stage(value):
    return send(value, [(i, i ^ 2) for i in range(4)])


def along(value, by):
    size = len(CYCLE)
    return lax.ppermute(value, "dp", [(CYCLE[i], CYCLE[(i + by) % size]) for i in range(size)])


def after(value, *others):
    return lax.optimization_barrier((value, *others))[0]


def ring_gather(piece, cut):
    ahead, behind, pieces = piece, piece, [piece]
    for _ in range(3):
        ahead, behind = along(ahead, 1), along(behind, -1)
        pieces += [ahead, behind]
    return pieces + [along(ahead[:cut], 1), along(behind[cut:], -1)]


def ring_scatter(keep, got, order, cut):
    def own(offset):
        place = order[OFFSETS.index(offset)]
        mine, theirs = (lax.dynamic_index_in_dim(part, place, 0, keepdims=False) for part in (keep, got))
        return mine.astype(F32) + theirs.astype(F32)

    far = own(4).astype(BF16)
    ahead, behind = along(far[:cut], 1), along(far[cut:], -1)
    for step in (3, 2, 1):
        front, back = own(step), own(-step)
        if step == 3:
            front = jnp.concatenate([front[:cut] + ahead.astype(F32), front[cut:]])
            back = jnp.concatenate([back[:cut], back[cut:] + behind.astype(F32)])
        else:
            front, back = front + ahead.astype(F32), back + behind.astype(F32)
        ahead, behind = along(front.astype(BF16), 1), along(back.astype(BF16), -1)
    return (own(0) + ahead.astype(F32) + behind.astype(F32)).astype(BF16)


def facts_table(dp_count):
    ring = dp_count == len(CYCLE)
    table = np.zeros((4, dp_count, 2 * (MICRO + 1), FACTS), np.int32)
    for section in range(4):
        core, stage = section % 2, section // 2
        for place in range(dp_count):
            for call in range(2 * (MICRO + 1)):
                late = stage if call <= MICRO else 1 - stage
                micro = call % (MICRO + 1) - late
                slot = min(max(micro, 0), MICRO - 1)
                row = table[section, place, call]
                row[[RUNS, SLOT, CORE, STAGE]] = int(0 <= micro < MICRO), slot, core, stage
                row[ROWS], row[PLACE] = core * MICRO + slot, place
                for i, offset in enumerate(OFFSETS):
                    row[ORDER + i] = CYCLE[(CYCLE.index(place) + offset) % dp_count] if ring else i
    return table


def on_device(
    frames_in,
    segment_ids,
    cotangent,
    w_qkv,
    w_out,
    w_up,
    w_down,
    norm1_gain,
    norm1_shift,
    norm2_gain,
    norm2_shift,
    up_bias,
    down_bias,
):
    section = lax.axis_index("section")
    dp_index, dp_count = lax.axis_index("dp"), lax.axis_size("dp")
    rows, frame_count, width = frames_in.shape
    hidden_units = w_up.shape[2]
    own_rows = rows // 2
    tokens = own_rows * frame_count // MICRO
    ring = dp_count == len(CYCLE)
    part = w_qkv.shape[1]
    cut = 3 * width // GROUPS

    table = jnp.asarray(facts_table(dp_count))
    facts = lax.dynamic_slice(table, (section, dp_index, 0, 0), (1, 1) + table.shape[2:])[0, 0]
    by_section = lambda *values: lax.select_n(section, *values)

    matrices = (w_qkv, w_out, w_up, w_down)
    vectors = (norm1_gain, norm1_shift, norm2_gain, norm2_shift, down_bias, up_bias)
    if ring:
        first, second = halves_call(facts, matrices, vectors)
        near = send(jnp.where(section == 0, second, first), [(0, 1), (3, 2)])
        far_first, far_second = send(first, [(1, 2), (2, 0)]), send(second, [(1, 3), (2, 1)])
        early = by_section(first, near, far_first, far_second)
        late = by_section(far_first, far_second, near, second)
        held = []
        own = None
        for piece in (early, late):
            if own is not None:
                piece = after(piece, own[5])
            own = ring_gather(piece, cut)
            other = [to_core(part_of) for part_of in own]
            weights = None
            for low, high in ((0, 3), (3, 5), (5, 7), (7, 9)):
                places = tuple(
                    (min(i, 7), cut if i == 8 else 0, cut if i == 7 else 2 * cut + SMALL_ROWS) for i in range(low, high)
                )
                weights = gather_call(facts, places, own[low:high], other[low:high], weights, width)
            held.append(weights)
    else:
        blocks = [w_qkv[0, :, :width], w_qkv[0, :, width : 2 * width]]
        blocks += [w_up[0, :, i * width : (i + 1) * width] for i in range(hidden_units // width)]
        blocks += [w_qkv[0, :, 2 * width :], w_out[0], w_down[0]]
        whole = jnp.concatenate([lax.all_gather(block.astype(BF16), "dp", axis=0, tiled=True) for block in blocks])
        flat = [lax.all_gather(vector[0].astype(BF16), "dp", axis=0, tiled=True) for vector in vectors]
        small = jnp.concatenate(flat + [jnp.zeros(((SMALL_ROWS - 5) * width - hidden_units,), BF16)])
        small = small.reshape(SMALL_ROWS, width).astype(F32)
        held = []
        for early_from in ((0, 1), (2, 3)):
            value = (whole, small)
            got = [jax.tree.map(lambda v: lax.all_gather(v, "section")[i], value) for i in early_from]
            held.append(jax.tree.map(lambda a, b: jnp.where(section < 2, a, b), *got))

    segments = lax.dynamic_slice_in_dim(segment_ids, section % 2 * own_rows, own_rows, 0).reshape(-1, 128)
    spot = jnp.arange(128, dtype=jnp.int32)
    allowed = (spot[None, :] <= spot[:, None]) & (spot[None, :] // frame_count == spot[:, None] // frame_count)
    allowed = allowed[None] & (segments[:, :, None] == segments[:, None, :])
    bias = jnp.where(allowed, 0.0, -1e30).astype(F32).reshape(MICRO, tokens, 128)
    frames = frames_in.reshape(2 * MICRO, tokens, width)
    last_grads = cotangent.reshape(2 * MICRO, tokens, width)
    sizes = (MICRO, tokens, width, hidden_units)

    states = [None, None]
    early_hops, late_hops, back_hops = [None], [None], [None]
    for t in range(MICRO + 1):
        states[0], low = forward_call(t, facts, (frames, early_hops[-1]), (True, False), bias, held[0], states[0], *sizes)
        early_hops.append(to_stage(low))
    sums = [None, None]

    def late_forward(t):
        states[1], low = forward_call(
            t, facts, (early_hops[min(t, MICRO - 1) + 2], late_hops[-1]), (False, False), bias, held[1], states[1], *sizes
        )
        late_hops.append(to_stage(low) if t < MICRO else None)

    def late_backward(t):
        states[1], sums[1], low = backward_call(
            MICRO + 1 + t, facts, (back_hops[-1], last_grads), (False, True), held[1], states[1], sums[1], *sizes
        )
        back_hops.append(to_stage(low))

    late_forward(0)
    for t in range(1, MICRO + 1):
        late_forward(t)
        late_backward(t - 1)
    late_backward(MICRO)
    early_back = [None]
    for t in range(MICRO + 1):
        states[0], sums[0], low = backward_call(
            MICRO + 1 + t,
            facts,
            (early_back[-1], back_hops[min(t, MICRO - 1) + 2]),
            (False, False),
            held[0],
            states[0],
            sums[0],
            *sizes,
        )
        early_back.append(to_stage(low) if t < MICRO else None)

    totals = []
    for layer in (1, 0):
        keep, give = weight_call(facts, states[layer], sums[layer], width, hidden_units)
        if ring:
            order = [facts[0, ORDER + i] for i in range(len(OFFSETS))]
            totals.append(ring_scatter(keep, to_core(give), order, cut))
        else:
            totals.append((keep, give))
    if ring:
        late_total, early_total = totals
        late_near = send(late_total, [(0, 2), (2, 3)])
        late_far = send(late_total, [(1, 2)])
        early_near = send(early_total, [(2, 1), (1, 0)])
        early_far = send(early_total, [(3, 1)])
        one = by_section(early_total, early_near, late_near, late_near)
        two = by_section(early_near, early_far, late_far, late_total)
        small = one[6 * part :]
        first_grads = [one[i * part : (i + 1) * part] for i in range(6)]
        second_grads = [two[:part], two[part : 2 * part], two[2 * part : 6 * part]]
    else:
        (late_one, late_two), (early_one, early_two) = [
            (jnp.where(section % 2 == 0, keep, give), jnp.where(section % 2 == 0, give, keep)) for keep, give in totals
        ]

        def to_layer(early, late):
            both = [v + to_core(v) for v in (early.astype(F32), late.astype(F32))]
            return by_section(both[0], to_stage(both[0]), to_stage(both[1]), both[1])

        one, two = to_layer(early_one, late_one), to_layer(early_two, late_two)
        small = lax.psum(one[0, 6 * width // GROUPS :], "dp")
        block = width // GROUPS
        natural = lambda half, low, high: lax.psum_scatter(
            half[:, low * block : high * block].reshape(-1, width), "dp", scatter_dimension=0, tiled=True
        )
        first_grads = [natural(one, i, i + 1) for i in range(6)]
        second_grads = [natural(two, 0, 1), natural(two, 1, 2), natural(two, 2, 6)]
    grad_vectors = [lax.dynamic_slice_in_dim(small[i : i + 1].reshape(-1), dp_index * part, part) for i in range(5)]
    grad_vectors.append(
        lax.dynamic_slice_in_dim(small[5 : 5 + hidden_units // width].reshape(-1), dp_index * 4 * part, 4 * part)
    )
    grad_vectors = [vector[None].astype(F32) for vector in grad_vectors]

    spans, _ = layout(width, hidden_units)

    def whole_rows(early_own, late_own, late_in, early_in):
        mine = by_section(early_own, late_in, early_in, late_own)
        theirs = to_core(by_section(late_in, early_own, late_own, early_in))
        both = jnp.where(section % 2 == 0, jnp.stack([mine, theirs]), jnp.stack([theirs, mine]))
        return both.astype(F32).reshape(1, rows, frame_count, width)

    values = lambda state, name: state[:, :, spans[name]]
    early_state, late_state = states
    outputs = whole_rows(
        values(early_state, "result"), values(late_state, "result"), values(late_state, "hidden"), values(late_state, "hidden")
    )
    input_grads = whole_rows(
        values(early_state, "grad"), values(late_state, "grad"), values(early_state, "upstream"), values(early_state, "upstream")
    )
    return (
        outputs,
        input_grads,
        jnp.concatenate([first_grads[0], first_grads[1], second_grads[0]], axis=1)[None].astype(F32),
        second_grads[1][None].astype(F32),
        jnp.concatenate(first_grads[2:], axis=1)[None].astype(F32),
        second_grads[2][None].astype(F32),
        *grad_vectors[:4],
        grad_vectors[5],
        grad_vectors[4],
    )


def solution(mesh):
    rows = P("dp", None, None)
    matrix, vector = P("section", "dp", None), P("section", "dp")
    result = P("section", "dp", None, None)
    return jax.shard_map(
        on_device,
        mesh=mesh,
        in_specs=(rows, P("dp", None), rows) + (matrix,) * 4 + (vector,) * 6,
        out_specs=(result, result) + (matrix,) * 4 + (vector,) * 6,
        check_vma=False,
    )
```

```python
import functools

import jax
import jax.numpy as jnp
import numpy as np
from jax import lax
from jax.experimental import pallas as pl
from jax.experimental.pallas import tpu as pltpu
from jax.sharding import PartitionSpec as P

HEADS = 8
HEAD_DIM = 64
GROUPS = 8
SMALL_ROWS = 16
MICRO = 2
BF16 = jnp.bfloat16
F32 = jnp.float32
ANY = pl.BlockSpec(memory_space=pl.ANY)
SMEM = pl.BlockSpec(memory_space=pltpu.SMEM)
VMEM = pl.BlockSpec(memory_space=pltpu.VMEM)
LIGHT = pl.CostEstimate(flops=1, bytes_accessed=1, transcendentals=0)
RUNS, SLOT, CORE, STAGE, ORDER, ROWS = 0, 1, 2, 3, 4, 12
PLACE = 13
FACTS = 16


class Plan:
    def __init__(self, micros, tokens, width, hidden_units):
        self.micros, self.tokens, self.width, self.hidden_units = micros, tokens, width, hidden_units
        self.blocks = hidden_units // width
        self.spans, at = {}, 0
        sizes = dict(hidden=1, q=1, k=1, v=1, probs=HEADS * 128 // width, mixed=1, middle=2, act=self.blocks, slope=self.blocks,
                     result=1, upstream=1, normed_two=1, r1=1, normed_one=1, grad=1)
        for name, size in sizes.items():
            self.spans[name] = slice(at, at + size * width)
            at += size * width
        self.state = pltpu.VMEM((micros, tokens, at), BF16)


def dot(left, right):
    return lax.dot_general(left, right, (((1,), (0,)), ((), ())), preferred_element_type=F32)


def dot_rhs_t(left, right):
    return lax.dot_general(left, right, (((1,), (1,)), ((), ())), preferred_element_type=F32)


def dot_lhs_t(left, right):
    return lax.dot_general(left, right, (((0,), (0,)), ((), ())), preferred_element_type=F32)


def in_hbm(values):
    return [pltpu.with_memory_space_constraint(value, pltpu.HBM) for value in values]


def params(mebibytes):
    return pltpu.CompilerParams(vmem_limit_bytes=mebibytes << 20)


def after(value, *others):
    return pl.pallas_call(
        lambda *refs: None,
        out_shape=jax.ShapeDtypeStruct(value.shape, value.dtype),
        in_specs=[pl.BlockSpec(memory_space=pl.ANY)] * (1 + len(others)),
        out_specs=pl.BlockSpec(memory_space=pl.ANY),
        input_output_aliases={0: 0},
        compiler_params=params(1),
        cost_estimate=LIGHT,
        name="after",
    )(value, *others)


def gather_kernel(places, has_weights, *refs):
    facts = refs[0]
    count = len(places)
    own, other = refs[1 : 1 + count], refs[1 + count]
    at = 2 + count + (2 if has_weights else 0)
    weights, small, arrived, sems = refs[at : at + 4]
    width = weights.shape[1]
    part = width // GROUPS
    full = 6 * part
    starts = [0]
    for _, low, high in places:
        starts.append(starts[-1] + high - low)

    def move(refs, first_rows, is_first):
        for ref, first_row, (place, low, high) in zip(refs, first_rows, places):
            source = facts[0, ORDER + place]
            if is_first:
                spans = [(i * part, part, i * width, part) for i in range(6)]
            else:
                spans = [(0, part, 6 * width, part), (part, part, 7 * width, part), (2 * part, 4 * part, 8 * width, 4 * part)]
            for start, size, block, step in spans:
                a, b = max(start, low), min(start + size, high)
                if a < b:
                    target = pl.multiple_of(block + source * step + (a - start), 16)
                    pltpu.make_async_copy(
                        ref.at[pl.ds(first_row + a - low, b - a)], weights.at[pl.ds(target, b - a)], sems.at[0]
                    ).start()

    moved = sum(min(high, full) - low for _, low, high in places)
    copies = []
    for ref, (place, low, high) in zip(own, places):
        if high > full:
            copies.append(pltpu.make_async_copy(ref.at[pl.ds(full - low, SMALL_ROWS)], arrived.at[len(copies)], sems.at[1]))
            copies[-1].start()

    def move_both(own_is_first):
        move(own, [0] * count, own_is_first)
        move([other] * count, starts, not own_is_first)

    @pl.when(facts[0, CORE] == 0)
    def _():
        move_both(True)

    @pl.when(facts[0, CORE] != 0)
    def _():
        move_both(False)

    for copy in copies:
        copy.wait()
    total = small[...] if has_weights else jnp.zeros(small.shape, F32)
    for index in range(len(copies)):
        total = total + arrived[index].astype(F32)
    small[...] = total
    whole = weights.at[pl.ds(0, moved)]
    for _ in range(2):
        pltpu.make_async_copy(whole, whole, sems.at[0]).wait()


def gather_call(facts, places, own, other, held, width):
    held = () if held is None else held
    count = 1 + len(own)
    return pl.pallas_call(
        functools.partial(gather_kernel, places, bool(held)),
        out_shape=(pltpu.VMEM((12 * width, width), BF16), pltpu.VMEM((SMALL_ROWS, width), F32)),
        in_specs=[SMEM] + [ANY] * count + [VMEM] * len(held),
        out_specs=(VMEM, VMEM),
        input_output_aliases={1 + count + i: i for i in range(len(held))},
        scratch_shapes=[pltpu.VMEM((GROUPS, SMALL_ROWS, width), BF16), pltpu.SemaphoreType.DMA((2,))],
        compiler_params=params(2),
        cost_estimate=LIGHT,
        name="lay_out_weights",
    )(facts, *own, other, *held)


def bundle_kernel(*refs):
    *pieces, out, sems = refs
    copies, at = [], 0
    for i, piece in enumerate(pieces):
        copies.append(pltpu.make_async_copy(piece, out.at[pl.ds(at, piece.shape[0])], sems.at[i]))
        at += piece.shape[0]
    for copy in copies:
        copy.start()
    for copy in copies:
        copy.wait()


def bundle(pieces):
    rows = sum(piece.shape[0] for piece in pieces)
    return pl.pallas_call(
        bundle_kernel,
        out_shape=jax.ShapeDtypeStruct((rows, pieces[0].shape[1]), BF16),
        in_specs=[ANY] * len(pieces),
        out_specs=VMEM,
        scratch_shapes=[pltpu.SemaphoreType.DMA((len(pieces),))],
        compiler_params=params(5),
        cost_estimate=LIGHT,
        name="bundle",
    )(*pieces)


def pick_kernel(facts, *refs):
    *options, out, sem = refs
    for section, option in enumerate(options):

        @pl.when(facts[0, STAGE] * 2 + facts[0, CORE] == section)
        def _():
            copy = pltpu.make_async_copy(option, out, sem)
            copy.start()
            copy.wait()


def pick(facts, options):
    return pl.pallas_call(
        pick_kernel,
        out_shape=jax.ShapeDtypeStruct(options[0].shape, options[0].dtype),
        in_specs=[SMEM] + [ANY] * len(options),
        out_specs=VMEM,
        scratch_shapes=[pltpu.SemaphoreType.DMA],
        compiler_params=params(3),
        cost_estimate=LIGHT,
        name="pick",
    )(facts, *options)


def split_kernel(first, second, low, high, sems):
    copies = [
        pltpu.make_async_copy(first.at[pl.ds(0, low.shape[0])], low, sems.at[0]),
        pltpu.make_async_copy(second.at[pl.ds(low.shape[0], high.shape[0])], high, sems.at[1]),
    ]
    for copy in copies:
        copy.start()
    for copy in copies:
        copy.wait()


def split(first, second, cut, *waits):
    rows, width = first.shape
    return pl.pallas_call(
        lambda *refs: split_kernel(*refs[:2], *refs[2 + len(waits) :]),
        out_shape=(jax.ShapeDtypeStruct((cut, width), BF16), jax.ShapeDtypeStruct((rows - cut, width), BF16)),
        in_specs=[ANY] * (2 + len(waits)),
        out_specs=(VMEM, VMEM),
        scratch_shapes=[pltpu.SemaphoreType.DMA((2,))],
        compiler_params=params(3),
        cost_estimate=LIGHT,
        name="split",
    )(first, second, *waits)


def ring_add_kernel(sums, cuts, n_arrived, facts, keep, got, *refs):
    arrived = refs[:n_arrived]
    outs = refs[n_arrived : n_arrived + len(sums)]
    mine, theirs, landed, sems = refs[n_arrived + len(sums) :]
    copies = []
    for i, (place, low, high, _) in enumerate(sums):
        block = facts[0, ORDER + place]
        rows = pl.ds(low, high - low)
        for source, target, sem in ((keep, mine, 0), (got, theirs, 1)):
            copies.append(pltpu.make_async_copy(source.at[block, rows], target.at[i, rows], sems.at[sem, i]))
    for i, ref in enumerate(arrived):
        copies.append(pltpu.make_async_copy(ref, landed.at[i, pl.ds(cuts[i], ref.shape[0])], sems.at[2, i]))
    for copy in copies:
        copy.start()
    for copy in copies:
        copy.wait()
    for i, (_, low, high, parts) in enumerate(sums):
        edges = sorted({low, high} | {cuts[p] for p in parts} | {cuts[p] + arrived[p].shape[0] for p in parts})
        for a, b in zip(edges, edges[1:]):
            total = mine[i, a:b].astype(F32) + theirs[i, a:b].astype(F32)
            for p in parts:
                if cuts[p] <= a and b <= cuts[p] + arrived[p].shape[0]:
                    total = total + landed[p, a:b].astype(F32)
            outs[i][a - low : b - low] = total.astype(BF16)


def ring_add(facts, keep, got, arrived, cuts, sums):
    _, rows, width = keep.shape
    return pl.pallas_call(
        functools.partial(ring_add_kernel, sums, cuts, len(arrived)),
        out_shape=tuple(jax.ShapeDtypeStruct((high - low, width), BF16) for _, low, high, _ in sums),
        in_specs=[SMEM] + [ANY] * (2 + len(arrived)),
        out_specs=tuple([VMEM] * len(sums)),
        scratch_shapes=[pltpu.VMEM((2, rows, width), BF16)] * 3 + [pltpu.SemaphoreType.DMA((3, 2))],
        compiler_params=params(6),
        cost_estimate=LIGHT,
        name="ring_add",
    )(facts, *in_hbm((keep, got)), *arrived)


def normalise(values):
    center = values - jnp.mean(values, axis=-1, keepdims=True)
    spread = jnp.mean(center * center, axis=-1, keepdims=True)
    scale = lax.rsqrt(spread + 1e-05)
    return center * scale, scale


def norm_back(grad, gain, unit, scale):
    grad_unit = grad * gain
    mean_grad = jnp.mean(grad_unit, axis=-1, keepdims=True)
    mean_dot = jnp.mean(grad_unit * unit, axis=-1, keepdims=True)
    return scale * (grad_unit - mean_grad - unit * mean_dot)


def stack_heads(pair, low_lanes):
    zero = jnp.zeros_like(pair)
    return jnp.concatenate([jnp.where(low_lanes, pair, zero), jnp.where(low_lanes, zero, pair)], axis=0)


def load_source(facts, call, sources, sliced, target, sem):
    for stage, (source, is_sliced) in enumerate(zip(sources, sliced)):
        if source is None:
            continue

        @pl.when(facts[call, STAGE] == stage)
        def _():
            ref = source.at[facts[call, ROWS]] if is_sliced else source
            pltpu.make_async_copy(ref, target, sem).start()


def read_sources(refs, present):
    given = iter(refs)
    return [next(given) if is_present else None for is_present in present]


def forward_kernel(plan, call, sliced, present, has_state, n_waits, facts, *refs):
    count = sum(present)
    sources = read_sources(refs, present)
    bias_v, weights, small_v = refs[count : count + 3]
    state, low_o, sem = refs[count + 3 + int(has_state) + n_waits :]
    tokens, width = plan.tokens, plan.width
    slot = facts[call, SLOT]
    value_of = lambda name: state.at[slot, :, plan.spans[name]]
    weight = lambda block: weights[block * width : (block + 1) * width]

    @pl.when(facts[call, RUNS] != 0)
    def _():
        hidden_v, q_v, k_v, v_v, probs_v, mixed_v, middle_v, act_v, slope_v = (
            value_of(name) for name in ("hidden", "q", "k", "v", "probs", "mixed", "middle", "act", "slope")
        )
        load_source(facts, call, sources, sliced, hidden_v, sem)
        small = small_v[...]
        gain_one, shift_one, gain_two, shift_two, down_bias = (small[i : i + 1] for i in range(5))
        pltpu.make_async_copy(hidden_v, hidden_v, sem).wait()
        hidden = hidden_v[...].astype(F32)
        unit, _ = normalise(hidden)
        normed = (unit * gain_one + shift_one).astype(BF16)
        q_v[...] = (dot(normed, weight(0)) * HEAD_DIM**-0.5).astype(BF16)
        k_v[...] = dot(normed, weight(1)).astype(BF16)
        v_v[...] = dot(normed, weight(6)).astype(BF16)
        low_lanes = lax.broadcasted_iota(jnp.int32, (128, 128), 1) < HEAD_DIM
        for group in range(tokens // 128):
            rows = slice(group * 128, group * 128 + 128)
            bias = bias_v[slot, rows]
            bias = jnp.concatenate([bias, bias], axis=0)
            for pair in range(width // 128):
                lanes = slice(pair * 128, pair * 128 + 128)
                query = stack_heads(q_v[rows, lanes], low_lanes)
                scores = dot_rhs_t(query, k_v[rows, lanes]) + bias
                raised = jnp.exp(scores - jnp.max(scores, axis=-1, keepdims=True))
                probs = (raised * (1.0 / jnp.sum(raised, axis=-1, keepdims=True))).astype(BF16)
                probs_v[rows, pair * 256 : pair * 256 + 128] = probs[:128]
                probs_v[rows, pair * 256 + 128 : pair * 256 + 256] = probs[128:]
                mixed = dot(probs, v_v[rows, lanes])
                mixed_v[rows, lanes] = jnp.where(low_lanes, mixed[:128], mixed[128:]).astype(BF16)
        middle = hidden + dot(mixed_v[...], weight(7))
        high = middle.astype(BF16)
        middle_v[:, :width] = high
        middle_v[:, width:] = (middle - high.astype(F32)).astype(BF16)
        unit, _ = normalise(middle)
        normed = (unit * gain_two + shift_two).astype(BF16)
        total = middle + down_bias
        for block in range(plan.blocks):
            lanes = slice(block * width, (block + 1) * width)
            before = dot(normed, weight(2 + block)) + small[5 + block : 6 + block]
            square = before * before
            tanh = jnp.tanh(before * (0.7978845608028654 + 0.035677408136300125 * square))
            half = 0.5 * tanh + 0.5
            act = (before * half).astype(BF16)
            act_v[:, lanes] = act
            slope = half + before * (0.5 - 0.5 * (tanh * tanh)) * (0.7978845608028654 + 0.10703222440890037 * square)
            slope_v[:, lanes] = slope.astype(BF16)
            total = total + dot(act, weight(8 + block))
        low = total.astype(BF16)
        low_o[...] = low
        value_of("result")[...] = low


def forward_call(plan, call, facts, sources, sliced, bias, held, state, waits=()):
    given = [source for source in sources if source is not None]
    state = [] if state is None else [state]
    tokens, width = plan.tokens, plan.width
    return pl.pallas_call(
        functools.partial(
            forward_kernel, plan, call, sliced, tuple(s is not None for s in sources), bool(state), len(waits)
        ),
        out_shape=(plan.state, jax.ShapeDtypeStruct((tokens, width), BF16)),
        in_specs=[SMEM] + [ANY] * len(given) + [VMEM] * (3 + len(state)) + [ANY] * len(waits),
        out_specs=(VMEM, VMEM),
        input_output_aliases={4 + len(given): 0} if state else {},
        scratch_shapes=[pltpu.SemaphoreType.DMA],
        compiler_params=params(8),
        cost_estimate=LIGHT,
        name="layer_forward",
    )(facts, *given, bias, *held, *state, *waits)


def backward_kernel(plan, call, sliced, present, has_sums, n_waits, facts, *refs):
    count = sum(present)
    sources = read_sources(refs, present)
    weights, small_v = refs[count : count + 2]
    state, sums_o, low_o, grad_v, do_v, sem = refs[count + 3 + int(has_sums) + n_waits :]
    tokens, width = plan.tokens, plan.width
    slot = facts[call, SLOT]
    value_of = lambda name: state.at[slot, :, plan.spans[name]]
    weight = lambda block: weights[block * width : (block + 1) * width]

    @pl.when(facts[call, RUNS] != 0)
    def _():
        upstream_v, hidden_v, q_v, k_v, v_v, probs_v, middle_v, du_v = (
            value_of(name) for name in ("upstream", "hidden", "q", "k", "v", "probs", "middle", "slope")
        )
        load_source(facts, call, sources, sliced, upstream_v, sem)
        small = small_v[...]
        gain_one, shift_one, gain_two, shift_two = (small[i : i + 1] for i in range(4))
        sums_v = sums_o.at[slot]
        sums_v[...] = jnp.zeros(sums_v.shape, F32)
        pltpu.make_async_copy(upstream_v, upstream_v, sem).wait()
        upstream_low = upstream_v[...]
        upstream = upstream_low.astype(F32)
        sums_v[4:5] = jnp.sum(upstream, axis=0, keepdims=True)
        da = jnp.zeros((tokens, width), F32)
        for block in range(plan.blocks):
            lanes = slice(block * width, (block + 1) * width)
            dz = dot_rhs_t(upstream_low, weight(8 + block))
            du = (dz * du_v[:, lanes].astype(F32)).astype(BF16)
            du_v[:, lanes] = du
            sums_v[5 + block : 6 + block] = jnp.sum(du.astype(F32), axis=0, keepdims=True)
            da = da + dot_rhs_t(du, weight(2 + block))
        unit, scale = normalise(middle_v[:, :width].astype(F32) + middle_v[:, width:].astype(F32))
        value_of("normed_two")[...] = (unit * gain_two + shift_two).astype(BF16)
        sums_v[2:3] = jnp.sum(da * unit, axis=0, keepdims=True)
        sums_v[3:4] = jnp.sum(da, axis=0, keepdims=True)
        grad_middle = upstream + norm_back(da, gain_two, unit, scale)
        grad_v[...] = grad_middle
        r1 = grad_middle.astype(BF16)
        value_of("r1")[...] = r1
        do_v[...] = dot_rhs_t(r1, weight(7)).astype(BF16)
        low_lanes = lax.broadcasted_iota(jnp.int32, (128, 128), 1) < HEAD_DIM
        for group in range(tokens // 128):
            rows = slice(group * 128, group * 128 + 128)
            for pair in range(width // 128):
                lanes = slice(pair * 128, pair * 128 + 128)
                query = stack_heads(q_v[rows, lanes], low_lanes)
                key = k_v[rows, lanes]
                grad_mixed = stack_heads(do_v[rows, lanes], low_lanes)
                probs = jnp.concatenate(
                    [probs_v[rows, pair * 256 : pair * 256 + 128], probs_v[rows, pair * 256 + 128 : pair * 256 + 256]], axis=0
                )
                grad_probs = dot_rhs_t(grad_mixed, v_v[rows, lanes])
                v_v[rows, lanes] = dot_lhs_t(probs, grad_mixed).astype(BF16)
                probs = probs.astype(F32)
                weighted = grad_probs * probs
                grad_scores = (weighted - probs * jnp.sum(weighted, axis=-1, keepdims=True)).astype(BF16)
                dq = dot(grad_scores, key) * HEAD_DIM**-0.5
                q_v[rows, lanes] = jnp.where(low_lanes, dq[:128], dq[128:]).astype(BF16)
                k_v[rows, lanes] = dot_lhs_t(grad_scores, query).astype(BF16)
        unit, scale = normalise(hidden_v[...].astype(F32))
        value_of("normed_one")[...] = (unit * gain_one + shift_one).astype(BF16)
        da = dot_rhs_t(q_v[...], weight(0)) + dot_rhs_t(k_v[...], weight(1)) + dot_rhs_t(v_v[...], weight(6))
        sums_v[0:1] = jnp.sum(da * unit, axis=0, keepdims=True)
        sums_v[1:2] = jnp.sum(da, axis=0, keepdims=True)
        low = (grad_v[...] + norm_back(da, gain_one, unit, scale)).astype(BF16)
        low_o[...] = low
        value_of("grad")[...] = low


def backward_call(plan, call, facts, sources, sliced, held, state, sums, waits=()):
    given = [source for source in sources if source is not None]
    tokens, width = plan.tokens, plan.width
    sums = [] if sums is None else [sums]
    return pl.pallas_call(
        functools.partial(
            backward_kernel, plan, call, sliced, tuple(s is not None for s in sources), bool(sums), len(waits)
        ),
        out_shape=(
            plan.state,
            pltpu.VMEM((plan.micros, SMALL_ROWS, width), F32),
            jax.ShapeDtypeStruct((tokens, width), BF16),
        ),
        in_specs=[SMEM] + [ANY] * len(given) + [VMEM] * (3 + len(sums)) + [ANY] * len(waits),
        out_specs=(VMEM, VMEM, VMEM),
        input_output_aliases={3 + len(given) + i: i for i in range(1 + len(sums))},
        scratch_shapes=[pltpu.VMEM((tokens, width), F32), pltpu.VMEM((tokens, width), BF16), pltpu.SemaphoreType.DMA],
        compiler_params=params(8),
        cost_estimate=LIGHT,
        name="layer_backward",
    )(facts, *given, *held, state, *sums, *waits)


def weight_kernel(plan, facts, sums, state, keep, give, result, out_sems):
    width, run = plan.width, plan.micros * plan.tokens
    part = width // GROUPS
    blocks = plan.blocks

    def value_of(name, block=0):
        at = plan.spans[name].start + block * width
        return state[:, :, at : at + width].reshape(run, width)

    sent = []

    def send(half, groups, rows):
        source = result.at[half, groups, rows]
        sem = out_sems.at[len(sent)]

        @pl.when(facts[0, CORE] == half)
        def _():
            pltpu.make_async_copy(source, keep.at[groups, rows], sem).start()

        @pl.when(facts[0, CORE] != half)
        def _():
            pltpu.make_async_copy(source, give.at[groups, rows], sem).start()

        sent.append(pltpu.make_async_copy(source, source, sem))

    def put(half, grad, groups, row, rows):
        groups, rows = pl.ds(groups.start, groups.stop - groups.start), pl.ds(row, rows)
        result[half, groups, rows] = grad.astype(BF16).reshape(groups.size, rows.size, width)
        send(half, groups, rows)

    everyone = slice(0, GROUPS)
    small = sums[0]
    for micro in range(1, plan.micros):
        small = small + sums[micro]
    small = jnp.broadcast_to(small[None], (GROUPS, SMALL_ROWS, width)).reshape(GROUPS * SMALL_ROWS, width)
    for half in range(2):
        put(half, small, everyone, 6 * part, SMALL_ROWS)
    left = value_of("normed_one").T
    for name, half, row in (("q", 0, 0), ("k", 0, part), ("v", 1, 0)):
        put(half, dot(left, value_of(name)), everyone, row, part)
    put(1, dot(value_of("mixed").T, value_of("r1")), everyone, part, part)
    left = value_of("normed_two").T
    for block in range(blocks):
        put(0, dot(left, value_of("slope", block)), everyone, (2 + block) * part, part)
    right = value_of("upstream")
    of_block = GROUPS // blocks
    for block in range(blocks):
        groups = slice(block * of_block, (block + 1) * of_block)
        put(1, dot(value_of("act", block).T, right), groups, 2 * part, 4 * part)
    for copy in sent:
        copy.wait()


def weight_call(plan, facts, state, sums):
    width = plan.width
    shape = (GROUPS, 6 * width // GROUPS + SMALL_ROWS, width)
    run = plan.micros * plan.tokens
    return pl.pallas_call(
        functools.partial(weight_kernel, plan),
        out_shape=(pltpu.HBM(shape, BF16),) * 2,
        in_specs=[SMEM, VMEM, VMEM],
        out_specs=(ANY, ANY),
        scratch_shapes=[pltpu.VMEM((2, *shape), BF16), pltpu.SemaphoreType.DMA((6 + 2 * plan.blocks,))],
        compiler_params=params(12),
        cost_estimate=LIGHT,
        name="weight_grads",
    )(facts, sums, state)


def halves_kernel(facts, *refs):
    inputs, (first, second), landed, sems = refs[:10], refs[10:12], refs[12:22], refs[22]
    copies = [pltpu.make_async_copy(source, target, sems.at[i]) for i, (source, target) in enumerate(zip(inputs, landed))]
    for copy in copies:
        copy.start()
    w_qkv, w_out, w_up, w_down, *vectors = landed
    part, width = w_out.shape[1:]
    for copy in copies[4:]:
        copy.wait()
    lane = lax.broadcasted_iota(jnp.int32, (1, width), 1)
    rows = []
    for vector in vectors:
        size = vector.shape[1]
        spread = jnp.concatenate([vector[...]] * (width // size), axis=1)
        for row in range(size * GROUPS // width):
            rows.append(jnp.where((lane + row * width) // size == facts[0, PLACE], spread, 0.0))
    rows.append(jnp.zeros((SMALL_ROWS - len(rows), width), F32))
    small = jnp.concatenate(rows, axis=0).astype(BF16)
    first[6 * part :] = small
    second[6 * part :] = small
    copies[0].wait()
    for i in range(2):
        first[i * part : (i + 1) * part] = w_qkv[0, :, i * width : (i + 1) * width].astype(BF16)
    second[:part] = w_qkv[0, :, 2 * width :].astype(BF16)
    copies[1].wait()
    second[part : 2 * part] = w_out[0].astype(BF16)
    copies[2].wait()
    for i in range(w_up.shape[2] // width):
        first[(2 + i) * part : (3 + i) * part] = w_up[0, :, i * width : (i + 1) * width].astype(BF16)
    copies[3].wait()
    second[2 * part : 6 * part] = w_down[0].astype(BF16)


def halves_call(facts, matrices, vectors):
    _, part, width = matrices[1].shape
    shape = jax.ShapeDtypeStruct((6 * part + SMALL_ROWS, width), BF16)
    inputs = (*matrices, *vectors)
    return pl.pallas_call(
        halves_kernel,
        out_shape=(shape, shape),
        in_specs=[SMEM] + [ANY] * len(inputs),
        out_specs=(VMEM, VMEM),
        scratch_shapes=[pltpu.VMEM(value.shape, F32) for value in inputs] + [pltpu.SemaphoreType.DMA((len(inputs),))],
        compiler_params=params(8),
        cost_estimate=LIGHT,
        name="round_shard",
    )(facts, *in_hbm(inputs))


CYCLE = (0, 2, 4, 6, 7, 5, 3, 1)
OFFSETS = (0, -1, 1, -2, 2, -3, 3, 4)
LAG = 2
CALLS = MICRO + LAG


def send(value, pairs):
    return lax.ppermute(value, "section", pairs)


def to_core(value):
    return send(value, [(i, i ^ 1) for i in range(4)])


def to_stage(value):
    return send(value, [(i, i ^ 2) for i in range(4)])


def onward(value):
    return send(value, [(0, 2), (1, 3)])


def backward(value):
    return send(value, [(2, 0), (3, 1)])


def along(value, by):
    size = len(CYCLE)
    return lax.ppermute(value, "dp", [(CYCLE[i], CYCLE[(i + by) % size]) for i in range(size)])


def both_ways(ahead, behind):
    return along(ahead, 1), along(behind, -1)


class Ring:
    def __init__(self, piece, cut):
        self.cut, self.arrived = cut, [piece]

    def step(self, *waits):
        ahead, behind = (self.arrived * 2)[-2:]
        if waits:
            ahead, behind = after(ahead, *waits), after(behind, *waits)
            self.arrived[-2:] = [ahead, behind]
        self.arrived += both_ways(ahead, behind)

    def last_step(self, *waits):
        self.arrived += both_ways(*split(*self.arrived[-2:], self.cut, *waits))

    def lay_out(self, facts, width):
        held = None
        for low, high in ((0, 5), (5, 9)):
            places = tuple(
                (min(i, 7), self.cut if i == 8 else 0, self.cut if i == 7 else 2 * self.cut + SMALL_ROWS)
                for i in range(low, high)
            )
            pieces = self.arrived[low:high]
            held = gather_call(facts, places, pieces, to_core(bundle(pieces)), held, width)
        return held


def scatter_step(step, facts, keep, got, arrived, cut):
    rows = keep.shape[1]
    at = OFFSETS.index
    if step == 4:
        sums = ((at(4), 0, cut, ()), (at(4), cut, rows, ()))
    elif step == 0:
        sums = ((at(0), 0, rows, (0, 1)),)
    else:
        sums = ((at(step), 0, rows, (0,)), (at(-step), 0, rows, (1,)))
    cuts = (0, cut) if step == 3 else (0, 0)
    totals = ring_add(facts, keep, got, arrived, cuts, sums)
    return both_ways(*totals) if step else totals[0]


def facts_table(dp_count):
    ring = dp_count == len(CYCLE)
    table = np.zeros((4, dp_count, 2 * CALLS, FACTS), np.int32)
    for section in range(4):
        core, stage = section % 2, section // 2
        for place in range(dp_count):
            for call in range(2 * CALLS):
                micro = call % CALLS - (LAG if stage == call // CALLS % 2 ^ 1 else 0)
                slot = min(max(micro, 0), MICRO - 1)
                row = table[section, place, call]
                row[[RUNS, SLOT, CORE, STAGE]] = int(0 <= micro < MICRO), slot, core, stage
                row[ROWS], row[PLACE] = core * MICRO + slot, place
                for i, offset in enumerate(OFFSETS):
                    row[ORDER + i] = CYCLE[(CYCLE.index(place) + offset) % dp_count] if ring else i
    return table


def on_device(
    frames_in,
    segment_ids,
    cotangent,
    w_qkv,
    w_out,
    w_up,
    w_down,
    norm1_gain,
    norm1_shift,
    norm2_gain,
    norm2_shift,
    up_bias,
    down_bias,
):
    section = lax.axis_index("section")
    dp_index, dp_count = lax.axis_index("dp"), lax.axis_size("dp")
    rows, frame_count, width = frames_in.shape
    hidden_units = w_up.shape[2]
    own_rows = rows // 2
    tokens = own_rows * frame_count // MICRO
    ring = dp_count == len(CYCLE)
    part = w_qkv.shape[1]
    cut = 3 * width // GROUPS
    plan = Plan(MICRO, tokens, width, hidden_units)

    table = jnp.asarray(facts_table(dp_count))
    facts = lax.dynamic_slice(table, (section, dp_index, 0, 0), (1, 1) + table.shape[2:])[0, 0]
    by_section = lambda *values: lax.select_n(section, *values)

    matrices = (w_qkv, w_out, w_up, w_down)
    vectors = (norm1_gain, norm1_shift, norm2_gain, norm2_shift, down_bias, up_bias)
    if ring:
        first, second = halves_call(facts, matrices, vectors)
        near = send(jnp.where(section == 0, second, first), [(0, 1), (3, 2)])
        early = pick(facts, (first, near, send(first, [(1, 2)]), send(second, [(1, 3)])))
        late = by_section(send(first, [(2, 0)]), send(second, [(2, 1)]), near, second)
        early_ring = Ring(early, cut)
        for _ in range(3):
            early_ring.step()
        early_ring.last_step()
        held = [early_ring.lay_out(facts, width)]
        first_step = early_ring.arrived[1:2]
        far = send(after(first, *first_step), [(2, 0)]), send(after(second, *first_step), [(2, 1)])
        late_ring = Ring(after(pick(facts, (*far, near, second)), *early_ring.arrived[-2:]), cut)
        late_ring.step()
        late_ring.step(held[0][1])
    else:
        late_ring = None
        blocks = [w_qkv[0, :, :width], w_qkv[0, :, width : 2 * width]]
        blocks += [w_up[0, :, i * width : (i + 1) * width] for i in range(hidden_units // width)]
        blocks += [w_qkv[0, :, 2 * width :], w_out[0], w_down[0]]
        whole = jnp.concatenate([lax.all_gather(block.astype(BF16), "dp", axis=0, tiled=True) for block in blocks])
        flat = [lax.all_gather(vector[0].astype(BF16), "dp", axis=0, tiled=True) for vector in vectors]
        small = jnp.concatenate(flat + [jnp.zeros(((SMALL_ROWS - 5) * width - hidden_units,), BF16)])
        value = (whole, small.reshape(SMALL_ROWS, width).astype(F32))
        got = [jax.tree.map(lambda v: lax.all_gather(v, "section")[i], value) for i in range(4)]
        held = [jax.tree.map(lambda a, b: jnp.where(section < 2, a, b), got[i], got[i + 1]) for i in (0, 2)]

    segments = lax.dynamic_slice_in_dim(segment_ids, section % 2 * own_rows, own_rows, 0).reshape(-1, 128)
    spot = jnp.arange(128, dtype=jnp.int32)
    allowed = (spot[None, :] <= spot[:, None]) & (spot[None, :] // frame_count == spot[:, None] // frame_count)
    allowed = allowed[None] & (segments[:, :, None] == segments[:, None, :])
    bias = jnp.where(allowed, 0.0, -1e30).astype(F32).reshape(MICRO, tokens, 128)
    frames = frames_in.reshape(2 * MICRO, tokens, width)
    last_grads = cotangent.reshape(2 * MICRO, tokens, width)

    states, sums = [None, None], [None, None]
    onward_early, back_early, onward_late = {}, {}, {}
    for t in range(CALLS):
        sources = (frames if t < MICRO else None, onward_early.get(t - LAG))
        states[0], low = forward_call(plan, t, facts, sources, (True, False), bias, held[0], states[0])
        if ring and t == 0:
            late_ring.step(low)
        elif ring and t == 1:
            late_ring.last_step(low)
        if t < MICRO:
            onward_early[t] = onward(low)
        if t >= LAG:
            back_early[t - LAG] = backward(low)

    if ring:
        held.append(late_ring.lay_out(facts, width))

    def late_forward(t):
        sources = (back_early.get(t), onward_late.get(t - LAG))
        states[1], low = forward_call(plan, t, facts, sources, (False, False), bias, held[1], states[1])
        if t < MICRO:
            onward_late[t] = onward(low)

    back_late, onward_back, back_back = {}, {}, {}

    def late_backward(t):
        sources = (back_late.get(t - LAG), last_grads if t < MICRO else None)
        states[1], sums[1], low = backward_call(
            plan, CALLS + t, facts, sources, (False, True), held[1], states[1], sums[1]
        )
        if t < MICRO:
            back_late[t] = backward(low)
        if t >= LAG:
            onward_back[t - LAG] = onward(low)

    for t in range(LAG):
        late_forward(t)
    for t in range(MICRO):
        late_forward(LAG + t)
        late_backward(t)
    for t in range(MICRO, CALLS):
        late_backward(t)
    keep, give = weight_call(plan, facts, states[1], sums[1])
    totals = [(keep, give)]
    if ring:
        got = to_core(give)
        moving = None
    for t in range(CALLS):
        waits = ()
        if ring and t < 4:
            waits = moving or (got,)
            moving = scatter_step(4 - t, facts, keep, got, moving or (), cut)
        sources = (back_back.get(t - LAG), onward_back.get(t))
        states[0], sums[0], low = backward_call(
            plan, CALLS + t, facts, sources, (False, False), held[0], states[0], sums[0], waits
        )
        if t < MICRO:
            back_back[t] = backward(low)
    late_keep, late_got = (keep, got) if ring else (None, None)
    keep, give = weight_call(plan, facts, states[0], sums[0])
    totals.append((keep, give))
    if ring:
        got = to_core(give)
        moving_early = scatter_step(4, facts, keep, got, (), cut)
        late_total = scatter_step(0, facts, late_keep, late_got, moving, cut)
        moving_early = scatter_step(3, facts, keep, got, moving_early, cut)
        late_near = send(late_total, [(0, 2), (2, 3)])
        late_far = send(late_total, [(1, 2)])
        moving_early = scatter_step(2, facts, keep, got, moving_early, cut)
        moving_early = scatter_step(1, facts, keep, got, moving_early, cut)
        early_total = scatter_step(0, facts, keep, got, moving_early, cut)
        early_near = send(early_total, [(2, 1), (1, 0)])
        early_far = send(early_total, [(3, 1)])
        one = by_section(early_total, early_near, late_near, late_near)
        two = by_section(early_near, early_far, late_far, late_total)
        small = one[6 * part :]
        first_grads = [one[i * part : (i + 1) * part] for i in range(6)]
        second_grads = [two[:part], two[part : 2 * part], two[2 * part : 6 * part]]
    else:
        (late_one, late_two), (early_one, early_two) = [
            (jnp.where(section % 2 == 0, keep, give), jnp.where(section % 2 == 0, give, keep)) for keep, give in totals
        ]

        def to_layer(early, late):
            both = [v + to_core(v) for v in (early.astype(F32), late.astype(F32))]
            return by_section(both[0], to_stage(both[0]), to_stage(both[1]), both[1])

        one, two = to_layer(early_one, late_one), to_layer(early_two, late_two)
        small = lax.psum(one[0, 6 * width // GROUPS :], "dp")
        block = width // GROUPS
        natural = lambda half, low, high: lax.psum_scatter(
            half[:, low * block : high * block].reshape(-1, width), "dp", scatter_dimension=0, tiled=True
        )
        first_grads = [natural(one, i, i + 1) for i in range(6)]
        second_grads = [natural(two, 0, 1), natural(two, 1, 2), natural(two, 2, 6)]
    grad_vectors = [lax.dynamic_slice_in_dim(small[i : i + 1].reshape(-1), dp_index * part, part) for i in range(5)]
    grad_vectors.append(
        lax.dynamic_slice_in_dim(small[5 : 5 + hidden_units // width].reshape(-1), dp_index * 4 * part, 4 * part)
    )
    grad_vectors = [vector[None].astype(F32) for vector in grad_vectors]

    def whole_rows(early_own, late_own, late_in, early_in):
        mine = by_section(early_own, late_in, early_in, late_own)
        theirs = to_core(by_section(late_in, early_own, late_own, early_in))
        both = jnp.where(section % 2 == 0, jnp.stack([mine, theirs]), jnp.stack([theirs, mine]))
        return both.astype(F32).reshape(1, rows, frame_count, width)

    value_of = lambda layer, name: states[layer][:, :, plan.spans[name]]
    outputs = whole_rows(value_of(0, "result"), value_of(1, "result"), value_of(1, "hidden"), value_of(1, "hidden"))
    input_grads = whole_rows(value_of(0, "grad"), value_of(1, "grad"), value_of(0, "upstream"), value_of(0, "upstream"))
    return (
        outputs,
        input_grads,
        jnp.concatenate([first_grads[0], first_grads[1], second_grads[0]], axis=1)[None].astype(F32),
        second_grads[1][None].astype(F32),
        jnp.concatenate(first_grads[2:], axis=1)[None].astype(F32),
        second_grads[2][None].astype(F32),
        *grad_vectors[:4],
        grad_vectors[5],
        grad_vectors[4],
    )


def solution(mesh):
    rows = P("dp", None, None)
    matrix, vector = P("section", "dp", None), P("section", "dp")
    result = P("section", "dp", None, None)
    return jax.shard_map(
        on_device,
        mesh=mesh,
        in_specs=(rows, P("dp", None), rows) + (matrix,) * 4 + (vector,) * 6,
        out_specs=(result, result) + (matrix,) * 4 + (vector,) * 6,
        check_vma=False,
    )
```

```python
import functools

import jax
import jax.numpy as jnp
import numpy as np
from jax import lax
from jax.experimental import pallas as pl
from jax.experimental.pallas import tpu as pltpu
from jax.sharding import PartitionSpec as P

HEADS = 8
HEAD_DIM = 64
GROUPS = 8
SMALL_ROWS = 16
MICRO = 2
BF16 = jnp.bfloat16
F32 = jnp.float32
ANY = pl.BlockSpec(memory_space=pl.ANY)
SMEM = pl.BlockSpec(memory_space=pltpu.SMEM)
VMEM = pl.BlockSpec(memory_space=pltpu.VMEM)
LIGHT = pl.CostEstimate(flops=1, bytes_accessed=1, transcendentals=0)
RUNS, SLOT, CORE, STAGE, ORDER, PLACE, SPOT = 0, 1, 2, 3, 4, 12, 16
FACTS = 24


class Plan:
    def __init__(self, micros, tokens, width, hidden_units):
        self.micros, self.tokens, self.width, self.hidden_units = micros, tokens, width, hidden_units
        self.blocks = hidden_units // width
        self.spans, at = {}, 0
        sizes = dict(hidden=1, q=1, k=1, v=1, probs=HEADS * 128 // width, mixed=1, middle=2, act=self.blocks, slope=self.blocks,
                     result=1, upstream=1, normed_two=1, r1=1, normed_one=1, grad=1)
        for name, size in sizes.items():
            self.spans[name] = slice(at, at + size * width)
            at += size * width
        self.state = pltpu.VMEM((micros, tokens, at), BF16)


def dot(left, right):
    return lax.dot_general(left, right, (((1,), (0,)), ((), ())), preferred_element_type=F32)


def dot_rhs_t(left, right):
    return lax.dot_general(left, right, (((1,), (1,)), ((), ())), preferred_element_type=F32)


def dot_lhs_t(left, right):
    return lax.dot_general(left, right, (((0,), (0,)), ((), ())), preferred_element_type=F32)


def in_hbm(values):
    return [pltpu.with_memory_space_constraint(value, pltpu.HBM) for value in values]


def params(mebibytes):
    return pltpu.CompilerParams(vmem_limit_bytes=mebibytes << 20)


def after(value, *others):
    return pl.pallas_call(
        lambda *refs: None,
        out_shape=jax.ShapeDtypeStruct(value.shape, value.dtype),
        in_specs=[pl.BlockSpec(memory_space=pl.ANY)] * (1 + len(others)),
        out_specs=pl.BlockSpec(memory_space=pl.ANY),
        input_output_aliases={0: 0},
        compiler_params=params(1),
        cost_estimate=LIGHT,
        name="after",
    )(value, *others)


def bundle_kernel(count, *refs):
    pieces, (out, sem) = refs[:count], refs[-2:]
    copies, at = [], 0
    for piece in pieces:
        copies.append(pltpu.make_async_copy(piece, out.at[pl.ds(at, piece.shape[0])], sem))
        copies[-1].start()
        at += piece.shape[0]
    pltpu.make_async_copy(out, out, sem).wait()


def bundle(pieces, waits=()):
    rows = sum(piece.shape[0] for piece in pieces)
    return pl.pallas_call(
        functools.partial(bundle_kernel, len(pieces)),
        out_shape=pltpu.VMEM((rows, pieces[0].shape[1]), BF16),
        in_specs=[ANY] * (len(pieces) + len(waits)),
        out_specs=VMEM,
        scratch_shapes=[pltpu.SemaphoreType.DMA],
        compiler_params=params(2),
        cost_estimate=LIGHT,
        name="bundle",
    )(*pieces, *waits)


def gather_kernel(places, facts, own, other, *refs):
    held, sem = refs[-2:]
    at = 0
    for place, low, high in places:
        for ref, half in ((own, facts[0, CORE]), (other, 1 - facts[0, CORE])):
            target = held.at[half, facts[0, ORDER + place], pl.ds(low, high - low)]
            pltpu.make_async_copy(ref.at[pl.ds(at, high - low)], target, sem).start()
        at += high - low
    for ref in (own, other):
        pltpu.make_async_copy(ref, ref, sem).wait()


def gather_call(facts, places, own, other, held, waits=()):
    held = () if held is None else (held,)
    width = own.shape[1]
    rows = 6 * width // GROUPS + SMALL_ROWS
    return pl.pallas_call(
        functools.partial(gather_kernel, places),
        out_shape=pltpu.VMEM((2, GROUPS, rows, width), BF16),
        in_specs=[SMEM, ANY, ANY] + [VMEM] * len(held) + [ANY] * len(waits),
        out_specs=VMEM,
        input_output_aliases={3: 0} if held else {},
        scratch_shapes=[pltpu.SemaphoreType.DMA],
        compiler_params=params(2),
        cost_estimate=LIGHT,
        name="lay_out_weights",
    )(facts, own, other, *held, *waits)


def weight_block(held, width, block):
    part = width // GROUPS
    if block < 6:
        return held[0, :, block * part : (block + 1) * part, :].reshape(width, width)
    if block < 8:
        return held[1, :, (block - 6) * part : (block - 5) * part, :].reshape(width, width)
    first = (block - 8) * 2
    return held[1, first : first + 2, 2 * part : 6 * part, :].reshape(width, width)


def small_rows(held, width):
    total = held[0, 0, 6 * width // GROUPS :].astype(F32)
    for group in range(1, GROUPS):
        total = total + held[0, group, 6 * width // GROUPS :].astype(F32)
    return total


def pick_kernel(parts, facts, *refs):
    outs, sems = refs[-1 - len(parts) : -1], refs[-1]
    options = refs[: 4 * sum(parts)]
    for section in range(4):

        @pl.when(facts[0, STAGE] * 2 + facts[0, CORE] == section)
        def _():
            copies, at = [], 0
            for out, count in zip(outs, parts):
                row = 0
                for i in range(count):
                    source = options[at + 4 * i + section]
                    copies.append(
                        pltpu.make_async_copy(source, out.at[pl.ds(row, source.shape[0])], sems.at[len(copies)])
                    )
                    row += source.shape[0]
                at += 4 * count
            for copy in copies:
                copy.start()
            for copy in copies:
                copy.wait()


def pick(facts, *choices, waits=()):
    shapes = [
        pltpu.VMEM((sum(options[0].shape[0] for options in parts), parts[0][0].shape[1]), BF16) for parts in choices
    ]
    given = [option for parts in choices for options in parts for option in options]
    return pl.pallas_call(
        functools.partial(pick_kernel, tuple(len(parts) for parts in choices)),
        out_shape=tuple(shapes),
        in_specs=[SMEM] + [ANY] * (len(given) + len(waits)),
        out_specs=tuple([VMEM] * len(choices)),
        scratch_shapes=[pltpu.SemaphoreType.DMA((sum(len(parts) for parts in choices),))],
        compiler_params=params(3),
        cost_estimate=LIGHT,
        name="pick",
    )(facts, *given, *waits)


def split_kernel(first, second, low, high, sems):
    copies = [
        pltpu.make_async_copy(first.at[pl.ds(0, low.shape[0])], low, sems.at[0]),
        pltpu.make_async_copy(second.at[pl.ds(low.shape[0], high.shape[0])], high, sems.at[1]),
    ]
    for copy in copies:
        copy.start()
    for copy in copies:
        copy.wait()


def split(first, second, cut, *waits):
    rows, width = first.shape
    return pl.pallas_call(
        lambda *refs: split_kernel(*refs[:2], *refs[2 + len(waits) :]),
        out_shape=(pltpu.VMEM((cut, width), BF16), pltpu.VMEM((rows - cut, width), BF16)),
        in_specs=[ANY] * (2 + len(waits)),
        out_specs=(VMEM, VMEM),
        scratch_shapes=[pltpu.SemaphoreType.DMA((2,))],
        compiler_params=params(3),
        cost_estimate=LIGHT,
        name="split",
    )(first, second, *waits)


def merge_kernel(keep, got, *refs):
    out, landed, sems = refs[-3:]
    copies = [pltpu.make_async_copy(got.at[i], landed.at[i], sems.at[i]) for i in range(got.shape[0])]
    for copy in copies:
        copy.start()
    for i, copy in enumerate(copies):
        copy.wait()
        out[i] = (keep[i].astype(F32) + landed[i].astype(F32)).astype(BF16)


def merge(keep, got, waits=()):
    return pl.pallas_call(
        merge_kernel,
        out_shape=pltpu.VMEM(keep.shape, BF16),
        in_specs=[VMEM, ANY] + [ANY] * len(waits),
        out_specs=VMEM,
        input_output_aliases={0: 0},
        scratch_shapes=[pltpu.VMEM(keep.shape, BF16), pltpu.SemaphoreType.DMA((keep.shape[0],))],
        compiler_params=params(6),
        cost_estimate=LIGHT,
        name="merge",
    )(keep, got, *waits)


def ring_add_kernel(sums, cuts, n_arrived, n_waits, held, *refs):
    arrived = refs[:n_arrived]
    outs = refs[n_arrived + n_waits :]
    for (block, low, high, parts), out in zip(sums, outs):
        edges = sorted({low, high} | {cuts[p] for p in parts} | {cuts[p] + arrived[p].shape[0] for p in parts})
        for a, b in zip(edges, edges[1:]):
            total = held[block, a:b].astype(F32)
            for p in parts:
                if cuts[p] <= a and b <= cuts[p] + arrived[p].shape[0]:
                    total = total + arrived[p][a - cuts[p] : b - cuts[p]].astype(F32)
            out[a - low : b - low] = total.astype(BF16)


def ring_add(held, arrived, cuts, sums, waits=()):
    width = held.shape[2]
    return pl.pallas_call(
        functools.partial(ring_add_kernel, sums, cuts, len(arrived), len(waits)),
        out_shape=tuple(pltpu.VMEM((high - low, width), BF16) for _, low, high, _ in sums),
        in_specs=[VMEM] * (1 + len(arrived)) + [ANY] * len(waits),
        out_specs=tuple([VMEM] * len(sums)),
        compiler_params=params(5),
        cost_estimate=LIGHT,
        name="ring_add",
    )(held, *arrived, *waits)


def normalise(values):
    center = values - jnp.mean(values, axis=-1, keepdims=True)
    spread = jnp.mean(center * center, axis=-1, keepdims=True)
    scale = lax.rsqrt(spread + 1e-05)
    return center * scale, scale


def norm_back(grad, gain, unit, scale):
    grad_unit = grad * gain
    mean_grad = jnp.mean(grad_unit, axis=-1, keepdims=True)
    mean_dot = jnp.mean(grad_unit * unit, axis=-1, keepdims=True)
    return scale * (grad_unit - mean_grad - unit * mean_dot)


def stack_heads(pair, low_lanes):
    zero = jnp.zeros_like(pair)
    return jnp.concatenate([jnp.where(low_lanes, pair, zero), jnp.where(low_lanes, zero, pair)], axis=0)


def load_source(facts, call, micros, slot, sources, kinds, target, sem):
    for stage, (refs, kind) in enumerate(zip(sources, kinds)):
        if not refs:
            continue

        @pl.when(facts[call, STAGE] == stage)
        def _():
            if kind == "each":
                for micro, ref in enumerate(refs):

                    @pl.when(slot == micro)
                    def _():
                        pltpu.make_async_copy(ref, target, sem).start()

            else:
                ref = refs[0]
                if kind == "core":
                    ref = ref.at[facts[call, CORE] * micros + slot]
                elif kind == "slot":
                    ref = ref.at[slot]
                pltpu.make_async_copy(ref, target, sem).start()


def for_slots(facts, call, micros, whole, work):
    @pl.when(facts[call, RUNS] != 0)
    def _():
        if whole:
            pl.loop(0, micros)(work)
        else:
            work(facts[call, SLOT])


def read_sources(refs, counts):
    refs = list(refs)
    return [[refs.pop(0) for _ in range(count)] for count in counts]


def forward_kernel(plan, call, whole, kinds, counts, has_state, n_waits, facts, *refs):
    count = sum(counts)
    sources = read_sources(refs, counts)
    bias_v, held = refs[count : count + 2]
    state, low_o, sem = refs[count + 2 + int(has_state) + n_waits :]
    tokens, width = plan.tokens, plan.width
    weight = lambda block: weight_block(held, width, block)

    def work(slot):
        value_of = lambda name: state.at[slot, :, plan.spans[name]]
        low_v = low_o.at[slot] if whole else low_o
        hidden_v, q_v, k_v, v_v, probs_v, mixed_v, middle_v, act_v, slope_v = (
            value_of(name) for name in ("hidden", "q", "k", "v", "probs", "mixed", "middle", "act", "slope")
        )
        load_source(facts, call, plan.micros, slot, sources, kinds, hidden_v, sem)
        small = small_rows(held, width)
        gain_one, shift_one, gain_two, shift_two, down_bias = (small[i : i + 1] for i in range(5))
        pltpu.make_async_copy(hidden_v, hidden_v, sem).wait()
        hidden = hidden_v[...].astype(F32)
        unit, _ = normalise(hidden)
        normed = (unit * gain_one + shift_one).astype(BF16)
        q_v[...] = (dot(normed, weight(0)) * HEAD_DIM**-0.5).astype(BF16)
        k_v[...] = dot(normed, weight(1)).astype(BF16)
        v_v[...] = dot(normed, weight(6)).astype(BF16)
        low_lanes = lax.broadcasted_iota(jnp.int32, (128, 128), 1) < HEAD_DIM
        for group in range(tokens // 128):
            rows = slice(group * 128, group * 128 + 128)
            bias = bias_v[slot, rows]
            bias = jnp.concatenate([bias, bias], axis=0)
            for pair in range(width // 128):
                lanes = slice(pair * 128, pair * 128 + 128)
                query = stack_heads(q_v[rows, lanes], low_lanes)
                scores = dot_rhs_t(query, k_v[rows, lanes]) + bias
                raised = jnp.exp(scores - jnp.max(scores, axis=-1, keepdims=True))
                probs = (raised * (1.0 / jnp.sum(raised, axis=-1, keepdims=True))).astype(BF16)
                probs_v[rows, pair * 256 : pair * 256 + 128] = probs[:128]
                probs_v[rows, pair * 256 + 128 : pair * 256 + 256] = probs[128:]
                mixed = dot(probs, v_v[rows, lanes])
                mixed_v[rows, lanes] = jnp.where(low_lanes, mixed[:128], mixed[128:]).astype(BF16)
        middle = hidden + dot(mixed_v[...], weight(7))
        high = middle.astype(BF16)
        middle_v[:, :width] = high
        middle_v[:, width:] = (middle - high.astype(F32)).astype(BF16)
        unit, _ = normalise(middle)
        normed = (unit * gain_two + shift_two).astype(BF16)
        total = middle + down_bias
        for block in range(plan.blocks):
            lanes = slice(block * width, (block + 1) * width)
            before = dot(normed, weight(2 + block)) + small[5 + block : 6 + block]
            square = before * before
            tanh = jnp.tanh(before * (0.7978845608028654 + 0.035677408136300125 * square))
            half = 0.5 * tanh + 0.5
            act = (before * half).astype(BF16)
            act_v[:, lanes] = act
            slope = half + before * (0.5 - 0.5 * (tanh * tanh)) * (0.7978845608028654 + 0.10703222440890037 * square)
            slope_v[:, lanes] = slope.astype(BF16)
            total = total + dot(act, weight(8 + block))
        low = total.astype(BF16)
        low_v[...] = low
        value_of("result")[...] = low

    for_slots(facts, call, plan.micros, whole, work)


def forward_call(plan, call, whole, facts, sources, kinds, bias, held, state, waits=()):
    given = [source for refs in sources for source in refs]
    state = [] if state is None else [state]
    tokens, width = plan.tokens, plan.width
    low = ((plan.micros,) if whole else ()) + (tokens, width)
    return pl.pallas_call(
        functools.partial(
            forward_kernel, plan, call, whole, kinds, tuple(len(refs) for refs in sources), bool(state), len(waits)
        ),
        out_shape=(plan.state, pltpu.VMEM(low, BF16)),
        in_specs=[SMEM] + [ANY] * len(given) + [VMEM] * (2 + len(state)) + [ANY] * len(waits),
        out_specs=(VMEM, VMEM),
        input_output_aliases={3 + len(given): 0} if state else {},
        scratch_shapes=[pltpu.SemaphoreType.DMA],
        compiler_params=params(8),
        cost_estimate=LIGHT,
        name="layer_forward",
    )(facts, *given, bias, held, *state, *waits)


def backward_kernel(plan, call, whole, kinds, counts, has_sums, n_waits, facts, *refs):
    count = sum(counts)
    sources = read_sources(refs, counts)
    held = refs[count]
    state, sums_o, low_o, grad_v, do_v, sem = refs[count + 2 + int(has_sums) + n_waits :]
    tokens, width = plan.tokens, plan.width
    weight = lambda block: weight_block(held, width, block)

    def work(slot):
        value_of = lambda name: state.at[slot, :, plan.spans[name]]
        low_v = low_o.at[slot] if whole else low_o
        upstream_v, hidden_v, q_v, k_v, v_v, probs_v, middle_v, du_v = (
            value_of(name) for name in ("upstream", "hidden", "q", "k", "v", "probs", "middle", "slope")
        )
        load_source(facts, call, plan.micros, slot, sources, kinds, upstream_v, sem)
        small = small_rows(held, width)
        gain_one, shift_one, gain_two, shift_two = (small[i : i + 1] for i in range(4))
        sums_v = sums_o.at[slot]
        sums_v[...] = jnp.zeros(sums_v.shape, F32)
        pltpu.make_async_copy(upstream_v, upstream_v, sem).wait()
        upstream_low = upstream_v[...]
        upstream = upstream_low.astype(F32)
        sums_v[4:5] = jnp.sum(upstream, axis=0, keepdims=True)
        da = jnp.zeros((tokens, width), F32)
        for block in range(plan.blocks):
            lanes = slice(block * width, (block + 1) * width)
            dz = dot_rhs_t(upstream_low, weight(8 + block))
            du = (dz * du_v[:, lanes].astype(F32)).astype(BF16)
            du_v[:, lanes] = du
            sums_v[5 + block : 6 + block] = jnp.sum(du.astype(F32), axis=0, keepdims=True)
            da = da + dot_rhs_t(du, weight(2 + block))
        unit, scale = normalise(middle_v[:, :width].astype(F32) + middle_v[:, width:].astype(F32))
        value_of("normed_two")[...] = (unit * gain_two + shift_two).astype(BF16)
        sums_v[2:3] = jnp.sum(da * unit, axis=0, keepdims=True)
        sums_v[3:4] = jnp.sum(da, axis=0, keepdims=True)
        grad_middle = upstream + norm_back(da, gain_two, unit, scale)
        grad_v[...] = grad_middle
        r1 = grad_middle.astype(BF16)
        value_of("r1")[...] = r1
        do_v[...] = dot_rhs_t(r1, weight(7)).astype(BF16)
        low_lanes = lax.broadcasted_iota(jnp.int32, (128, 128), 1) < HEAD_DIM
        for group in range(tokens // 128):
            rows = slice(group * 128, group * 128 + 128)
            for pair in range(width // 128):
                lanes = slice(pair * 128, pair * 128 + 128)
                query = stack_heads(q_v[rows, lanes], low_lanes)
                key = k_v[rows, lanes]
                grad_mixed = stack_heads(do_v[rows, lanes], low_lanes)
                probs = jnp.concatenate(
                    [probs_v[rows, pair * 256 : pair * 256 + 128], probs_v[rows, pair * 256 + 128 : pair * 256 + 256]], axis=0
                )
                grad_probs = dot_rhs_t(grad_mixed, v_v[rows, lanes])
                v_v[rows, lanes] = dot_lhs_t(probs, grad_mixed).astype(BF16)
                probs = probs.astype(F32)
                weighted = grad_probs * probs
                grad_scores = (weighted - probs * jnp.sum(weighted, axis=-1, keepdims=True)).astype(BF16)
                dq = dot(grad_scores, key) * HEAD_DIM**-0.5
                q_v[rows, lanes] = jnp.where(low_lanes, dq[:128], dq[128:]).astype(BF16)
                k_v[rows, lanes] = dot_lhs_t(grad_scores, query).astype(BF16)
        unit, scale = normalise(hidden_v[...].astype(F32))
        value_of("normed_one")[...] = (unit * gain_one + shift_one).astype(BF16)
        da = dot_rhs_t(q_v[...], weight(0)) + dot_rhs_t(k_v[...], weight(1)) + dot_rhs_t(v_v[...], weight(6))
        sums_v[0:1] = jnp.sum(da * unit, axis=0, keepdims=True)
        sums_v[1:2] = jnp.sum(da, axis=0, keepdims=True)
        low = (grad_v[...] + norm_back(da, gain_one, unit, scale)).astype(BF16)
        low_v[...] = low
        value_of("grad")[...] = low

    for_slots(facts, call, plan.micros, whole, work)


def backward_call(plan, call, whole, facts, sources, kinds, held, state, sums, waits=()):
    given = [source for refs in sources for source in refs]
    tokens, width = plan.tokens, plan.width
    sums = [] if sums is None else [sums]
    low = ((plan.micros,) if whole else ()) + (tokens, width)
    return pl.pallas_call(
        functools.partial(
            backward_kernel, plan, call, whole, kinds, tuple(len(refs) for refs in sources), bool(sums), len(waits)
        ),
        out_shape=(
            plan.state,
            pltpu.VMEM((plan.micros, SMALL_ROWS, width), F32),
            pltpu.VMEM(low, BF16),
        ),
        in_specs=[SMEM] + [ANY] * len(given) + [VMEM] * (2 + len(sums)) + [ANY] * len(waits),
        out_specs=(VMEM, VMEM, VMEM),
        input_output_aliases={2 + len(given) + i: i for i in range(1 + len(sums))},
        scratch_shapes=[pltpu.VMEM((tokens, width), F32), pltpu.VMEM((tokens, width), BF16), pltpu.SemaphoreType.DMA],
        compiler_params=params(8),
        cost_estimate=LIGHT,
        name="layer_backward",
    )(facts, *given, held, state, *sums, *waits)


def weight_kernel(plan, facts, sums, state, *refs):
    keep, give, result, out_sems = refs[-4:]
    width, run = plan.width, plan.micros * plan.tokens
    part = width // GROUPS

    def value_of(name, block=0):
        at = plan.spans[name].start + block * width
        return state[:, :, at : at + width].reshape(run, width)

    sent = []

    def put(half, grad, groups, row, rows):
        grad = grad.astype(BF16)
        for index, group in enumerate(groups):
            result[half, facts[0, SPOT + group], row : row + rows] = grad[index * rows : (index + 1) * rows]

    def send(half, row, rows):
        source, rows = result.at[half, :, row : row + rows], pl.ds(row, rows)
        sem = out_sems.at[len(sent)]

        @pl.when(facts[0, CORE] == half)
        def _():
            pltpu.make_async_copy(source, keep.at[:, rows], sem).start()

        @pl.when(facts[0, CORE] != half)
        def _():
            pltpu.make_async_copy(source, give.at[:, rows], sem).start()

        sent.append(pltpu.make_async_copy(source, source, sem))

    everyone = range(GROUPS)
    small = sums[0]
    for micro in range(1, plan.micros):
        small = small + sums[micro]
    small = small.astype(BF16)
    for half in range(2):
        for group in everyone:
            result[half, group, 6 * part :] = small
    left = value_of("normed_one").T
    put(0, dot(left, value_of("q")), everyone, 0, part)
    put(0, dot(left, value_of("k")), everyone, part, part)
    put(1, dot(left, value_of("v")), everyone, 0, part)
    put(1, dot(value_of("mixed").T, value_of("r1")), everyone, part, part)
    send(0, 0, 2 * part)
    send(1, 0, 2 * part)
    left = value_of("normed_two").T
    for block in range(plan.blocks):
        put(0, dot(left, value_of("slope", block)), everyone, (2 + block) * part, part)
    send(0, 2 * part, 4 * part + SMALL_ROWS)
    right = value_of("upstream")
    of_block = GROUPS // plan.blocks
    for block in range(plan.blocks):
        groups = range(block * of_block, (block + 1) * of_block)
        put(1, dot(value_of("act", block).T, right), groups, 2 * part, 4 * part)
    send(1, 2 * part, 4 * part + SMALL_ROWS)
    for copy in sent:
        copy.wait()


def weight_call(plan, facts, state, sums, waits=()):
    width = plan.width
    shape = (GROUPS, 6 * width // GROUPS + SMALL_ROWS, width)
    run = plan.micros * plan.tokens
    return pl.pallas_call(
        functools.partial(weight_kernel, plan),
        out_shape=(pltpu.VMEM(shape, BF16), pltpu.VMEM(shape, BF16)),
        in_specs=[SMEM, VMEM, VMEM] + [ANY] * len(waits),
        out_specs=(VMEM, VMEM),
        scratch_shapes=[pltpu.VMEM((2, *shape), BF16), pltpu.SemaphoreType.DMA((4,))],
        compiler_params=params(12),
        cost_estimate=LIGHT,
        name="weight_grads",
    )(facts, sums, state, *waits)


def halves_kernel(facts, *refs):
    inputs, outs, landed, (whole, sems) = refs[:10], refs[10:16], refs[16:26], refs[26:]
    copies = [pltpu.make_async_copy(source, target, sems.at[i]) for i, (source, target) in enumerate(zip(inputs, landed))]
    for copy in copies:
        copy.start()
    w_qkv, w_out, w_up, w_down, *vectors = landed
    part, width = w_out.shape[1:]
    for copy in copies[4:]:
        copy.wait()
    lane = lax.broadcasted_iota(jnp.int32, (1, width), 1)
    rows = []
    for vector in vectors:
        size = vector.shape[1]
        spread = jnp.concatenate([vector[...]] * (width // size), axis=1)
        for row in range(size * GROUPS // width):
            rows.append(jnp.where((lane + row * width) // size == facts[0, PLACE], spread, 0.0))
    rows.append(jnp.zeros((SMALL_ROWS - len(rows), width), F32))
    small = jnp.concatenate(rows, axis=0).astype(BF16)
    first, second = whole.at[0], whole.at[1]
    first[6 * part :] = small
    second[6 * part :] = small
    copies[0].wait()
    for i in range(2):
        first[i * part : (i + 1) * part] = w_qkv[0, :, i * width : (i + 1) * width].astype(BF16)
    second[:part] = w_qkv[0, :, 2 * width :].astype(BF16)
    copies[1].wait()
    second[part : 2 * part] = w_out[0].astype(BF16)
    copies[2].wait()
    for i in range(w_up.shape[2] // width):
        first[(2 + i) * part : (3 + i) * part] = w_up[0, :, i * width : (i + 1) * width].astype(BF16)
    copies[3].wait()
    second[2 * part : 6 * part] = w_down[0].astype(BF16)
    cut = outs[0].shape[0]
    for i, rows in enumerate((slice(0, cut), slice(cut, None))):
        outs[i][...] = first[rows]
        outs[2 + i][...] = second[rows]
        outs[4 + i][...] = whole[1 - facts[0, CORE], rows]


def halves_call(facts, matrices, vectors, cut):
    _, part, width = matrices[1].shape
    rows = 6 * part + SMALL_ROWS
    shapes = [pltpu.VMEM((size, width), BF16) for size in (cut, rows - cut)]
    inputs = (*matrices, *vectors)
    outs = pl.pallas_call(
        halves_kernel,
        out_shape=tuple(shapes * 3),
        in_specs=[SMEM] + [ANY] * len(inputs),
        out_specs=tuple([VMEM] * 6),
        scratch_shapes=[pltpu.VMEM(value.shape, F32) for value in inputs]
        + [pltpu.VMEM((2, rows, width), BF16), pltpu.SemaphoreType.DMA((len(inputs),))],
        compiler_params=params(8),
        cost_estimate=LIGHT,
        name="round_shard",
    )(facts, *in_hbm(inputs))
    return outs[:2], outs[2:4], outs[4:]


def assemble_kernel(facts, mine, theirs, *refs):
    out, landed, wide, sems = refs[-4:]
    copies = [pltpu.make_async_copy(source, landed.at[i], sems.at[i]) for i, source in enumerate((mine, theirs))]
    for copy in copies:
        copy.start()
    saves = []
    for i, copy in enumerate(copies):
        copy.wait()
        wide[i] = landed[i].astype(F32)
        half = facts[0, CORE] if i == 0 else 1 - facts[0, CORE]
        saves.append(pltpu.make_async_copy(wide.at[i], out.at[half], sems.at[2 + i]))
        saves[-1].start()
    for copy in saves:
        copy.wait()


def assemble(facts, mine, theirs, waits):
    rows, width = mine.shape
    return pl.pallas_call(
        assemble_kernel,
        out_shape=jax.ShapeDtypeStruct((2, rows, width), F32),
        in_specs=[SMEM] + [ANY] * (2 + len(waits)),
        out_specs=ANY,
        scratch_shapes=[
            pltpu.VMEM((2, rows, width), BF16),
            pltpu.VMEM((2, rows, width), F32),
            pltpu.SemaphoreType.DMA((4,)),
        ],
        compiler_params=params(6),
        cost_estimate=LIGHT,
        name="assemble",
    )(facts, mine, theirs, *waits)


def unpack_kernel(counts, facts, *refs):
    total = 4 * sum(counts)
    options, outs, (landed, sems) = refs[:total], refs[total : total + 10], refs[total + 10 :]
    grad_qkv, grad_out, grad_up, grad_down, *vectors = outs
    for section in range(4):

        @pl.when(facts[0, STAGE] * 2 + facts[0, CORE] == section)
        def _():
            for half, count in enumerate(counts):
                row = 0
                for i in range(count):
                    source = options[4 * (sum(counts[:half]) + i) + section]
                    target = landed.at[half, pl.ds(row, source.shape[0])]
                    pltpu.make_async_copy(source, target, sems.at[half]).start()
                    row += source.shape[0]

    for half in range(2):
        pltpu.make_async_copy(landed.at[half], landed.at[half], sems.at[half]).wait()
    part, width = grad_out.shape[1:]
    block = lambda half, first, count=1: landed[half, first * part : (first + count) * part].astype(F32)
    grad_qkv[0, :, :width] = block(0, 0)
    grad_qkv[0, :, width : 2 * width] = block(0, 1)
    grad_qkv[0, :, 2 * width :] = block(1, 0)
    grad_out[0] = block(1, 1)
    for i in range(grad_up.shape[2] // width):
        grad_up[0, :, i * width : (i + 1) * width] = block(0, 2 + i)
    grad_down[0] = block(1, 2, 4)
    small = landed[0, 6 * part :].astype(F32)
    for place in range(GROUPS):

        @pl.when(facts[0, PLACE] == place)
        def _():
            row = 0
            for vector in vectors:
                size = vector.shape[1]
                first = row * width + place * size
                lanes = first % width
                vector[...] = small[first // width : first // width + 1, lanes : lanes + size]
                row += size * GROUPS // width


def unpack(facts, first, second, shapes):
    given = [option for parts in (first, second) for options in parts for option in options]
    rows = sum(options[0].shape[0] for options in first)
    return pl.pallas_call(
        functools.partial(unpack_kernel, (len(first), len(second))),
        out_shape=tuple(jax.ShapeDtypeStruct(shape, F32) for shape in shapes),
        in_specs=[SMEM] + [ANY] * len(given),
        out_specs=tuple([VMEM] * len(shapes)),
        scratch_shapes=[pltpu.VMEM((2, rows, first[0][0].shape[1]), BF16), pltpu.SemaphoreType.DMA((2,))],
        compiler_params=params(8),
        cost_estimate=LIGHT,
        name="unpack",
    )(facts, *given)


CYCLE = (0, 2, 4, 6, 7, 5, 3, 1)
OFFSETS = (0, -1, 1, -2, 2, -3, 3, 4)
CALLS = 2 * (1 + MICRO)


def row(stage, micro=None):
    return stage * (1 + MICRO) + (0 if micro is None else 1 + micro)


def send(value, pairs):
    return lax.ppermute(value, "section", pairs)


def to_core(value):
    return send(value, [(i, i ^ 1) for i in range(4)])


def onward(value):
    return send(value, [(0, 2), (1, 3)])


def backward(value):
    return send(value, [(2, 0), (3, 1)])


def along(value, by):
    size = len(CYCLE)
    return lax.ppermute(value, "dp", [(CYCLE[i], CYCLE[(i + by) % size]) for i in range(size)])


class Ring:
    def __init__(self, piece, low, high, cut):
        self.low, self.high, self.cut = low, high, cut
        self.arrived, self.places = [piece], [(0, low, high)]

    def step(self, *waits):
        ahead, behind = (self.arrived * 2)[-2:]
        if waits:
            ahead, behind = after(ahead, *waits), after(behind, *waits)
            self.arrived[-2:] = [ahead, behind]
        self.arrived += along(ahead, 1), along(behind, -1)
        self.places += [(len(self.places) + i, self.low, self.high) for i in range(2)]

    def last_step(self, *waits):
        ahead, behind = self.arrived[-2:]
        if self.cut == self.high:
            self.arrived.append(along(ahead, 1))
            self.places.append((7, self.low, self.high))
        elif self.cut == self.low:
            self.arrived.append(along(behind, -1))
            self.places.append((7, self.low, self.high))
        else:
            ahead, behind = split(ahead, behind, self.cut, *waits)
            self.arrived += along(ahead, 1), along(behind, -1)
            self.places += (7, self.low, self.cut), (7, self.cut, self.high)
            return ahead


class Gather:
    def __init__(self, facts, rings):
        self.facts, self.rings, self.done, self.swapped, self.held = facts, rings, 0, [], None

    def swap(self, count, *waits):
        span = slice(self.done, count)
        pieces = [piece for ring in self.rings for piece in ring.arrived[span]]
        places = tuple(place for ring in self.rings for place in ring.places[span])
        self.done = count
        sent = bundle(pieces, waits)
        self.swapped.append((places, sent, to_core(sent)))
        return sent

    def lay_out(self, *waits):
        places, own, other = self.swapped.pop(0)
        self.held = gather_call(self.facts, places, own, other, self.held, waits)
        return self.held


class Scatter:
    def __init__(self, held, low, high, cut):
        self.held, self.low, self.high, self.cut = held, low, high, cut
        self.next, self.arrived = 4, {}

    def step(self, *waits):
        low, high, cut, step, at = self.low, self.high, self.cut, self.next, OFFSETS.index
        if step == 4:
            ways = [(way, at(4), a, b) for way, a, b in ((1, low, cut), (-1, cut, high)) if a < b]
        elif step:
            ways = [(1, at(step), low, high), (-1, at(-step), low, high)]
        else:
            ways = [(0, at(0), low, high)]
        arrived = list(self.arrived.items())
        parts_of = lambda way: tuple(i for i, (came, _) in enumerate(arrived) if not way or came == way)
        sums = tuple((place, a, b, parts_of(way)) for way, place, a, b in ways)
        cuts = tuple(cut if step == 3 and way == -1 else low for way, _ in arrived)
        parts = ring_add(self.held, [part for _, part in arrived], cuts, sums, waits)
        self.next -= 1
        if step:
            self.arrived = {way: along(part, way) for (way, _, _, _), part in zip(ways, parts)}
        else:
            self.total = parts[0]
        return parts[0]


def facts_table(dp_count):
    ring = dp_count == len(CYCLE)
    table = np.zeros((4, dp_count, CALLS, FACTS), np.int32)
    for section in range(4):
        core, stage = section % 2, section // 2
        for place in range(dp_count):
            rows = table[section, place]
            rows[:, CORE], rows[:, STAGE], rows[:, PLACE] = core, stage, place
            for i, offset in enumerate(OFFSETS):
                owner = CYCLE[(CYCLE.index(place) + offset) % dp_count] if ring else i
                rows[:, ORDER + i], rows[:, SPOT + owner] = owner, i
            rows[row(stage) : row(stage) + 1 + MICRO, RUNS] = 1
            for micro in range(MICRO):
                rows[row(stage, micro), SLOT] = micro
    return table


def on_device(
    frames_in,
    segment_ids,
    cotangent,
    w_qkv,
    w_out,
    w_up,
    w_down,
    norm1_gain,
    norm1_shift,
    norm2_gain,
    norm2_shift,
    up_bias,
    down_bias,
):
    section = lax.axis_index("section")
    dp_index, dp_count = lax.axis_index("dp"), lax.axis_size("dp")
    rows, frame_count, width = frames_in.shape
    hidden_units = w_up.shape[2]
    own_rows = rows // 2
    tokens = own_rows * frame_count // MICRO
    ring = dp_count == len(CYCLE)
    part = w_qkv.shape[1]
    cut = 3 * width // GROUPS
    plan = Plan(MICRO, tokens, width, hidden_units)

    table = jnp.asarray(facts_table(dp_count))
    facts = lax.dynamic_slice(table, (section, dp_index, 0, 0), (1, 1) + table.shape[2:])[0, 0]

    matrices = (w_qkv, w_out, w_up, w_down)
    vectors = (norm1_gain, norm1_shift, norm2_gain, norm2_shift, down_bias, up_bias)
    if ring:
        height = 2 * cut + SMALL_ROWS
        one, two, spare = halves_call(facts, matrices, vectors, cut)
        near = [to_core(part_of) for part_of in spare]
        first_parts = [pick(facts, [(one[i], near[i]) * 2])[0] for i in range(2)]
        spans = ((0, cut), (cut, height))
        rings = [Ring(piece, *span, cut) for piece, span in zip(first_parts, spans)]
        for _ in range(3):
            for each in rings:
                each.step()
        for each in rings:
            each.last_step()
        second_parts = pick(
            facts, *([(near[i], two[i]) * 2] for i in range(2)), waits=[each.arrived[-1] for each in rings]
        )
        second_rings = [Ring(piece, *span, cut) for piece, span in zip(second_parts, spans)]
        for _ in range(2):
            for each in second_rings:
                each.step()
        gather = Gather(facts, rings)
        token = gather.swap(5, *(part_of for each in rings for part_of in each.arrived[5:7]))
        token = gather.swap(8, token)
        token = gather.lay_out(token)
        token = gather.lay_out(token)
        held = [gather.held]
    else:
        token = facts
        blocks = [w_qkv[0, :, :width], w_qkv[0, :, width : 2 * width]]
        blocks += [w_up[0, :, i * width : (i + 1) * width] for i in range(hidden_units // width)]
        blocks += [w_qkv[0, :, 2 * width :], w_out[0], w_down[0]]
        whole = jnp.concatenate([lax.all_gather(block.astype(BF16), "dp", axis=0, tiled=True) for block in blocks])
        flat = [lax.all_gather(vector[0].astype(BF16), "dp", axis=0, tiled=True) for vector in vectors]
        small = jnp.concatenate(flat + [jnp.zeros(((SMALL_ROWS - 5) * width - hidden_units,), BF16)])
        grouped = lambda low, count: jnp.swapaxes(
            whole[low * width : (low + count) * width].reshape(count, GROUPS, -1, width), 0, 1
        ).reshape(GROUPS, -1, width)
        small = jnp.pad(small.reshape(1, SMALL_ROWS, width), ((0, GROUPS - 1), (0, 0), (0, 0)))
        down = whole[8 * width :].reshape(GROUPS, -1, width)
        value = jnp.stack(
            [jnp.concatenate([grouped(0, 6), small], 1), jnp.concatenate([grouped(6, 2), down, small], 1)]
        )
        got = lax.all_gather(value, "section")
        held = [jnp.where(section < 2, got[i], got[i + 2]) for i in (0, 1)]

    segments = lax.dynamic_slice_in_dim(segment_ids, section % 2 * own_rows, own_rows, 0).reshape(-1, 128)
    spot = jnp.arange(128, dtype=jnp.int32)
    allowed = (spot[None, :] <= spot[:, None]) & (spot[None, :] // frame_count == spot[:, None] // frame_count)
    allowed = allowed[None] & (segments[:, :, None] == segments[:, None, :])
    bias = jnp.where(allowed, 0.0, -1e30).astype(F32).reshape(MICRO, tokens, 128)
    frames = frames_in.reshape(2 * MICRO, tokens, width)
    last_grads = cotangent.reshape(2 * MICRO, tokens, width)

    states, sums = [None, None], [None, None]

    def run_forward(layer, stage, micro, source, token):
        kind, *refs = source
        sources, kinds = ([refs, []], (kind, "")) if stage == 0 else ([[], refs], ("", kind))
        states[layer], low = forward_call(
            plan, row(stage, micro), micro is None, facts, sources, kinds, bias, held[layer], states[layer], (token,)
        )
        return low

    def run_backward(layer, stage, micro, source, token):
        kind, *refs = source
        sources, kinds = ([refs, []], (kind, "")) if stage == 0 else ([[], refs], ("", kind))
        states[layer], sums[layer], low = backward_call(
            plan, row(stage, micro), micro is None, facts, sources, kinds, held[layer], states[layer], sums[layer], (token,)
        )
        return low

    token = stage_zero_low = run_forward(0, 0, None, ("core", frames), token)
    if ring:
        for each in second_rings:
            each.step(token)
        for each in second_rings:
            each.last_step()
        gather = Gather(facts, second_rings)
        token = gather.swap(5, *(part_of for each in second_rings for part_of in each.arrived[5:7]), token)
        token = gather.swap(8, token)
        token = gather.lay_out(token)
        token = gather.lay_out(token)
        held.append(gather.held)
    hops = []
    for micro in range(MICRO):
        token = run_forward(1, 0, micro, ("slot", stage_zero_low), token)
        hops.append(onward(token))
    lows = []
    for micro in range(MICRO):
        token = run_forward(0, 1, micro, ("one", hops[micro]), token)
        lows.append(token)
    token = run_forward(1, 1, None, ("each", *lows), token)
    token = stage_one_back = run_backward(1, 1, None, ("core", last_grads), token)
    hops = []
    for micro in range(MICRO):
        token = run_backward(0, 1, micro, ("slot", stage_one_back), token)
        hops.append(backward(token))
    lows = []
    for micro in range(MICRO):
        token = run_backward(1, 0, micro, ("one", hops[micro]), token)
        lows.append(token)

    def whole_rows(name, token):
        mine, theirs = (states[layer][:, :, plan.spans[name]].reshape(-1, width) for layer in (0, 1))
        is_first = section % 2 == 0
        theirs = to_core(jnp.where(is_first, theirs, mine)), jnp.where(is_first, mine, theirs)
        return assemble(facts, theirs[1], theirs[0], (token,)).reshape(1, rows, frame_count, width)

    keep, give = weight_call(plan, facts, states[1], sums[1], (token,))
    totals = [(keep, give)]
    if ring:
        got = to_core(give)
        token = run_backward(0, 0, 0, ("one", lows[0]), give)
        token = merge(keep, got, (token,))
        second = [Scatter(token, *span, cut) for span in spans]
        for each in second:
            token = each.step(token)
        for micro in range(1, MICRO):
            token = run_backward(0, 0, micro, ("one", lows[micro]), token)
        for each in second:
            token = each.step(token)
        keep, give = weight_call(plan, facts, states[0], sums[0], (token,))
        got = to_core(give)
        token = give
        for each in second:
            token = each.step(token)
        token = merge(keep, got, (token,))
        first = [Scatter(token, *span, cut) for span in spans]
        token = outputs = whole_rows("result", token)
        for each in first + second + first + second + first:
            token = each.step(token)
        token = input_grads = whole_rows("grad", token)
        for each in first + first:
            token = each.step(token)
        mine = [(one.total, two.total) for one, two in zip(first, second)]
        is_first = section % 2 == 0
        theirs = [to_core(jnp.where(is_first, two, one)) for one, two in mine]
        grads = unpack(
            facts,
            [(one, other) * 2 for (one, _), other in zip(mine, theirs)],
            [(other, two) * 2 for (_, two), other in zip(mine, theirs)],
            [value.shape for value in matrices + vectors],
        )
        return (outputs, input_grads, *grads[:8], grads[9], grads[8])
    else:
        run_backward(0, 0, None, ("each", *lows), keep)
        totals.append(weight_call(plan, facts, states[0], sums[0]))
        (late_one, late_two), (early_one, early_two) = [
            (jnp.where(section % 2 == 0, keep, give), jnp.where(section % 2 == 0, give, keep)) for keep, give in totals
        ]

        is_first = section % 2 == 0

        def to_layer(first, second):
            first, second = first.astype(F32), second.astype(F32)
            return jnp.where(is_first, first, second) + to_core(jnp.where(is_first, second, first))

        one, two = to_layer(early_one, late_one), to_layer(early_two, late_two)
        small = lax.psum(one[0, 6 * width // GROUPS :], "dp")
        block = width // GROUPS
        natural = lambda half, low, high: lax.psum_scatter(
            half[:, low * block : high * block].reshape(-1, width), "dp", scatter_dimension=0, tiled=True
        )
        first_grads = [natural(one, i, i + 1) for i in range(6)]
        second_grads = [natural(two, 0, 1), natural(two, 1, 2), natural(two, 2, 6)]
    grad_vectors = [lax.dynamic_slice_in_dim(small[i : i + 1].reshape(-1), dp_index * part, part) for i in range(5)]
    grad_vectors.append(
        lax.dynamic_slice_in_dim(small[5 : 5 + hidden_units // width].reshape(-1), dp_index * 4 * part, 4 * part)
    )
    grad_vectors = [vector[None].astype(F32) for vector in grad_vectors]

    outputs, input_grads = whole_rows("result", small), whole_rows("grad", small)
    return (
        outputs,
        input_grads,
        jnp.concatenate([first_grads[0], first_grads[1], second_grads[0]], axis=1)[None].astype(F32),
        second_grads[1][None].astype(F32),
        jnp.concatenate(first_grads[2:], axis=1)[None].astype(F32),
        second_grads[2][None].astype(F32),
        *grad_vectors[:4],
        grad_vectors[5],
        grad_vectors[4],
    )


def solution(mesh):
    rows = P("dp", None, None)
    matrix, vector = P("section", "dp", None), P("section", "dp")
    result = P("section", "dp", None, None)
    return jax.shard_map(
        on_device,
        mesh=mesh,
        in_specs=(rows, P("dp", None), rows) + (matrix,) * 4 + (vector,) * 6,
        out_specs=(result, result) + (matrix,) * 4 + (vector,) * 6,
        check_vma=False,
    )
```

```python
import functools

import jax
import jax.numpy as jnp
import numpy as np
from jax import lax
from jax.experimental import pallas as pl
from jax.experimental.pallas import tpu as pltpu
from jax.sharding import PartitionSpec as P

HEADS = 8
HEAD_DIM = 64
GROUPS = 8
SMALL_ROWS = 16
MICRO = 2
BF16 = jnp.bfloat16
F32 = jnp.float32
ANY = pl.BlockSpec(memory_space=pl.ANY)
SMEM = pl.BlockSpec(memory_space=pltpu.SMEM)
VMEM = pl.BlockSpec(memory_space=pltpu.VMEM)
LIGHT = pl.CostEstimate(flops=1, bytes_accessed=1, transcendentals=0)
CORE, STAGE, PLACE, ORDER, SPOT = 0, 1, 2, 4, 12
FACTS = 20


class Plan:
    def __init__(self, micros, tokens, width, hidden_units):
        self.micros, self.tokens, self.width, self.hidden_units = micros, tokens, width, hidden_units
        self.blocks = hidden_units // width
        self.spans, at = {}, 0
        sizes = dict(hidden=1, q=1, k=1, v=1, probs=HEADS * 128 // width, mixed=1, middle=2, act=self.blocks, slope=self.blocks,
                     result=1, upstream=1, normed_two=1, r1=1, normed_one=1, grad=1)
        for name, size in sizes.items():
            self.spans[name] = slice(at, at + size * width)
            at += size * width
        self.state = pltpu.VMEM((micros, tokens, at), BF16)


def dot(left, right):
    return lax.dot_general(left, right, (((1,), (0,)), ((), ())), preferred_element_type=F32)


def dot_rhs_t(left, right):
    return lax.dot_general(left, right, (((1,), (1,)), ((), ())), preferred_element_type=F32)


def dot_lhs_t(left, right):
    return lax.dot_general(left, right, (((0,), (0,)), ((), ())), preferred_element_type=F32)


def in_hbm(values):
    return [pltpu.with_memory_space_constraint(value, pltpu.HBM) for value in values]


def params(mebibytes):
    return pltpu.CompilerParams(vmem_limit_bytes=mebibytes << 20)


def after(value, *others):
    return pl.pallas_call(
        lambda *refs: None,
        out_shape=jax.ShapeDtypeStruct(value.shape, value.dtype),
        in_specs=[pl.BlockSpec(memory_space=pl.ANY)] * (1 + len(others)),
        out_specs=pl.BlockSpec(memory_space=pl.ANY),
        input_output_aliases={0: 0},
        compiler_params=params(1),
        cost_estimate=LIGHT,
        name="after",
    )(value, *others)


def bundle_kernel(count, *refs):
    pieces, (out, sem) = refs[:count], refs[-2:]
    copies, at = [], 0
    for piece in pieces:
        copies.append(pltpu.make_async_copy(piece, out.at[pl.ds(at, piece.shape[0])], sem))
        copies[-1].start()
        at += piece.shape[0]
    pltpu.make_async_copy(out, out, sem).wait()


def bundle(pieces, waits=()):
    rows = sum(piece.shape[0] for piece in pieces)
    return pl.pallas_call(
        functools.partial(bundle_kernel, len(pieces)),
        out_shape=pltpu.VMEM((rows, pieces[0].shape[1]), BF16),
        in_specs=[ANY] * (len(pieces) + len(waits)),
        out_specs=VMEM,
        scratch_shapes=[pltpu.SemaphoreType.DMA],
        compiler_params=params(2),
        cost_estimate=LIGHT,
        name="bundle",
    )(*pieces, *waits)


def gather_kernel(places, facts, own, other, *refs):
    held = refs[-1]
    at = 0
    for place, low, high in places:
        for ref, half in ((own, facts[0, CORE]), (other, 1 - facts[0, CORE])):
            held[half, facts[0, ORDER + place], low:high] = ref[at : at + high - low]
        at += high - low


def gather_call(facts, places, own, other, held, waits=()):
    held = () if held is None else (held,)
    width = own.shape[1]
    rows = 6 * width // GROUPS + SMALL_ROWS
    return pl.pallas_call(
        functools.partial(gather_kernel, places),
        out_shape=pltpu.VMEM((2, GROUPS, rows, width), BF16),
        in_specs=[SMEM, VMEM, VMEM] + [VMEM] * len(held) + [ANY] * len(waits),
        out_specs=VMEM,
        input_output_aliases={3: 0} if held else {},
        compiler_params=params(5),
        cost_estimate=LIGHT,
        name="lay_out_weights",
    )(facts, own, other, *held, *waits)


def weight_block(held, width, block):
    part = width // GROUPS
    if block < 6:
        return held[0, :, block * part : (block + 1) * part, :].reshape(width, width)
    if block < 8:
        return held[1, :, (block - 6) * part : (block - 5) * part, :].reshape(width, width)
    first = (block - 8) * 2
    return held[1, first : first + 2, 2 * part : 6 * part, :].reshape(width, width)


def small_rows(held, width):
    total = held[0, 0, 6 * width // GROUPS :].astype(F32)
    for group in range(1, GROUPS):
        total = total + held[0, group, 6 * width // GROUPS :].astype(F32)
    return total


def pick_kernel(parts, facts, *refs):
    outs, sems = refs[-1 - len(parts) : -1], refs[-1]
    options = refs[: 4 * sum(parts)]
    for section in range(4):

        @pl.when(facts[0, STAGE] * 2 + facts[0, CORE] == section)
        def _():
            copies, at = [], 0
            for out, count in zip(outs, parts):
                row = 0
                for i in range(count):
                    source = options[at + 4 * i + section]
                    copies.append(
                        pltpu.make_async_copy(source, out.at[pl.ds(row, source.shape[0])], sems.at[len(copies)])
                    )
                    row += source.shape[0]
                at += 4 * count
            for copy in copies:
                copy.start()
            for copy in copies:
                copy.wait()


def pick(facts, *choices, waits=()):
    shapes = [
        pltpu.VMEM((sum(options[0].shape[0] for options in parts), parts[0][0].shape[1]), BF16) for parts in choices
    ]
    given = [option for parts in choices for options in parts for option in options]
    return pl.pallas_call(
        functools.partial(pick_kernel, tuple(len(parts) for parts in choices)),
        out_shape=tuple(shapes),
        in_specs=[SMEM] + [ANY] * (len(given) + len(waits)),
        out_specs=tuple([VMEM] * len(choices)),
        scratch_shapes=[pltpu.SemaphoreType.DMA((sum(len(parts) for parts in choices),))],
        compiler_params=params(3),
        cost_estimate=LIGHT,
        name="pick",
    )(facts, *(in_hbm(given) if waits else given), *waits)


def split_kernel(first, second, low, high, sems):
    copies = [
        pltpu.make_async_copy(first.at[pl.ds(0, low.shape[0])], low, sems.at[0]),
        pltpu.make_async_copy(second.at[pl.ds(low.shape[0], high.shape[0])], high, sems.at[1]),
    ]
    for copy in copies:
        copy.start()
    for copy in copies:
        copy.wait()


def split(first, second, cut, *waits):
    rows, width = first.shape
    return pl.pallas_call(
        lambda *refs: split_kernel(*refs[:2], *refs[2 + len(waits) :]),
        out_shape=(pltpu.VMEM((cut, width), BF16), pltpu.VMEM((rows - cut, width), BF16)),
        in_specs=[ANY] * (2 + len(waits)),
        out_specs=(VMEM, VMEM),
        scratch_shapes=[pltpu.SemaphoreType.DMA((2,))],
        compiler_params=params(3),
        cost_estimate=LIGHT,
        name="split",
    )(first, second, *waits)


def merge_kernel(keep, got, *refs):
    out, landed, sems = refs[-3:]
    copies = [pltpu.make_async_copy(got.at[i], landed.at[i], sems.at[i]) for i in range(got.shape[0])]
    for copy in copies:
        copy.start()
    for i, copy in enumerate(copies):
        copy.wait()
        out[i] = keep[i] + landed[i]


def merge(keep, got, waits=()):
    return pl.pallas_call(
        merge_kernel,
        out_shape=pltpu.VMEM(keep.shape, BF16),
        in_specs=[VMEM, ANY] + [ANY] * len(waits),
        out_specs=VMEM,
        input_output_aliases={0: 0},
        scratch_shapes=[pltpu.VMEM(keep.shape, BF16), pltpu.SemaphoreType.DMA((keep.shape[0],))],
        compiler_params=params(6),
        cost_estimate=LIGHT,
        name="merge",
    )(keep, got, *waits)


def ring_add_kernel(sums, cuts, n_arrived, n_waits, held, *refs):
    arrived = refs[:n_arrived]
    outs = refs[n_arrived + n_waits :]
    for (block, low, high, parts), out in zip(sums, outs):
        edges = sorted({low, high} | {cuts[p] for p in parts} | {cuts[p] + arrived[p].shape[0] for p in parts})
        for a, b in zip(edges, edges[1:]):
            total = held[block, a:b].astype(F32)
            for p in parts:
                if cuts[p] <= a and b <= cuts[p] + arrived[p].shape[0]:
                    total = total + arrived[p][a - cuts[p] : b - cuts[p]].astype(F32)
            out[a - low : b - low] = total.astype(BF16)


def ring_add(held, arrived, cuts, sums, waits=()):
    width = held.shape[2]
    return pl.pallas_call(
        functools.partial(ring_add_kernel, sums, cuts, len(arrived), len(waits)),
        out_shape=tuple(pltpu.VMEM((high - low, width), BF16) for _, low, high, _ in sums),
        in_specs=[VMEM] * (1 + len(arrived)) + [ANY] * len(waits),
        out_specs=tuple([VMEM] * len(sums)),
        compiler_params=params(5),
        cost_estimate=LIGHT,
        name="ring_add",
    )(held, *arrived, *waits)


def normalise(values):
    center = values - jnp.mean(values, axis=-1, keepdims=True)
    spread = jnp.mean(center * center, axis=-1, keepdims=True)
    scale = lax.rsqrt(spread + 1e-05)
    return center * scale, scale


def norm_back(grad, gain, unit, scale):
    grad_unit = grad * gain
    mean_grad = jnp.mean(grad_unit, axis=-1, keepdims=True)
    mean_dot = jnp.mean(grad_unit * unit, axis=-1, keepdims=True)
    return scale * (grad_unit - mean_grad - unit * mean_dot)


def stack_heads(pair, low_lanes):
    zero = jnp.zeros_like(pair)
    return jnp.concatenate([jnp.where(low_lanes, pair, zero), jnp.where(low_lanes, zero, pair)], axis=0)


def load_source(slot, kind, refs, target, sem):
    if kind == "each":
        for micro, ref in enumerate(refs):

            @pl.when(slot == micro)
            def _():
                pltpu.make_async_copy(ref, target, sem).start()

    else:
        pltpu.make_async_copy(refs[0].at[slot] if kind == "slot" else refs[0], target, sem).start()


def for_slots(flag, micros, micro, work):
    @pl.when(jnp.max(flag[...]) > 0.5)
    def _():
        if micro is None:
            pl.loop(0, micros)(work)
        else:
            work(micro)


def forward_kernel(plan, micro, kind, count, has_state, n_waits, flag, *refs):
    sources, whole = refs[:count], micro is None
    bias_v, held = refs[count : count + 2]
    state, low_o, sem = refs[count + 2 + int(has_state) + n_waits :]
    tokens, width = plan.tokens, plan.width
    weight = lambda block: weight_block(held, width, block)

    def work(slot):
        value_of = lambda name: state.at[slot, :, plan.spans[name]]
        low_v = low_o.at[slot] if whole else low_o
        hidden_v, q_v, k_v, v_v, probs_v, mixed_v, middle_v, act_v, slope_v = (
            value_of(name) for name in ("hidden", "q", "k", "v", "probs", "mixed", "middle", "act", "slope")
        )
        load_source(slot, kind, sources, hidden_v, sem)
        small = small_rows(held, width)
        gain_one, shift_one, gain_two, shift_two, down_bias = (small[i : i + 1] for i in range(5))
        pltpu.make_async_copy(hidden_v, hidden_v, sem).wait()
        hidden = hidden_v[...].astype(F32)
        unit, _ = normalise(hidden)
        normed = (unit * gain_one + shift_one).astype(BF16)
        q_v[...] = (dot(normed, weight(0)) * HEAD_DIM**-0.5).astype(BF16)
        k_v[...] = dot(normed, weight(1)).astype(BF16)
        v_v[...] = dot(normed, weight(6)).astype(BF16)
        low_lanes = lax.broadcasted_iota(jnp.int32, (128, 128), 1) < HEAD_DIM
        for group in range(tokens // 128):
            rows = slice(group * 128, group * 128 + 128)
            bias = bias_v[slot, rows]
            bias = jnp.concatenate([bias, bias], axis=0)
            for pair in range(width // 128):
                lanes = slice(pair * 128, pair * 128 + 128)
                query = stack_heads(q_v[rows, lanes], low_lanes)
                scores = dot_rhs_t(query, k_v[rows, lanes]) + bias
                raised = jnp.exp(scores - jnp.max(scores, axis=-1, keepdims=True))
                probs = (raised * (1.0 / jnp.sum(raised, axis=-1, keepdims=True))).astype(BF16)
                probs_v[rows, pair * 256 : pair * 256 + 128] = probs[:128]
                probs_v[rows, pair * 256 + 128 : pair * 256 + 256] = probs[128:]
                mixed = dot(probs, v_v[rows, lanes])
                mixed_v[rows, lanes] = jnp.where(low_lanes, mixed[:128], mixed[128:]).astype(BF16)
        middle = hidden + dot(mixed_v[...], weight(7))
        high = middle.astype(BF16)
        middle_v[:, :width] = high
        middle_v[:, width:] = (middle - high.astype(F32)).astype(BF16)
        unit, _ = normalise(middle)
        normed = (unit * gain_two + shift_two).astype(BF16)
        total = middle + down_bias
        for block in range(plan.blocks):
            lanes = slice(block * width, (block + 1) * width)
            before = dot(normed, weight(2 + block)) + small[5 + block : 6 + block]
            square = before * before
            tanh = jnp.tanh(before * (0.7978845608028654 + 0.035677408136300125 * square))
            half = 0.5 * tanh + 0.5
            act = (before * half).astype(BF16)
            act_v[:, lanes] = act
            slope = half + before * (0.5 - 0.5 * (tanh * tanh)) * (0.7978845608028654 + 0.10703222440890037 * square)
            slope_v[:, lanes] = slope.astype(BF16)
            total = total + dot(act, weight(8 + block))
        low = total.astype(BF16)
        low_v[...] = low
        value_of("result")[...] = low

    for_slots(flag, plan.micros, micro, work)


def forward_call(plan, flag, micro, source, bias, held, state, waits=()):
    kind, *given = source
    state = [] if state is None else [state]
    tokens, width = plan.tokens, plan.width
    low = ((plan.micros,) if micro is None else ()) + (tokens, width)
    return pl.pallas_call(
        functools.partial(forward_kernel, plan, micro, kind, len(given), bool(state), len(waits)),
        out_shape=(plan.state, pltpu.VMEM(low, BF16)),
        in_specs=[VMEM] + [ANY] * len(given) + [VMEM] * (2 + len(state)) + [ANY] * len(waits),
        out_specs=(VMEM, VMEM),
        input_output_aliases={3 + len(given): 0} if state else {},
        scratch_shapes=[pltpu.SemaphoreType.DMA],
        compiler_params=params(8),
        cost_estimate=LIGHT,
        name="layer_forward",
    )(flag, *given, bias, held, *state, *waits)


def backward_kernel(plan, micro, kind, count, has_sums, n_waits, flag, *refs):
    sources, whole = refs[:count], micro is None
    held = refs[count]
    state, sums_o, low_o, grad_v, do_v, sem = refs[count + 2 + int(has_sums) + n_waits :]
    tokens, width = plan.tokens, plan.width
    weight = lambda block: weight_block(held, width, block)

    def work(slot):
        value_of = lambda name: state.at[slot, :, plan.spans[name]]
        low_v = low_o.at[slot] if whole else low_o
        upstream_v, hidden_v, q_v, k_v, v_v, probs_v, middle_v, du_v = (
            value_of(name) for name in ("upstream", "hidden", "q", "k", "v", "probs", "middle", "slope")
        )
        load_source(slot, kind, sources, upstream_v, sem)
        small = small_rows(held, width)
        gain_one, shift_one, gain_two, shift_two = (small[i : i + 1] for i in range(4))
        sums_v = sums_o.at[slot]
        sums_v[...] = jnp.zeros(sums_v.shape, F32)
        pltpu.make_async_copy(upstream_v, upstream_v, sem).wait()
        upstream_low = upstream_v[...]
        upstream = upstream_low.astype(F32)
        sums_v[4:5] = jnp.sum(upstream, axis=0, keepdims=True)
        da = jnp.zeros((tokens, width), F32)
        for block in range(plan.blocks):
            lanes = slice(block * width, (block + 1) * width)
            dz = dot_rhs_t(upstream_low, weight(8 + block))
            du = (dz * du_v[:, lanes].astype(F32)).astype(BF16)
            du_v[:, lanes] = du
            sums_v[5 + block : 6 + block] = jnp.sum(du.astype(F32), axis=0, keepdims=True)
            da = da + dot_rhs_t(du, weight(2 + block))
        unit, scale = normalise(middle_v[:, :width].astype(F32) + middle_v[:, width:].astype(F32))
        value_of("normed_two")[...] = (unit * gain_two + shift_two).astype(BF16)
        sums_v[2:3] = jnp.sum(da * unit, axis=0, keepdims=True)
        sums_v[3:4] = jnp.sum(da, axis=0, keepdims=True)
        grad_middle = upstream + norm_back(da, gain_two, unit, scale)
        grad_v[...] = grad_middle
        r1 = grad_middle.astype(BF16)
        value_of("r1")[...] = r1
        do_v[...] = dot_rhs_t(r1, weight(7)).astype(BF16)
        low_lanes = lax.broadcasted_iota(jnp.int32, (128, 128), 1) < HEAD_DIM
        for group in range(tokens // 128):
            rows = slice(group * 128, group * 128 + 128)
            for pair in range(width // 128):
                lanes = slice(pair * 128, pair * 128 + 128)
                query = stack_heads(q_v[rows, lanes], low_lanes)
                key = k_v[rows, lanes]
                grad_mixed = stack_heads(do_v[rows, lanes], low_lanes)
                probs = jnp.concatenate(
                    [probs_v[rows, pair * 256 : pair * 256 + 128], probs_v[rows, pair * 256 + 128 : pair * 256 + 256]], axis=0
                )
                grad_probs = dot_rhs_t(grad_mixed, v_v[rows, lanes])
                v_v[rows, lanes] = dot_lhs_t(probs, grad_mixed).astype(BF16)
                probs = probs.astype(F32)
                weighted = grad_probs * probs
                grad_scores = (weighted - probs * jnp.sum(weighted, axis=-1, keepdims=True)).astype(BF16)
                dq = dot(grad_scores, key) * HEAD_DIM**-0.5
                q_v[rows, lanes] = jnp.where(low_lanes, dq[:128], dq[128:]).astype(BF16)
                k_v[rows, lanes] = dot_lhs_t(grad_scores, query).astype(BF16)
        unit, scale = normalise(hidden_v[...].astype(F32))
        value_of("normed_one")[...] = (unit * gain_one + shift_one).astype(BF16)
        da = dot_rhs_t(q_v[...], weight(0)) + dot_rhs_t(k_v[...], weight(1)) + dot_rhs_t(v_v[...], weight(6))
        sums_v[0:1] = jnp.sum(da * unit, axis=0, keepdims=True)
        sums_v[1:2] = jnp.sum(da, axis=0, keepdims=True)
        low = (grad_v[...] + norm_back(da, gain_one, unit, scale)).astype(BF16)
        low_v[...] = low
        value_of("grad")[...] = low

    for_slots(flag, plan.micros, micro, work)


def backward_call(plan, flag, micro, source, held, state, sums, waits=()):
    kind, *given = source
    tokens, width = plan.tokens, plan.width
    sums = [] if sums is None else [sums]
    low = ((plan.micros,) if micro is None else ()) + (tokens, width)
    return pl.pallas_call(
        functools.partial(backward_kernel, plan, micro, kind, len(given), bool(sums), len(waits)),
        out_shape=(
            plan.state,
            pltpu.VMEM((plan.micros, SMALL_ROWS, width), F32),
            pltpu.VMEM(low, BF16),
        ),
        in_specs=[VMEM] + [ANY] * len(given) + [VMEM] * (2 + len(sums)) + [ANY] * len(waits),
        out_specs=(VMEM, VMEM, VMEM),
        input_output_aliases={2 + len(given) + i: i for i in range(1 + len(sums))},
        scratch_shapes=[pltpu.VMEM((tokens, width), F32), pltpu.VMEM((tokens, width), BF16), pltpu.SemaphoreType.DMA],
        compiler_params=params(8),
        cost_estimate=LIGHT,
        name="layer_backward",
    )(flag, *given, held, state, *sums, *waits)


def weight_kernel(plan, facts, sums, state, *refs):
    targets = refs[-2:]
    width, run = plan.width, plan.micros * plan.tokens
    part = width // GROUPS

    def value_of(name, block=0):
        at = plan.spans[name].start + block * width
        return state[:, :, at : at + width].reshape(run, width)

    def put(half, grad, groups, row, rows):
        grad = grad.astype(BF16)
        for given, target in enumerate(targets):

            @pl.when((facts[0, CORE] == half) == (given == 0))
            def _():
                for index, group in enumerate(groups):
                    source = grad[index * rows : (index + 1) * rows] if grad.shape[0] > rows else grad
                    target[facts[0, SPOT + group], row : row + rows] = source

    everyone = range(GROUPS)
    small = sums[0]
    for micro in range(1, plan.micros):
        small = small + sums[micro]
    for half in range(2):
        put(half, small, everyone, 6 * part, SMALL_ROWS)
    left = value_of("normed_one").T
    put(0, dot(left, value_of("q")), everyone, 0, part)
    put(0, dot(left, value_of("k")), everyone, part, part)
    put(1, dot(left, value_of("v")), everyone, 0, part)
    put(1, dot(value_of("mixed").T, value_of("r1")), everyone, part, part)
    left = value_of("normed_two").T
    for block in range(plan.blocks):
        put(0, dot(left, value_of("slope", block)), everyone, (2 + block) * part, part)
    right = value_of("upstream")
    of_block = GROUPS // plan.blocks
    for block in range(plan.blocks):
        groups = range(block * of_block, (block + 1) * of_block)
        put(1, dot(value_of("act", block).T, right), groups, 2 * part, 4 * part)


def weight_call(plan, facts, state, sums, waits=()):
    width = plan.width
    shape = (GROUPS, 6 * width // GROUPS + SMALL_ROWS, width)
    run = plan.micros * plan.tokens
    return pl.pallas_call(
        functools.partial(weight_kernel, plan),
        out_shape=(pltpu.VMEM(shape, BF16), pltpu.VMEM(shape, BF16)),
        in_specs=[SMEM, VMEM, VMEM] + [ANY] * len(waits),
        out_specs=(VMEM, VMEM),
        compiler_params=params(8),
        cost_estimate=LIGHT,
        name="weight_grads",
    )(facts, sums, state, *waits)


def halves_kernel(facts, *refs):
    inputs, outs, landed, (whole, sems) = refs[:10], refs[10:16], refs[16:26], refs[26:]
    copies = [pltpu.make_async_copy(source, target, sems.at[i]) for i, (source, target) in enumerate(zip(inputs, landed))]
    for copy in copies:
        copy.start()
    w_qkv, w_out, w_up, w_down, *vectors = landed
    part, width = w_out.shape[1:]
    for copy in copies[4:]:
        copy.wait()
    lane = lax.broadcasted_iota(jnp.int32, (1, width), 1)
    rows = []
    for vector in vectors:
        size = vector.shape[1]
        spread = jnp.concatenate([vector[...]] * (width // size), axis=1)
        for row in range(size * GROUPS // width):
            rows.append(jnp.where((lane + row * width) // size == facts[0, PLACE], spread, 0.0))
    rows.append(jnp.zeros((SMALL_ROWS - len(rows), width), F32))
    small = jnp.concatenate(rows, axis=0).astype(BF16)
    first, second = whole.at[0], whole.at[1]
    first[6 * part :] = small
    second[6 * part :] = small
    copies[0].wait()
    for i in range(2):
        first[i * part : (i + 1) * part] = w_qkv[0, :, i * width : (i + 1) * width].astype(BF16)
    second[:part] = w_qkv[0, :, 2 * width :].astype(BF16)
    copies[1].wait()
    second[part : 2 * part] = w_out[0].astype(BF16)
    copies[2].wait()
    for i in range(w_up.shape[2] // width):
        first[(2 + i) * part : (3 + i) * part] = w_up[0, :, i * width : (i + 1) * width].astype(BF16)
    copies[3].wait()
    second[2 * part : 6 * part] = w_down[0].astype(BF16)
    cut = outs[0].shape[0]
    for i, rows in enumerate((slice(0, cut), slice(cut, None))):
        outs[i][...] = first[rows]
        outs[2 + i][...] = second[rows]
        outs[4 + i][...] = whole[1 - facts[0, CORE], rows]


def halves_call(facts, matrices, vectors, cut):
    _, part, width = matrices[1].shape
    rows = 6 * part + SMALL_ROWS
    shapes = [pltpu.VMEM((size, width), BF16) for size in (cut, rows - cut)]
    inputs = (*matrices, *vectors)
    outs = pl.pallas_call(
        halves_kernel,
        out_shape=(*shapes, *(pltpu.HBM(shape.shape, BF16) for shape in shapes), *shapes),
        in_specs=[SMEM] + [ANY] * len(inputs),
        out_specs=tuple([VMEM] * 6),
        scratch_shapes=[pltpu.VMEM(value.shape, F32) for value in inputs]
        + [pltpu.VMEM((2, rows, width), BF16), pltpu.SemaphoreType.DMA((len(inputs),))],
        compiler_params=params(8),
        cost_estimate=LIGHT,
        name="round_shard",
    )(facts, *in_hbm(inputs))
    return outs[:2], outs[2:4], outs[4:]


def assemble_kernel(facts, mine, theirs, *refs):
    out, token, landed, wide, sems = refs[-5:]
    token[...] = jnp.zeros_like(token)
    copies = [pltpu.make_async_copy(source, landed.at[i], sems.at[i]) for i, source in enumerate((mine, theirs))]
    for copy in copies:
        copy.start()
    saves = []
    for i, copy in enumerate(copies):
        copy.wait()
        wide[i] = landed[i].astype(F32)
        half = facts[0, CORE] if i == 0 else 1 - facts[0, CORE]
        saves.append(pltpu.make_async_copy(wide.at[i], out.at[half], sems.at[2 + i]))
        saves[-1].start()
    for copy in saves:
        copy.wait()


def assemble(facts, mine, theirs, waits):
    rows, width = mine.shape
    return pl.pallas_call(
        assemble_kernel,
        out_shape=(pltpu.HBM((2, rows, width), F32), pltpu.VMEM((8, 128), F32)),
        in_specs=[SMEM] + [ANY] * (2 + len(waits)),
        out_specs=(ANY, VMEM),
        scratch_shapes=[
            pltpu.VMEM((2, rows, width), BF16),
            pltpu.VMEM((2, rows, width), F32),
            pltpu.SemaphoreType.DMA((4,)),
        ],
        compiler_params=params(6),
        cost_estimate=LIGHT,
        name="assemble",
    )(facts, mine, theirs, *waits)


def unpack_kernel(counts, facts, *refs):
    total = 4 * sum(counts)
    options, outs, (landed, sems) = refs[:total], refs[total : total + 10], refs[total + 10 :]
    grad_qkv, grad_out, grad_up, grad_down, *vectors = outs
    for section in range(4):

        @pl.when(facts[0, STAGE] * 2 + facts[0, CORE] == section)
        def _():
            for half, count in enumerate(counts):
                row = 0
                for i in range(count):
                    source = options[4 * (sum(counts[:half]) + i) + section]
                    target = landed.at[half, pl.ds(row, source.shape[0])]
                    pltpu.make_async_copy(source, target, sems.at[half]).start()
                    row += source.shape[0]

    for half in range(2):
        pltpu.make_async_copy(landed.at[half], landed.at[half], sems.at[half]).wait()
    part, width = grad_out.shape[1:]
    block = lambda half, first, count=1: landed[half, first * part : (first + count) * part].astype(F32)
    grad_qkv[0, :, :width] = block(0, 0)
    grad_qkv[0, :, width : 2 * width] = block(0, 1)
    grad_qkv[0, :, 2 * width :] = block(1, 0)
    grad_out[0] = block(1, 1)
    for i in range(grad_up.shape[2] // width):
        grad_up[0, :, i * width : (i + 1) * width] = block(0, 2 + i)
    grad_down[0] = block(1, 2, 4)
    small = landed[0, 6 * part :].astype(F32)
    for place in range(GROUPS):

        @pl.when(facts[0, PLACE] == place)
        def _():
            row = 0
            for vector in vectors:
                size = vector.shape[1]
                first = row * width + place * size
                lanes = first % width
                vector[...] = small[first // width : first // width + 1, lanes : lanes + size]
                row += size * GROUPS // width


def unpack(facts, first, second, shapes):
    given = [option for parts in (first, second) for options in parts for option in options]
    rows = sum(options[0].shape[0] for options in first)
    return pl.pallas_call(
        functools.partial(unpack_kernel, (len(first), len(second))),
        out_shape=tuple(jax.ShapeDtypeStruct(shape, F32) for shape in shapes),
        in_specs=[SMEM] + [ANY] * len(given),
        out_specs=tuple([VMEM] * len(shapes)),
        scratch_shapes=[pltpu.VMEM((2, rows, first[0][0].shape[1]), BF16), pltpu.SemaphoreType.DMA((2,))],
        compiler_params=params(8),
        cost_estimate=LIGHT,
        name="unpack",
    )(facts, *given)


CYCLE = (0, 2, 4, 6, 7, 5, 3, 1)
OFFSETS = (0, -1, 1, -2, 2, -3, 3, 4)


def send(value, pairs):
    return lax.ppermute(value, "section", pairs)


def to_core(value):
    return send(value, [(i, i ^ 1) for i in range(4)])


def onward(value):
    return send(value, [(0, 2), (1, 3)])


def backward(value):
    return send(value, [(2, 0), (3, 1)])


def along(value, by):
    size = len(CYCLE)
    return lax.ppermute(value, "dp", [(CYCLE[i], CYCLE[(i + by) % size]) for i in range(size)])


class Ring:
    def __init__(self, piece, low, high, cut):
        self.low, self.high, self.cut = low, high, cut
        self.arrived, self.places = [piece], [(0, low, high)]

    def level(self, *waits):
        if len(self.arrived) > 1:
            ahead, behind = self.arrived[-2:]
            ahead = after(ahead, behind, *waits)
            self.arrived[-2:] = [ahead, after(behind, ahead)]
        return (self.arrived * 2)[-2:]

    def step(self, *waits):
        ahead, behind = self.level(*waits)
        self.arrived += along(ahead, 1), along(behind, -1)
        self.places += [(len(self.places) + i, self.low, self.high) for i in range(2)]

    def last_step(self, *waits):
        ahead, behind = self.level(*waits)
        if self.cut == self.high:
            self.arrived.append(along(ahead, 1))
            self.places.append((7, self.low, self.high))
        else:
            self.arrived.append(along(behind, -1))
            self.places.append((7, self.low, self.high))


class Gather:
    def __init__(self, facts, rings):
        self.facts, self.rings, self.done, self.swapped, self.held = facts, rings, 0, [], None

    def swap(self, count, *waits):
        span = slice(self.done, count)
        pieces = [piece for ring in self.rings for piece in ring.arrived[span]]
        places = tuple(place for ring in self.rings for place in ring.places[span])
        self.done = count
        sent = bundle(pieces, waits)
        self.swapped.append((places, sent, to_core(sent)))
        return sent

    def lay_out(self, *waits):
        places, own, other = self.swapped.pop(0)
        self.held = gather_call(self.facts, places, own, other, self.held, waits)
        return self.held


class Scatter:
    def __init__(self, held, low, high, cut):
        self.held, self.low, self.high, self.cut = held, low, high, cut
        self.next, self.arrived = 4, {}

    def step(self, *waits):
        low, high, cut, step, at = self.low, self.high, self.cut, self.next, OFFSETS.index
        if step == 4:
            ways = [(way, at(4), a, b) for way, a, b in ((1, low, cut), (-1, cut, high)) if a < b]
        elif step:
            ways = [(1, at(step), low, high), (-1, at(-step), low, high)]
        else:
            ways = [(0, at(0), low, high)]
        arrived = list(self.arrived.items())
        parts_of = lambda way: tuple(i for i, (came, _) in enumerate(arrived) if not way or came == way)
        sums = tuple((place, a, b, parts_of(way)) for way, place, a, b in ways)
        cuts = tuple(cut if step == 3 and way == -1 else low for way, _ in arrived)
        parts = ring_add(self.held, [part for _, part in arrived], cuts, sums, waits)
        self.next -= 1
        if step:
            self.arrived = {way: along(part, way) for (way, _, _, _), part in zip(ways, parts)}
        else:
            self.total = parts[0]
        return parts[0]


def facts_table(dp_count):
    ring = dp_count == len(CYCLE)
    table = np.zeros((4, dp_count, 1, FACTS), np.int32)
    for section in range(4):
        for place in range(dp_count):
            facts = table[section, place, 0]
            facts[[CORE, STAGE, PLACE]] = section % 2, section // 2, place
            for i, offset in enumerate(OFFSETS):
                owner = CYCLE[(CYCLE.index(place) + offset) % dp_count] if ring else i
                facts[ORDER + i], facts[SPOT + owner] = owner, i
    return table


def on_device(
    frames_in,
    segment_ids,
    cotangent,
    w_qkv,
    w_out,
    w_up,
    w_down,
    norm1_gain,
    norm1_shift,
    norm2_gain,
    norm2_shift,
    up_bias,
    down_bias,
):
    section = lax.axis_index("section")
    dp_index, dp_count = lax.axis_index("dp"), lax.axis_size("dp")
    rows, frame_count, width = frames_in.shape
    hidden_units = w_up.shape[2]
    own_rows = rows // 2
    tokens = own_rows * frame_count // MICRO
    ring = dp_count == len(CYCLE)
    part = w_qkv.shape[1]
    cut = 3 * width // GROUPS
    plan = Plan(MICRO, tokens, width, hidden_units)

    table = jnp.asarray(facts_table(dp_count))
    facts = lax.dynamic_slice(table, (section, dp_index, 0, 0), (1, 1) + table.shape[2:])[0, 0]

    segments = lax.dynamic_slice_in_dim(segment_ids, section % 2 * own_rows, own_rows, 0).reshape(-1, 128)
    spot = jnp.arange(128, dtype=jnp.int32)
    allowed = (spot[None, :] <= spot[:, None]) & (spot[None, :] // frame_count == spot[:, None] // frame_count)
    allowed = allowed[None] & (segments[:, :, None] == segments[:, None, :])
    bias = jnp.where(allowed, 0.0, -1e30).astype(F32).reshape(MICRO, tokens, 128)
    frames, last_grads = (
        lax.dynamic_slice_in_dim(value, section % 2 * own_rows, own_rows, 0).reshape(MICRO, tokens, width)
        for value in (frames_in, cotangent)
    )
    flags = [jnp.full((8, 128), section // 2 == stage, F32) for stage in range(2)]

    matrices = (w_qkv, w_out, w_up, w_down)
    vectors = (norm1_gain, norm1_shift, norm2_gain, norm2_shift, down_bias, up_bias)
    if ring:
        height = 2 * cut + SMALL_ROWS
        one, two, spare = halves_call(facts, matrices, vectors, cut)
        near = [to_core(part_of) for part_of in spare]
        first_parts = [pick(facts, [(one[i], near[i]) * 2])[0] for i in range(2)]
        spans = ((0, cut), (cut, height))
        rings = [Ring(piece, *span, cut) for piece, span in zip(first_parts, spans)]
        besides = (frames, last_grads, bias, *flags)
        for step in range(3):
            for each in rings:
                each.step(*(besides if step == 1 else ()))
        for each in rings:
            each.last_step()
        last = [each.arrived[-1] for each in rings]
        second_parts = [pick(facts, [(near[i], two[i]) * 2], waits=last)[0] for i in range(2)]
        second_rings = [Ring(piece, *span, cut) for piece, span in zip(second_parts, spans)]
        for _ in range(3):
            for each in second_rings:
                each.step()
        gather = Gather(facts, rings)
        token = gather.swap(5, *(each.arrived[-1] for each in rings), *second_parts)
        token = gather.swap(8, token)
        gather.lay_out(token)
        token = gather.lay_out()
        held = [gather.held]
    else:
        token = facts
        blocks = [w_qkv[0, :, :width], w_qkv[0, :, width : 2 * width]]
        blocks += [w_up[0, :, i * width : (i + 1) * width] for i in range(hidden_units // width)]
        blocks += [w_qkv[0, :, 2 * width :], w_out[0], w_down[0]]
        whole = jnp.concatenate([lax.all_gather(block.astype(BF16), "dp", axis=0, tiled=True) for block in blocks])
        flat = [lax.all_gather(vector[0].astype(BF16), "dp", axis=0, tiled=True) for vector in vectors]
        small = jnp.concatenate(flat + [jnp.zeros(((SMALL_ROWS - 5) * width - hidden_units,), BF16)])
        grouped = lambda low, count: jnp.swapaxes(
            whole[low * width : (low + count) * width].reshape(count, GROUPS, -1, width), 0, 1
        ).reshape(GROUPS, -1, width)
        small = jnp.pad(small.reshape(1, SMALL_ROWS, width), ((0, GROUPS - 1), (0, 0), (0, 0)))
        down = whole[8 * width :].reshape(GROUPS, -1, width)
        value = jnp.stack(
            [jnp.concatenate([grouped(0, 6), small], 1), jnp.concatenate([grouped(6, 2), down, small], 1)]
        )
        got = lax.all_gather(value, "section")
        held = [jnp.where(section < 2, got[i], got[i + 2]) for i in (0, 1)]

    states, sums = [None, None], [None, None]

    def run_forward(layer, stage, micro, source, token):
        states[layer], low = forward_call(
            plan, flags[stage], micro, source, bias, held[layer], states[layer], (token,)
        )
        return low

    def run_backward(layer, stage, micro, source, token):
        states[layer], sums[layer], low = backward_call(
            plan, flags[stage], micro, source, held[layer], states[layer], sums[layer], (token,)
        )
        return low

    token = stage_zero_low = run_forward(0, 0, None, ("slot", frames), token)
    if ring:
        for each in second_rings:
            each.last_step(token)
        gather = Gather(facts, second_rings)
        token = gather.swap(5, *(each.arrived[-1] for each in second_rings), token)
        token = gather.swap(8, token)
        gather.lay_out(token)
        token = gather.lay_out()
        held.append(gather.held)
    hops = []
    for micro in range(MICRO):
        token = run_forward(1, 0, micro, ("slot", stage_zero_low), token)
        hops.append(onward(token))
    lows = []
    for micro in range(MICRO):
        token = run_forward(0, 1, micro, ("one", hops[micro]), token)
        lows.append(token)
    token = run_forward(1, 1, None, ("each", *lows), token)
    token = stage_one_back = run_backward(1, 1, None, ("slot", last_grads), token)
    hops = []
    for micro in range(MICRO):
        token = run_backward(0, 1, micro, ("slot", stage_one_back), token)
        hops.append(backward(token))
    lows = []
    for micro in range(MICRO):
        token = run_backward(1, 0, micro, ("one", hops[micro]), token)
        lows.append(token)

    def whole_rows(name, token):
        mine, theirs = (states[layer][:, :, plan.spans[name]].reshape(-1, width) for layer in (0, 1))
        is_first = section % 2 == 0
        theirs = to_core(jnp.where(is_first, theirs, mine)), jnp.where(is_first, mine, theirs)
        whole, token = assemble(facts, theirs[1], theirs[0], (token,))
        return whole.reshape(1, rows, frame_count, width), token

    keep, give = weight_call(plan, facts, states[1], sums[1], (token,))
    totals = [(keep, give)]
    if ring:
        got = to_core(give)
        token = run_backward(0, 0, 0, ("one", lows[0]), give)
        token = merge(keep, got, (token,))
        second = [Scatter(token, *span, cut) for span in spans]
        for each in second:
            token = each.step(token)
        for micro in range(1, MICRO):
            token = run_backward(0, 0, micro, ("one", lows[micro]), token)
        for each in second:
            token = each.step(token)
        keep, give = weight_call(plan, facts, states[0], sums[0], (token,))
        token = give
        for each in second:
            token = each.step(token)
        got = to_core(after(give, token))
        outputs, token = whole_rows("result", token)
        token = merge(keep, got, (token,))
        first = [Scatter(token, *span, cut) for span in spans]
        for each in first + second + first + second + first:
            token = each.step(token)
        input_grads, token = whole_rows("grad", token)
        for each in first + first:
            token = each.step(token)
        mine = [(one.total, two.total) for one, two in zip(first, second)]
        is_first = section % 2 == 0
        theirs = [to_core(jnp.where(is_first, two, one)) for one, two in mine]
        grads = unpack(
            facts,
            [(one, other) * 2 for (one, _), other in zip(mine, theirs)],
            [(other, two) * 2 for (_, two), other in zip(mine, theirs)],
            [value.shape for value in matrices + vectors],
        )
        return (outputs, input_grads, *grads[:8], grads[9], grads[8])
    else:
        run_backward(0, 0, None, ("each", *lows), keep)
        totals.append(weight_call(plan, facts, states[0], sums[0]))
        (late_one, late_two), (early_one, early_two) = [
            (jnp.where(section % 2 == 0, keep, give), jnp.where(section % 2 == 0, give, keep)) for keep, give in totals
        ]

        is_first = section % 2 == 0

        def to_layer(first, second):
            first, second = first.astype(F32), second.astype(F32)
            return jnp.where(is_first, first, second) + to_core(jnp.where(is_first, second, first))

        one, two = to_layer(early_one, late_one), to_layer(early_two, late_two)
        small = lax.psum(one[0, 6 * width // GROUPS :], "dp")
        block = width // GROUPS
        natural = lambda half, low, high: lax.psum_scatter(
            half[:, low * block : high * block].reshape(-1, width), "dp", scatter_dimension=0, tiled=True
        )
        first_grads = [natural(one, i, i + 1) for i in range(6)]
        second_grads = [natural(two, 0, 1), natural(two, 1, 2), natural(two, 2, 6)]
    grad_vectors = [lax.dynamic_slice_in_dim(small[i : i + 1].reshape(-1), dp_index * part, part) for i in range(5)]
    grad_vectors.append(
        lax.dynamic_slice_in_dim(small[5 : 5 + hidden_units // width].reshape(-1), dp_index * 4 * part, 4 * part)
    )
    grad_vectors = [vector[None].astype(F32) for vector in grad_vectors]

    outputs, input_grads = whole_rows("result", small)[0], whole_rows("grad", small)[0]
    return (
        outputs,
        input_grads,
        jnp.concatenate([first_grads[0], first_grads[1], second_grads[0]], axis=1)[None].astype(F32),
        second_grads[1][None].astype(F32),
        jnp.concatenate(first_grads[2:], axis=1)[None].astype(F32),
        second_grads[2][None].astype(F32),
        *grad_vectors[:4],
        grad_vectors[5],
        grad_vectors[4],
    )


def solution(mesh):
    rows = P("dp", None, None)
    matrix, vector = P("section", "dp", None), P("section", "dp")
    result = P("section", "dp", None, None)
    return jax.shard_map(
        on_device,
        mesh=mesh,
        in_specs=(rows, P("dp", None), rows) + (matrix,) * 4 + (vector,) * 6,
        out_specs=(result, result) + (matrix,) * 4 + (vector,) * 6,
        check_vma=False,
    )
```

```python
import functools

import jax
import jax.numpy as jnp
import numpy as np
from jax import lax
from jax.experimental import pallas as pl
from jax.experimental.pallas import tpu as pltpu
from jax.sharding import PartitionSpec as P

HEADS = 8
HEAD_DIM = 64
GROUPS = 8
SMALL_ROWS = 16
MICRO = 2
BF16 = jnp.bfloat16
F32 = jnp.float32
ANY = pl.BlockSpec(memory_space=pl.ANY)
SMEM = pl.BlockSpec(memory_space=pltpu.SMEM)
VMEM = pl.BlockSpec(memory_space=pltpu.VMEM)
LIGHT = pl.CostEstimate(flops=1, bytes_accessed=1, transcendentals=0)
STEP = pl.CostEstimate(flops=3 * 10**8, bytes_accessed=1, transcendentals=0)
HEAVY = pl.CostEstimate(flops=10**10, bytes_accessed=1, transcendentals=0)
CORE, STAGE, PLACE, ORDER, SPOT = 0, 1, 2, 4, 12
FACTS = 20


class Plan:
    def __init__(self, micros, tokens, width, hidden_units):
        self.micros, self.tokens, self.width, self.hidden_units = micros, tokens, width, hidden_units
        self.blocks = hidden_units // width
        self.spans, at = {}, 0
        sizes = dict(hidden=1, q=1, k=1, v=1, probs=HEADS * 128 // width, mixed=1, middle=2, act=self.blocks, slope=self.blocks,
                     result=1, upstream=1, normed_two=1, r1=1, normed_one=1, grad=1)
        for name, size in sizes.items():
            self.spans[name] = slice(at, at + size * width)
            at += size * width
        self.state = pltpu.VMEM((micros, tokens, at), BF16)


def dot(left, right):
    return lax.dot_general(left, right, (((1,), (0,)), ((), ())), preferred_element_type=F32)


def dot_rhs_t(left, right):
    return lax.dot_general(left, right, (((1,), (1,)), ((), ())), preferred_element_type=F32)


def dot_lhs_t(left, right):
    return lax.dot_general(left, right, (((0,), (0,)), ((), ())), preferred_element_type=F32)


def in_hbm(values):
    return [pltpu.with_memory_space_constraint(value, pltpu.HBM) for value in values]


def params(mebibytes):
    return pltpu.CompilerParams(vmem_limit_bytes=mebibytes << 20)


def after(value, *others):
    return pl.pallas_call(
        lambda *refs: None,
        out_shape=jax.ShapeDtypeStruct(value.shape, value.dtype),
        in_specs=[pl.BlockSpec(memory_space=pl.ANY)] * (1 + len(others)),
        out_specs=pl.BlockSpec(memory_space=pl.ANY),
        input_output_aliases={0: 0},
        compiler_params=params(1),
        cost_estimate=STEP,
        name="after",
    )(value, *others)


def gather_kernel(places, facts, *refs):
    held, count = refs[-1], len(places)
    for own, other, (place, low, high) in zip(refs[:count], refs[count : 2 * count], places):
        for ref, half in ((own, facts[0, CORE]), (other, 1 - facts[0, CORE])):
            held[half, facts[0, ORDER + place], low:high] = ref[...]


def gather_call(facts, places, own, other, held, waits=()):
    held = () if held is None else (held,)
    width = own[0].shape[1]
    rows = 6 * width // GROUPS + SMALL_ROWS
    return pl.pallas_call(
        functools.partial(gather_kernel, places),
        out_shape=pltpu.VMEM((2, GROUPS, rows, width), BF16),
        in_specs=[SMEM] + [VMEM] * (2 * len(own) + len(held)) + [ANY] * len(waits),
        out_specs=VMEM,
        input_output_aliases={1 + 2 * len(own): 0} if held else {},
        compiler_params=params(8),
        cost_estimate=LIGHT,
        name="lay_out_weights",
    )(facts, *own, *other, *held, *waits)


def weight_block(held, width, block):
    part = width // GROUPS
    if block < 6:
        return held[0, :, block * part : (block + 1) * part, :].reshape(width, width)
    if block < 8:
        return held[1, :, (block - 6) * part : (block - 5) * part, :].reshape(width, width)
    first = (block - 8) * 2
    return held[1, first : first + 2, 2 * part : 6 * part, :].reshape(width, width)


def small_rows(held, width):
    total = held[0, 0, 6 * width // GROUPS :].astype(F32)
    for group in range(1, GROUPS):
        total = total + held[0, group, 6 * width // GROUPS :].astype(F32)
    return total


def pick_kernel(parts, facts, *refs):
    outs, sems = refs[-1 - len(parts) : -1], refs[-1]
    options = refs[: 4 * sum(parts)]
    for section in range(4):

        @pl.when(facts[0, STAGE] * 2 + facts[0, CORE] == section)
        def _():
            copies, at = [], 0
            for out, count in zip(outs, parts):
                row = 0
                for i in range(count):
                    source = options[at + 4 * i + section]
                    copies.append(
                        pltpu.make_async_copy(source, out.at[pl.ds(row, source.shape[0])], sems.at[len(copies)])
                    )
                    row += source.shape[0]
                at += 4 * count
            for copy in copies:
                copy.start()
            for copy in copies:
                copy.wait()


def pick(facts, *choices, waits=()):
    shapes = [
        pltpu.VMEM((sum(options[0].shape[0] for options in parts), parts[0][0].shape[1]), BF16) for parts in choices
    ]
    given = [option for parts in choices for options in parts for option in options]
    return pl.pallas_call(
        functools.partial(pick_kernel, tuple(len(parts) for parts in choices)),
        out_shape=tuple(shapes),
        in_specs=[SMEM] + [ANY] * (len(given) + len(waits)),
        out_specs=tuple([VMEM] * len(choices)),
        scratch_shapes=[pltpu.SemaphoreType.DMA((sum(len(parts) for parts in choices),))],
        compiler_params=params(3),
        cost_estimate=LIGHT,
        name="pick",
    )(facts, *(in_hbm(given) if waits else given), *waits)


def split_kernel(first, second, low, high, sems):
    copies = [
        pltpu.make_async_copy(first.at[pl.ds(0, low.shape[0])], low, sems.at[0]),
        pltpu.make_async_copy(second.at[pl.ds(low.shape[0], high.shape[0])], high, sems.at[1]),
    ]
    for copy in copies:
        copy.start()
    for copy in copies:
        copy.wait()


def split(first, second, cut, *waits):
    rows, width = first.shape
    return pl.pallas_call(
        lambda *refs: split_kernel(*refs[:2], *refs[2 + len(waits) :]),
        out_shape=(pltpu.VMEM((cut, width), BF16), pltpu.VMEM((rows - cut, width), BF16)),
        in_specs=[ANY] * (2 + len(waits)),
        out_specs=(VMEM, VMEM),
        scratch_shapes=[pltpu.SemaphoreType.DMA((2,))],
        compiler_params=params(3),
        cost_estimate=LIGHT,
        name="split",
    )(first, second, *waits)


def chosen(core_flag, kernel):
    is_first = jnp.max(core_flag[...]) < 0.5
    pl.when(is_first)(functools.partial(kernel, True))
    pl.when(jnp.logical_not(is_first))(functools.partial(kernel, False))


def spare_kernel(core_flag, first, second, *refs):
    def copy(is_first):
        refs[-1][...] = second[...] if is_first else first[...]

    chosen(core_flag, copy)


def spare_half(core_flag, first, second):
    return pl.pallas_call(
        spare_kernel,
        out_shape=pltpu.VMEM(first.shape, BF16),
        in_specs=[VMEM] * 3,
        out_specs=VMEM,
        compiler_params=params(2),
        cost_estimate=LIGHT,
        name="spare_half",
    )(core_flag, first, second)


def merge_kernel(core_flag, first, second, got, *refs):
    out, landed, sems = refs[-3:]
    copies = [pltpu.make_async_copy(got.at[i], landed.at[i], sems.at[i]) for i in range(got.shape[0])]
    for copy in copies:
        copy.start()

    def add(is_first):
        keep = first if is_first else second
        for i, copy in enumerate(copies):
            copy.wait()
            out[i] = keep[i] + landed[i]

    chosen(core_flag, add)


def merge(core_flag, first, second, got, waits=()):
    return pl.pallas_call(
        merge_kernel,
        out_shape=pltpu.VMEM(first.shape, BF16),
        in_specs=[VMEM] * 3 + [ANY] * (1 + len(waits)),
        out_specs=VMEM,
        scratch_shapes=[pltpu.VMEM(first.shape, BF16), pltpu.SemaphoreType.DMA((first.shape[0],))],
        compiler_params=params(6),
        cost_estimate=STEP,
        name="merge",
    )(core_flag, first, second, got, *waits)


def rows_kernel(plan, name, core_flag, first, second, *refs):
    mine, theirs = refs[-2:]
    span, run = plan.spans[name], plan.micros * plan.tokens

    def copy(is_first):
        one, two = (first, second) if is_first else (second, first)
        mine[...] = one[:, :, span].reshape(run, plan.width)
        theirs[...] = two[:, :, span].reshape(run, plan.width)

    chosen(core_flag, copy)


def layer_rows(plan, name, core_flag, states, waits):
    shape = pltpu.VMEM((plan.micros * plan.tokens, plan.width), BF16)
    return pl.pallas_call(
        functools.partial(rows_kernel, plan, name),
        out_shape=(shape, shape),
        in_specs=[VMEM] * 3 + [ANY] * len(waits),
        out_specs=(VMEM, VMEM),
        compiler_params=params(2),
        cost_estimate=STEP,
        name="layer_rows",
    )(core_flag, *states, *waits)


def ring_add_kernel(sums, cuts, n_arrived, n_waits, held, *refs):
    arrived = refs[:n_arrived]
    outs = refs[n_arrived + n_waits :]
    for (block, low, high, parts), out in zip(sums, outs):
        edges = sorted({low, high} | {cuts[p] for p in parts} | {cuts[p] + arrived[p].shape[0] for p in parts})
        for a, b in zip(edges, edges[1:]):
            total = held[block, a:b].astype(F32)
            for p in parts:
                if cuts[p] <= a and b <= cuts[p] + arrived[p].shape[0]:
                    total = total + arrived[p][a - cuts[p] : b - cuts[p]].astype(F32)
            out[a - low : b - low] = total.astype(BF16)


def ring_add(held, arrived, cuts, sums, waits=()):
    width = held.shape[2]
    return pl.pallas_call(
        functools.partial(ring_add_kernel, sums, cuts, len(arrived), len(waits)),
        out_shape=tuple(pltpu.VMEM((high - low, width), BF16) for _, low, high, _ in sums),
        in_specs=[VMEM] * (1 + len(arrived)) + [ANY] * len(waits),
        out_specs=tuple([VMEM] * len(sums)),
        compiler_params=params(5),
        cost_estimate=STEP,
        name="ring_add",
    )(held, *arrived, *waits)


def normalise(values):
    center = values - jnp.mean(values, axis=-1, keepdims=True)
    spread = jnp.mean(center * center, axis=-1, keepdims=True)
    scale = lax.rsqrt(spread + 1e-05)
    return center * scale, scale


def norm_back(grad, gain, unit, scale):
    grad_unit = grad * gain
    mean_grad = jnp.mean(grad_unit, axis=-1, keepdims=True)
    mean_dot = jnp.mean(grad_unit * unit, axis=-1, keepdims=True)
    return scale * (grad_unit - mean_grad - unit * mean_dot)


def stack_heads(pair, low_lanes):
    zero = jnp.zeros_like(pair)
    return jnp.concatenate([jnp.where(low_lanes, pair, zero), jnp.where(low_lanes, zero, pair)], axis=0)


def load_source(slot, kind, refs, target, sem):
    if kind == "each":
        for micro, ref in enumerate(refs):

            @pl.when(slot == micro)
            def _():
                pltpu.make_async_copy(ref, target, sem).start()

    else:
        pltpu.make_async_copy(refs[0].at[slot] if kind == "slot" else refs[0], target, sem).start()


def for_slots(flag, micros, micro, work):
    @pl.when(jnp.max(flag[...]) > 0.5)
    def _():
        if micro is None:
            pl.loop(0, micros)(work)
        else:
            work(micro)


def forward_kernel(plan, micro, kind, count, has_state, n_waits, flag, *refs):
    sources, whole = refs[:count], micro is None
    bias_v, held = refs[count : count + 2]
    state, low_o, sem = refs[count + 2 + int(has_state) + n_waits :]
    tokens, width = plan.tokens, plan.width
    weight = lambda block: weight_block(held, width, block)

    def work(slot):
        value_of = lambda name: state.at[slot, :, plan.spans[name]]
        low_v = low_o.at[slot] if whole else low_o
        hidden_v, q_v, k_v, v_v, probs_v, mixed_v, middle_v, act_v, slope_v = (
            value_of(name) for name in ("hidden", "q", "k", "v", "probs", "mixed", "middle", "act", "slope")
        )
        load_source(slot, kind, sources, hidden_v, sem)
        small = small_rows(held, width)
        gain_one, shift_one, gain_two, shift_two, down_bias = (small[i : i + 1] for i in range(5))
        pltpu.make_async_copy(hidden_v, hidden_v, sem).wait()
        hidden = hidden_v[...].astype(F32)
        unit, _ = normalise(hidden)
        normed = (unit * gain_one + shift_one).astype(BF16)
        q_v[...] = (dot(normed, weight(0)) * HEAD_DIM**-0.5).astype(BF16)
        k_v[...] = dot(normed, weight(1)).astype(BF16)
        v_v[...] = dot(normed, weight(6)).astype(BF16)
        low_lanes = lax.broadcasted_iota(jnp.int32, (128, 128), 1) < HEAD_DIM
        for group in range(tokens // 128):
            rows = slice(group * 128, group * 128 + 128)
            bias = bias_v[slot, rows]
            bias = jnp.concatenate([bias, bias], axis=0)
            for pair in range(width // 128):
                lanes = slice(pair * 128, pair * 128 + 128)
                query = stack_heads(q_v[rows, lanes], low_lanes)
                scores = dot_rhs_t(query, k_v[rows, lanes]) + bias
                raised = jnp.exp(scores - jnp.max(scores, axis=-1, keepdims=True))
                probs = (raised * (1.0 / jnp.sum(raised, axis=-1, keepdims=True))).astype(BF16)
                probs_v[rows, pair * 256 : pair * 256 + 128] = probs[:128]
                probs_v[rows, pair * 256 + 128 : pair * 256 + 256] = probs[128:]
                mixed = dot(probs, v_v[rows, lanes])
                mixed_v[rows, lanes] = jnp.where(low_lanes, mixed[:128], mixed[128:]).astype(BF16)
        middle = hidden + dot(mixed_v[...], weight(7))
        high = middle.astype(BF16)
        middle_v[:, :width] = high
        middle_v[:, width:] = (middle - high.astype(F32)).astype(BF16)
        unit, _ = normalise(middle)
        normed = (unit * gain_two + shift_two).astype(BF16)
        total = middle + down_bias
        for block in range(plan.blocks):
            lanes = slice(block * width, (block + 1) * width)
            before = dot(normed, weight(2 + block)) + small[5 + block : 6 + block]
            square = before * before
            tanh = jnp.tanh(before * (0.7978845608028654 + 0.035677408136300125 * square))
            half = 0.5 * tanh + 0.5
            act = (before * half).astype(BF16)
            act_v[:, lanes] = act
            slope = half + before * (0.5 - 0.5 * (tanh * tanh)) * (0.7978845608028654 + 0.10703222440890037 * square)
            slope_v[:, lanes] = slope.astype(BF16)
            total = total + dot(act, weight(8 + block))
        low = total.astype(BF16)
        low_v[...] = low
        value_of("result")[...] = low

    for_slots(flag, plan.micros, micro, work)


def forward_call(plan, flag, micro, source, bias, held, state, waits=(), cost=LIGHT):
    kind, *given = source
    state = [] if state is None else [state]
    tokens, width = plan.tokens, plan.width
    low = ((plan.micros,) if micro is None else ()) + (tokens, width)
    return pl.pallas_call(
        functools.partial(forward_kernel, plan, micro, kind, len(given), bool(state), len(waits)),
        out_shape=(plan.state, pltpu.VMEM(low, BF16)),
        in_specs=[VMEM] + [ANY] * len(given) + [VMEM] * (2 + len(state)) + [ANY] * len(waits),
        out_specs=(VMEM, VMEM),
        input_output_aliases={3 + len(given): 0} if state else {},
        scratch_shapes=[pltpu.SemaphoreType.DMA],
        compiler_params=params(8),
        cost_estimate=cost,
        name="layer_forward",
    )(flag, *given, bias, held, *state, *waits)


def backward_kernel(plan, micro, kind, count, has_sums, n_waits, flag, *refs):
    sources, whole = refs[:count], micro is None
    held = refs[count]
    state, sums_o, low_o, grad_v, do_v, sem = refs[count + 2 + int(has_sums) + n_waits :]
    tokens, width = plan.tokens, plan.width
    weight = lambda block: weight_block(held, width, block)

    def work(slot):
        value_of = lambda name: state.at[slot, :, plan.spans[name]]
        low_v = low_o.at[slot] if whole else low_o
        upstream_v, hidden_v, q_v, k_v, v_v, probs_v, middle_v, du_v = (
            value_of(name) for name in ("upstream", "hidden", "q", "k", "v", "probs", "middle", "slope")
        )
        load_source(slot, kind, sources, upstream_v, sem)
        small = small_rows(held, width)
        gain_one, shift_one, gain_two, shift_two = (small[i : i + 1] for i in range(4))
        sums_v = sums_o.at[slot]
        sums_v[...] = jnp.zeros(sums_v.shape, F32)
        pltpu.make_async_copy(upstream_v, upstream_v, sem).wait()
        upstream_low = upstream_v[...]
        upstream = upstream_low.astype(F32)
        sums_v[4:5] = jnp.sum(upstream, axis=0, keepdims=True)
        da = jnp.zeros((tokens, width), F32)
        for block in range(plan.blocks):
            lanes = slice(block * width, (block + 1) * width)
            dz = dot_rhs_t(upstream_low, weight(8 + block))
            du = (dz * du_v[:, lanes].astype(F32)).astype(BF16)
            du_v[:, lanes] = du
            sums_v[5 + block : 6 + block] = jnp.sum(du.astype(F32), axis=0, keepdims=True)
            da = da + dot_rhs_t(du, weight(2 + block))
        unit, scale = normalise(middle_v[:, :width].astype(F32) + middle_v[:, width:].astype(F32))
        value_of("normed_two")[...] = (unit * gain_two + shift_two).astype(BF16)
        sums_v[2:3] = jnp.sum(da * unit, axis=0, keepdims=True)
        sums_v[3:4] = jnp.sum(da, axis=0, keepdims=True)
        grad_middle = upstream + norm_back(da, gain_two, unit, scale)
        grad_v[...] = grad_middle
        r1 = grad_middle.astype(BF16)
        value_of("r1")[...] = r1
        do_v[...] = dot_rhs_t(r1, weight(7)).astype(BF16)
        low_lanes = lax.broadcasted_iota(jnp.int32, (128, 128), 1) < HEAD_DIM
        for group in range(tokens // 128):
            rows = slice(group * 128, group * 128 + 128)
            for pair in range(width // 128):
                lanes = slice(pair * 128, pair * 128 + 128)
                query = stack_heads(q_v[rows, lanes], low_lanes)
                key = k_v[rows, lanes]
                grad_mixed = stack_heads(do_v[rows, lanes], low_lanes)
                probs = jnp.concatenate(
                    [probs_v[rows, pair * 256 : pair * 256 + 128], probs_v[rows, pair * 256 + 128 : pair * 256 + 256]], axis=0
                )
                grad_probs = dot_rhs_t(grad_mixed, v_v[rows, lanes])
                v_v[rows, lanes] = dot_lhs_t(probs, grad_mixed).astype(BF16)
                probs = probs.astype(F32)
                weighted = grad_probs * probs
                grad_scores = (weighted - probs * jnp.sum(weighted, axis=-1, keepdims=True)).astype(BF16)
                dq = dot(grad_scores, key) * HEAD_DIM**-0.5
                q_v[rows, lanes] = jnp.where(low_lanes, dq[:128], dq[128:]).astype(BF16)
                k_v[rows, lanes] = dot_lhs_t(grad_scores, query).astype(BF16)
        unit, scale = normalise(hidden_v[...].astype(F32))
        value_of("normed_one")[...] = (unit * gain_one + shift_one).astype(BF16)
        da = dot_rhs_t(q_v[...], weight(0)) + dot_rhs_t(k_v[...], weight(1)) + dot_rhs_t(v_v[...], weight(6))
        sums_v[0:1] = jnp.sum(da * unit, axis=0, keepdims=True)
        sums_v[1:2] = jnp.sum(da, axis=0, keepdims=True)
        low = (grad_v[...] + norm_back(da, gain_one, unit, scale)).astype(BF16)
        low_v[...] = low
        value_of("grad")[...] = low

    for_slots(flag, plan.micros, micro, work)


def backward_call(plan, flag, micro, source, held, state, sums, waits=()):
    kind, *given = source
    tokens, width = plan.tokens, plan.width
    sums = [] if sums is None else [sums]
    low = ((plan.micros,) if micro is None else ()) + (tokens, width)
    return pl.pallas_call(
        functools.partial(backward_kernel, plan, micro, kind, len(given), bool(sums), len(waits)),
        out_shape=(
            plan.state,
            pltpu.VMEM((plan.micros, SMALL_ROWS, width), F32),
            pltpu.VMEM(low, BF16),
        ),
        in_specs=[VMEM] + [ANY] * len(given) + [VMEM] * (2 + len(sums)) + [ANY] * len(waits),
        out_specs=(VMEM, VMEM, VMEM),
        input_output_aliases={2 + len(given) + i: i for i in range(1 + len(sums))},
        scratch_shapes=[pltpu.VMEM((tokens, width), F32), pltpu.VMEM((tokens, width), BF16), pltpu.SemaphoreType.DMA],
        compiler_params=params(8),
        cost_estimate=LIGHT,
        name="layer_backward",
    )(flag, *given, held, state, *sums, *waits)


def weight_kernel(plan, facts, sums, state, *refs):
    halves = refs[-2:]
    width, run = plan.width, plan.micros * plan.tokens
    part = width // GROUPS

    def value_of(name, block=0):
        at = plan.spans[name].start + block * width
        return state[:, :, at : at + width].reshape(run, width)

    def put(half, grad, groups, row, rows):
        grad = grad.astype(BF16)
        for index, group in enumerate(groups):
            source = grad[index * rows : (index + 1) * rows] if grad.shape[0] > rows else grad
            halves[half][facts[0, SPOT + group], row : row + rows] = source

    everyone = range(GROUPS)
    small = sums[0]
    for micro in range(1, plan.micros):
        small = small + sums[micro]
    for half in range(2):
        put(half, small, everyone, 6 * part, SMALL_ROWS)
    left = value_of("normed_one").T
    put(0, dot(left, value_of("q")), everyone, 0, part)
    put(0, dot(left, value_of("k")), everyone, part, part)
    put(1, dot(left, value_of("v")), everyone, 0, part)
    put(1, dot(value_of("mixed").T, value_of("r1")), everyone, part, part)
    left = value_of("normed_two").T
    for block in range(plan.blocks):
        put(0, dot(left, value_of("slope", block)), everyone, (2 + block) * part, part)
    right = value_of("upstream")
    of_block = GROUPS // plan.blocks
    for block in range(plan.blocks):
        groups = range(block * of_block, (block + 1) * of_block)
        put(1, dot(value_of("act", block).T, right), groups, 2 * part, 4 * part)


def weight_call(plan, facts, state, sums, waits=()):
    width = plan.width
    shape = (GROUPS, 6 * width // GROUPS + SMALL_ROWS, width)
    run = plan.micros * plan.tokens
    return pl.pallas_call(
        functools.partial(weight_kernel, plan),
        out_shape=(pltpu.VMEM(shape, BF16), pltpu.VMEM(shape, BF16)),
        in_specs=[SMEM, VMEM, VMEM] + [ANY] * len(waits),
        out_specs=(VMEM, VMEM),
        compiler_params=params(8),
        cost_estimate=LIGHT,
        name="weight_grads",
    )(facts, sums, state, *waits)


def halves_kernel(facts, *refs):
    inputs, outs, landed, (whole, sems) = refs[:10], refs[10:16], refs[16:26], refs[26:]
    copies = [pltpu.make_async_copy(source, target, sems.at[i]) for i, (source, target) in enumerate(zip(inputs, landed))]
    for copy in copies:
        copy.start()
    w_qkv, w_out, w_up, w_down, *vectors = landed
    part, width = w_out.shape[1:]
    for copy in copies[4:]:
        copy.wait()
    lane = lax.broadcasted_iota(jnp.int32, (1, width), 1)
    rows = []
    for vector in vectors:
        size = vector.shape[1]
        spread = jnp.concatenate([vector[...]] * (width // size), axis=1)
        for row in range(size * GROUPS // width):
            rows.append(jnp.where((lane + row * width) // size == facts[0, PLACE], spread, 0.0))
    rows.append(jnp.zeros((SMALL_ROWS - len(rows), width), F32))
    small = jnp.concatenate(rows, axis=0).astype(BF16)
    first, second = whole.at[0], whole.at[1]
    first[6 * part :] = small
    second[6 * part :] = small
    copies[0].wait()
    for i in range(2):
        first[i * part : (i + 1) * part] = w_qkv[0, :, i * width : (i + 1) * width].astype(BF16)
    second[:part] = w_qkv[0, :, 2 * width :].astype(BF16)
    copies[1].wait()
    second[part : 2 * part] = w_out[0].astype(BF16)
    copies[2].wait()
    for i in range(w_up.shape[2] // width):
        first[(2 + i) * part : (3 + i) * part] = w_up[0, :, i * width : (i + 1) * width].astype(BF16)
    copies[3].wait()
    second[2 * part : 6 * part] = w_down[0].astype(BF16)
    cut = outs[0].shape[0]
    for i, rows in enumerate((slice(0, cut), slice(cut, None))):
        outs[i][...] = first[rows]
        outs[2 + i][...] = second[rows]
        outs[4 + i][...] = whole[1 - facts[0, CORE], rows]


def halves_call(facts, matrices, vectors, cut):
    _, part, width = matrices[1].shape
    rows = 6 * part + SMALL_ROWS
    shapes = [pltpu.VMEM((size, width), BF16) for size in (cut, rows - cut)]
    inputs = (*matrices, *vectors)
    outs = pl.pallas_call(
        halves_kernel,
        out_shape=(*shapes, *shapes, *shapes),
        in_specs=[SMEM] + [ANY] * len(inputs),
        out_specs=tuple([VMEM] * 6),
        scratch_shapes=[pltpu.VMEM(value.shape, F32) for value in inputs]
        + [pltpu.VMEM((2, rows, width), BF16), pltpu.SemaphoreType.DMA((len(inputs),))],
        compiler_params=params(8),
        cost_estimate=LIGHT,
        name="round_shard",
    )(facts, *in_hbm(inputs))
    return outs[:2], outs[2:4], outs[4:]


def assemble_kernel(facts, mine, theirs, *refs):
    out, token, landed, wide, sems = refs[-5:]
    token[...] = jnp.zeros_like(token)
    copies = [pltpu.make_async_copy(source, landed.at[i], sems.at[i]) for i, source in enumerate((mine, theirs))]
    for copy in copies:
        copy.start()
    saves = []
    for i, copy in enumerate(copies):
        copy.wait()
        wide[i] = landed[i].astype(F32)
        half = facts[0, CORE] if i == 0 else 1 - facts[0, CORE]
        saves.append(pltpu.make_async_copy(wide.at[i], out.at[half], sems.at[2 + i]))
        saves[-1].start()
    for copy in saves:
        copy.wait()


def assemble(facts, mine, theirs, waits):
    rows, width = mine.shape
    return pl.pallas_call(
        assemble_kernel,
        out_shape=(pltpu.HBM((2, rows, width), F32), pltpu.VMEM((8, 128), F32)),
        in_specs=[SMEM] + [ANY] * (2 + len(waits)),
        out_specs=(ANY, VMEM),
        scratch_shapes=[
            pltpu.VMEM((2, rows, width), BF16),
            pltpu.VMEM((2, rows, width), F32),
            pltpu.SemaphoreType.DMA((4,)),
        ],
        compiler_params=params(6),
        cost_estimate=STEP,
        name="assemble",
    )(facts, mine, theirs, *waits)


def unpack_kernel(counts, facts, *refs):
    total = 4 * sum(counts)
    options, outs, (landed, sems) = refs[:total], refs[total : total + 10], refs[total + 10 :]
    grad_qkv, grad_out, grad_up, grad_down, *vectors = outs
    for section in range(4):

        @pl.when(facts[0, STAGE] * 2 + facts[0, CORE] == section)
        def _():
            for half, count in enumerate(counts):
                row = 0
                for i in range(count):
                    source = options[4 * (sum(counts[:half]) + i) + section]
                    target = landed.at[half, pl.ds(row, source.shape[0])]
                    pltpu.make_async_copy(source, target, sems.at[half]).start()
                    row += source.shape[0]

    for half in range(2):
        pltpu.make_async_copy(landed.at[half], landed.at[half], sems.at[half]).wait()
    part, width = grad_out.shape[1:]
    block = lambda half, first, count=1: landed[half, first * part : (first + count) * part].astype(F32)
    grad_qkv[0, :, :width] = block(0, 0)
    grad_qkv[0, :, width : 2 * width] = block(0, 1)
    grad_qkv[0, :, 2 * width :] = block(1, 0)
    grad_out[0] = block(1, 1)
    for i in range(grad_up.shape[2] // width):
        grad_up[0, :, i * width : (i + 1) * width] = block(0, 2 + i)
    grad_down[0] = block(1, 2, 4)
    small = landed[0, 6 * part :].astype(F32)
    for place in range(GROUPS):

        @pl.when(facts[0, PLACE] == place)
        def _():
            row = 0
            for vector in vectors:
                size = vector.shape[1]
                first = row * width + place * size
                lanes = first % width
                vector[...] = small[first // width : first // width + 1, lanes : lanes + size]
                row += size * GROUPS // width


def unpack(facts, first, second, shapes):
    given = [option for parts in (first, second) for options in parts for option in options]
    rows = sum(options[0].shape[0] for options in first)
    return pl.pallas_call(
        functools.partial(unpack_kernel, (len(first), len(second))),
        out_shape=tuple(jax.ShapeDtypeStruct(shape, F32) for shape in shapes),
        in_specs=[SMEM] + [ANY] * len(given),
        out_specs=tuple([VMEM] * len(shapes)),
        scratch_shapes=[pltpu.VMEM((2, rows, first[0][0].shape[1]), BF16), pltpu.SemaphoreType.DMA((2,))],
        compiler_params=params(8),
        cost_estimate=LIGHT,
        name="unpack",
    )(facts, *given)


CYCLE = (0, 2, 4, 6, 7, 5, 3, 1)
OFFSETS = (0, -1, 1, -2, 2, -3, 3, 4)


def send(value, pairs):
    return lax.ppermute(value, "section", pairs)


def to_core(value):
    return send(value, [(i, i ^ 1) for i in range(4)])


def onward(value):
    return send(value, [(0, 2), (1, 3)])


def backward(value):
    return send(value, [(2, 0), (3, 1)])


def along(value, by):
    size = len(CYCLE)
    return lax.ppermute(value, "dp", [(CYCLE[i], CYCLE[(i + by) % size]) for i in range(size)])


class Ring:
    def __init__(self, piece, low, high, cut):
        self.low, self.high, self.cut = low, high, cut
        self.arrived, self.places = [piece], [(0, low, high)]

    def level(self, *waits):
        if len(self.arrived) > 1:
            ahead, behind = self.arrived[-2:]
            ahead = after(ahead, behind, *waits)
            self.arrived[-2:] = [ahead, after(behind, ahead)]
        return (self.arrived * 2)[-2:]

    def step(self, *waits):
        ahead, behind = self.level(*waits)
        self.arrived += along(ahead, 1), along(behind, -1)
        self.places += [(len(self.places) + i, self.low, self.high) for i in range(2)]

    def last_step(self, *waits):
        ahead, behind = self.level(*waits)
        if self.cut == self.high:
            self.arrived.append(along(ahead, 1))
            self.places.append((7, self.low, self.high))
        else:
            self.arrived.append(along(behind, -1))
            self.places.append((7, self.low, self.high))


def advance(rings):
    ahead = ()
    for ring in rings:
        before = ring.arrived[-2:]
        ring.step(*ahead)
        ahead = (*ahead, *before)


class Gather:
    def __init__(self, facts, rings):
        self.facts, self.rings, self.done, self.held = facts, rings, 0, None

    def lay_out(self, count, *waits):
        span = slice(self.done, count)
        pieces = [piece for ring in self.rings for piece in ring.arrived[span]]
        places = tuple(place for ring in self.rings for place in ring.places[span])
        self.done = count
        self.held = gather_call(self.facts, places, pieces, [to_core(piece) for piece in pieces], self.held, waits)
        return self.held


class Scatter:
    def __init__(self, held, low, high, cut):
        self.held, self.low, self.high, self.cut = held, low, high, cut
        self.next, self.arrived = 4, {}

    def step(self, *waits):
        low, high, cut, step, at = self.low, self.high, self.cut, self.next, OFFSETS.index
        if step == 4:
            ways = [(way, at(4), a, b) for way, a, b in ((1, low, cut), (-1, cut, high)) if a < b]
        elif step:
            ways = [(1, at(step), low, high), (-1, at(-step), low, high)]
        else:
            ways = [(0, at(0), low, high)]
        arrived = list(self.arrived.items())
        parts_of = lambda way: tuple(i for i, (came, _) in enumerate(arrived) if not way or came == way)
        sums = tuple((place, a, b, parts_of(way)) for way, place, a, b in ways)
        cuts = tuple(cut if step == 3 and way == -1 else low for way, _ in arrived)
        parts = ring_add(self.held, [part for _, part in arrived], cuts, sums, waits)
        self.next -= 1
        if step:
            self.arrived = {way: along(part, way) for (way, _, _, _), part in zip(ways, parts)}
        else:
            self.total = parts[0]
        return parts[0]


def facts_table(dp_count):
    ring = dp_count == len(CYCLE)
    table = np.zeros((4, dp_count, 1, FACTS), np.int32)
    for section in range(4):
        for place in range(dp_count):
            facts = table[section, place, 0]
            facts[[CORE, STAGE, PLACE]] = section % 2, section // 2, place
            for i, offset in enumerate(OFFSETS):
                owner = CYCLE[(CYCLE.index(place) + offset) % dp_count] if ring else i
                facts[ORDER + i], facts[SPOT + owner] = owner, i
    return table


def on_device(
    frames_in,
    segment_ids,
    cotangent,
    w_qkv,
    w_out,
    w_up,
    w_down,
    norm1_gain,
    norm1_shift,
    norm2_gain,
    norm2_shift,
    up_bias,
    down_bias,
):
    section = lax.axis_index("section")
    dp_index, dp_count = lax.axis_index("dp"), lax.axis_size("dp")
    rows, frame_count, width = frames_in.shape
    hidden_units = w_up.shape[2]
    own_rows = rows // 2
    tokens = own_rows * frame_count // MICRO
    ring = dp_count == len(CYCLE)
    part = w_qkv.shape[1]
    cut = 3 * width // GROUPS
    plan = Plan(MICRO, tokens, width, hidden_units)

    table = jnp.asarray(facts_table(dp_count))
    facts = lax.dynamic_slice(table, (section, dp_index, 0, 0), (1, 1) + table.shape[2:])[0, 0]

    segments = lax.dynamic_slice_in_dim(segment_ids, section % 2 * own_rows, own_rows, 0).reshape(-1, 128)
    spot = jnp.arange(128, dtype=jnp.int32)
    allowed = (spot[None, :] <= spot[:, None]) & (spot[None, :] // frame_count == spot[:, None] // frame_count)
    allowed = allowed[None] & (segments[:, :, None] == segments[:, None, :])
    bias = jnp.where(allowed, 0.0, -1e30).astype(F32).reshape(MICRO, tokens, 128)
    frames, last_grads = (
        lax.dynamic_slice_in_dim(value, section % 2 * own_rows, own_rows, 0).reshape(MICRO, tokens, width)
        for value in (frames_in, cotangent)
    )
    flags = [jnp.full((8, 128), flag, F32) for flag in (section < 2, section >= 2, section % 2 == 1)]

    matrices = (w_qkv, w_out, w_up, w_down)
    vectors = (norm1_gain, norm1_shift, norm2_gain, norm2_shift, down_bias, up_bias)
    if ring:
        height = 2 * cut + SMALL_ROWS
        one, two, spare = halves_call(facts, matrices, vectors, cut)
        near = [to_core(part_of) for part_of in spare]
        first_parts = [pick(facts, [(one[i], near[i]) * 2])[0] for i in range(2)]
        spans = ((0, cut), (cut, height))
        rings = [Ring(piece, *span, cut) for piece, span in zip(first_parts, spans)]
        second_parts = [pick(facts, [(near[i], two[i]) * 2])[0] for i in range(2)]
        besides = (frames, last_grads, bias, *flags, *second_parts)
        for step in range(3):
            for each in rings:
                each.step(*(besides if step == 1 else ()))
        for each in rings:
            each.last_step()
        last = [each.arrived[-1] for each in rings]
        second_rings = [Ring(after(piece, *last), *span, cut) for piece, span in zip(second_parts, spans)]
        for each in second_rings:
            each.step()
        advance(second_rings)
        for each in second_rings:
            each.step()
        gather = Gather(facts, rings)
        gather.lay_out(5)
        token = gather.lay_out(8)
        held = [gather.held]
    else:
        token = facts
        blocks = [w_qkv[0, :, :width], w_qkv[0, :, width : 2 * width]]
        blocks += [w_up[0, :, i * width : (i + 1) * width] for i in range(hidden_units // width)]
        blocks += [w_qkv[0, :, 2 * width :], w_out[0], w_down[0]]
        whole = jnp.concatenate([lax.all_gather(block.astype(BF16), "dp", axis=0, tiled=True) for block in blocks])
        flat = [lax.all_gather(vector[0].astype(BF16), "dp", axis=0, tiled=True) for vector in vectors]
        small = jnp.concatenate(flat + [jnp.zeros(((SMALL_ROWS - 5) * width - hidden_units,), BF16)])
        grouped = lambda low, count: jnp.swapaxes(
            whole[low * width : (low + count) * width].reshape(count, GROUPS, -1, width), 0, 1
        ).reshape(GROUPS, -1, width)
        small = jnp.pad(small.reshape(1, SMALL_ROWS, width), ((0, GROUPS - 1), (0, 0), (0, 0)))
        down = whole[8 * width :].reshape(GROUPS, -1, width)
        value = jnp.stack(
            [jnp.concatenate([grouped(0, 6), small], 1), jnp.concatenate([grouped(6, 2), down, small], 1)]
        )
        got = lax.all_gather(value, "section")
        held = [jnp.where(section < 2, got[i], got[i + 2]) for i in (0, 1)]

    states, sums = [None, None], [None, None]

    def whole_rows(name, token):
        mine, theirs = layer_rows(plan, name, flags[2], states, (token,))
        whole, token = assemble(facts, mine, to_core(theirs), (mine,))
        return whole.reshape(1, rows, frame_count, width), token


    def run_forward(layer, stage, micro, source, token, cost=LIGHT):
        states[layer], low = forward_call(
            plan, flags[stage], micro, source, bias, held[layer], states[layer], (token,), cost
        )
        return low

    def run_backward(layer, stage, micro, source, token):
        states[layer], sums[layer], low = backward_call(
            plan, flags[stage], micro, source, held[layer], states[layer], sums[layer], (token,)
        )
        return low

    token = stage_zero_low = run_forward(0, 0, None, ("slot", frames), token, HEAVY)
    if ring:
        for each in second_rings:
            each.last_step(token)
        gather = Gather(facts, second_rings)
        gather.lay_out(5, token)
        token = gather.lay_out(8)
        held.append(gather.held)
    hops = []
    for micro in range(MICRO):
        token = run_forward(1, 0, micro, ("slot", stage_zero_low), token)
        hops.append(onward(token))
    lows = []
    for micro in range(MICRO):
        token = run_forward(0, 1, micro, ("one", hops[micro]), token)
        lows.append(token)
    token = run_forward(1, 1, None, ("each", *lows), token)
    token = stage_one_back = run_backward(1, 1, None, ("slot", last_grads), token)
    hops = []
    for micro in range(MICRO):
        token = run_backward(0, 1, micro, ("slot", stage_one_back), token)
        hops.append(backward(token))
    lows = []
    for micro in range(MICRO):
        token = run_backward(1, 0, micro, ("one", hops[micro]), token)
        lows.append(token)

    halves = weight_call(plan, facts, states[1], sums[1], (token,))
    totals = [halves]
    if ring:
        give = spare_half(flags[2], *halves)
        got = to_core(give)
        token = run_backward(0, 0, 0, ("one", lows[0]), give)
        token = merge(flags[2], *halves, got, (token,))
        second = [Scatter(token, *span, cut) for span in spans]
        for each in second:
            token = each.step(token)
        for micro in range(1, MICRO):
            token = run_backward(0, 0, micro, ("one", lows[micro]), token)
        for each in second:
            token = each.step(token)
        halves = weight_call(plan, facts, states[0], sums[0], (token,))
        token = halves[0]
        for each in second:
            token = each.step(token)
        give = spare_half(flags[2], *halves)
        got = to_core(after(give, token))
        for each in second:
            token = each.step(token)
        token = merge(flags[2], *halves, got, (token,))
        first = [Scatter(token, *span, cut) for span in spans]
        for each in first + second:
            token = each.step(token)
        input_grads, token = whole_rows("grad", token)
        for each in first:
            token = each.step(token)
        outputs, token = whole_rows("result", token)
        for each in first + first + first:
            token = each.step(token)
        mine = [(one.total, two.total) for one, two in zip(first, second)]
        is_first = section % 2 == 0
        theirs = [to_core(jnp.where(is_first, two, one)) for one, two in mine]
        grads = unpack(
            facts,
            [(one, other) * 2 for (one, _), other in zip(mine, theirs)],
            [(other, two) * 2 for (_, two), other in zip(mine, theirs)],
            [value.shape for value in matrices + vectors],
        )
        return (outputs, input_grads, *grads[:8], grads[9], grads[8])
    else:
        run_backward(0, 0, None, ("each", *lows), halves[0])
        totals.append(weight_call(plan, facts, states[0], sums[0]))
        (late_one, late_two), (early_one, early_two) = totals
        is_first = section % 2 == 0

        def to_layer(first, second):
            first, second = first.astype(F32), second.astype(F32)
            return jnp.where(is_first, first, second) + to_core(jnp.where(is_first, second, first))

        one, two = to_layer(early_one, late_one), to_layer(early_two, late_two)
        small = lax.psum(one[0, 6 * width // GROUPS :], "dp")
        block = width // GROUPS
        natural = lambda half, low, high: lax.psum_scatter(
            half[:, low * block : high * block].reshape(-1, width), "dp", scatter_dimension=0, tiled=True
        )
        first_grads = [natural(one, i, i + 1) for i in range(6)]
        second_grads = [natural(two, 0, 1), natural(two, 1, 2), natural(two, 2, 6)]
    grad_vectors = [lax.dynamic_slice_in_dim(small[i : i + 1].reshape(-1), dp_index * part, part) for i in range(5)]
    grad_vectors.append(
        lax.dynamic_slice_in_dim(small[5 : 5 + hidden_units // width].reshape(-1), dp_index * 4 * part, 4 * part)
    )
    grad_vectors = [vector[None].astype(F32) for vector in grad_vectors]

    outputs, input_grads = whole_rows("result", small)[0], whole_rows("grad", small)[0]
    return (
        outputs,
        input_grads,
        jnp.concatenate([first_grads[0], first_grads[1], second_grads[0]], axis=1)[None].astype(F32),
        second_grads[1][None].astype(F32),
        jnp.concatenate(first_grads[2:], axis=1)[None].astype(F32),
        second_grads[2][None].astype(F32),
        *grad_vectors[:4],
        grad_vectors[5],
        grad_vectors[4],
    )


def solution(mesh):
    rows = P("dp", None, None)
    matrix, vector = P("section", "dp", None), P("section", "dp")
    result = P("section", "dp", None, None)
    return jax.shard_map(
        on_device,
        mesh=mesh,
        in_specs=(rows, P("dp", None), rows) + (matrix,) * 4 + (vector,) * 6,
        out_specs=(result, result) + (matrix,) * 4 + (vector,) * 6,
        check_vma=False,
    )
```

```python
import functools

import jax
import jax.numpy as jnp
import numpy as np
from jax import lax
from jax.experimental import pallas as pl
from jax.experimental.pallas import tpu as pltpu
from jax.sharding import PartitionSpec as P

HEADS = 8
HEAD_DIM = 64
GROUPS = 8
SMALL_ROWS = 16
MICRO = 2
BF16 = jnp.bfloat16
F32 = jnp.float32
ANY = pl.BlockSpec(memory_space=pl.ANY)
SMEM = pl.BlockSpec(memory_space=pltpu.SMEM)
VMEM = pl.BlockSpec(memory_space=pltpu.VMEM)
LIGHT = pl.CostEstimate(flops=1, bytes_accessed=1, transcendentals=0)
STEP = pl.CostEstimate(flops=3 * 10**8, bytes_accessed=1, transcendentals=0)
HEAVY = pl.CostEstimate(flops=10**10, bytes_accessed=1, transcendentals=0)
CORE, STAGE, PLACE, ORDER, SPOT = 0, 1, 2, 4, 12
FACTS = 20


class Plan:
    def __init__(self, micros, tokens, width, hidden_units):
        self.micros, self.tokens, self.width, self.hidden_units = micros, tokens, width, hidden_units
        self.blocks = hidden_units // width
        self.spans, at = {}, 0
        sizes = dict(hidden=1, q=1, k=1, v=1, probs=HEADS * 128 // width, mixed=1, middle=2, act=self.blocks, slope=self.blocks,
                     result=1, upstream=1, normed_two=1, r1=1, normed_one=1, grad=1)
        for name, size in sizes.items():
            self.spans[name] = slice(at, at + size * width)
            at += size * width
        self.state = pltpu.VMEM((micros, tokens, at), BF16)


def dot(left, right):
    return lax.dot_general(left, right, (((1,), (0,)), ((), ())), preferred_element_type=F32)


def dot_rhs_t(left, right):
    return lax.dot_general(left, right, (((1,), (1,)), ((), ())), preferred_element_type=F32)


def dot_lhs_t(left, right):
    return lax.dot_general(left, right, (((0,), (0,)), ((), ())), preferred_element_type=F32)


def in_hbm(values):
    return [pltpu.with_memory_space_constraint(value, pltpu.HBM) for value in values]


def params(mebibytes):
    return pltpu.CompilerParams(vmem_limit_bytes=mebibytes << 20)


def after(value, *others):
    return pl.pallas_call(
        lambda *refs: None,
        out_shape=jax.ShapeDtypeStruct(value.shape, value.dtype),
        in_specs=[pl.BlockSpec(memory_space=pl.ANY)] * (1 + len(others)),
        out_specs=pl.BlockSpec(memory_space=pl.ANY),
        input_output_aliases={0: 0},
        compiler_params=params(1),
        cost_estimate=STEP,
        name="after",
    )(value, *others)


def gather_kernel(places, facts, *refs):
    held, count = refs[-1], len(places)
    for own, other, (place, low, high) in zip(refs[:count], refs[count : 2 * count], places):
        for ref, half in ((own, facts[0, CORE]), (other, 1 - facts[0, CORE])):
            held[half, facts[0, ORDER + place], low:high] = ref[...]


def gather_call(facts, places, own, other, held, waits=()):
    held = () if held is None else (held,)
    width = own[0].shape[1]
    rows = 6 * width // GROUPS + SMALL_ROWS
    return pl.pallas_call(
        functools.partial(gather_kernel, places),
        out_shape=pltpu.VMEM((2, GROUPS, rows, width), BF16),
        in_specs=[SMEM] + [VMEM] * (2 * len(own) + len(held)) + [ANY] * len(waits),
        out_specs=VMEM,
        input_output_aliases={1 + 2 * len(own): 0} if held else {},
        compiler_params=params(8),
        cost_estimate=LIGHT,
        name="lay_out_weights",
    )(facts, *own, *other, *held, *waits)


def weight_block(held, width, block):
    part = width // GROUPS
    if block < 6:
        return held[0, :, block * part : (block + 1) * part, :].reshape(width, width)
    if block < 8:
        return held[1, :, (block - 6) * part : (block - 5) * part, :].reshape(width, width)
    first = (block - 8) * 2
    return held[1, first : first + 2, 2 * part : 6 * part, :].reshape(width, width)


def small_rows(held, width):
    total = held[0, 0, 6 * width // GROUPS :].astype(F32)
    for group in range(1, GROUPS):
        total = total + held[0, group, 6 * width // GROUPS :].astype(F32)
    return total


def pick_kernel(parts, facts, *refs):
    outs, sems = refs[-1 - len(parts) : -1], refs[-1]
    options = refs[: 4 * sum(parts)]
    for section in range(4):

        @pl.when(facts[0, STAGE] * 2 + facts[0, CORE] == section)
        def _():
            copies, at = [], 0
            for out, count in zip(outs, parts):
                row = 0
                for i in range(count):
                    source = options[at + 4 * i + section]
                    copies.append(
                        pltpu.make_async_copy(source, out.at[pl.ds(row, source.shape[0])], sems.at[len(copies)])
                    )
                    row += source.shape[0]
                at += 4 * count
            for copy in copies:
                copy.start()
            for copy in copies:
                copy.wait()


def pick(facts, *choices, waits=()):
    shapes = [
        pltpu.VMEM((sum(options[0].shape[0] for options in parts), parts[0][0].shape[1]), BF16) for parts in choices
    ]
    given = [option for parts in choices for options in parts for option in options]
    return pl.pallas_call(
        functools.partial(pick_kernel, tuple(len(parts) for parts in choices)),
        out_shape=tuple(shapes),
        in_specs=[SMEM] + [ANY] * (len(given) + len(waits)),
        out_specs=tuple([VMEM] * len(choices)),
        scratch_shapes=[pltpu.SemaphoreType.DMA((sum(len(parts) for parts in choices),))],
        compiler_params=params(3),
        cost_estimate=LIGHT,
        name="pick",
    )(facts, *(in_hbm(given) if waits else given), *waits)


def split_kernel(first, second, low, high, sems):
    copies = [
        pltpu.make_async_copy(first.at[pl.ds(0, low.shape[0])], low, sems.at[0]),
        pltpu.make_async_copy(second.at[pl.ds(low.shape[0], high.shape[0])], high, sems.at[1]),
    ]
    for copy in copies:
        copy.start()
    for copy in copies:
        copy.wait()


def split(first, second, cut, *waits):
    rows, width = first.shape
    return pl.pallas_call(
        lambda *refs: split_kernel(*refs[:2], *refs[2 + len(waits) :]),
        out_shape=(pltpu.VMEM((cut, width), BF16), pltpu.VMEM((rows - cut, width), BF16)),
        in_specs=[ANY] * (2 + len(waits)),
        out_specs=(VMEM, VMEM),
        scratch_shapes=[pltpu.SemaphoreType.DMA((2,))],
        compiler_params=params(3),
        cost_estimate=LIGHT,
        name="split",
    )(first, second, *waits)


def chosen(core_flag, kernel):
    is_first = jnp.max(core_flag[...]) < 0.5
    pl.when(is_first)(functools.partial(kernel, True))
    pl.when(jnp.logical_not(is_first))(functools.partial(kernel, False))


def spare_kernel(spans, core_flag, first, second, *refs):
    def copy(is_first):
        for span, out in zip(spans, refs):
            out[...] = (second if is_first else first)[:, slice(*span)]

    chosen(core_flag, copy)


def spare_half(core_flag, first, second, spans):
    blocks, _, width = first.shape
    return pl.pallas_call(
        functools.partial(spare_kernel, spans),
        out_shape=tuple(pltpu.VMEM((blocks, high - low, width), BF16) for low, high in spans),
        in_specs=[VMEM] * 3,
        out_specs=tuple([VMEM] * len(spans)),
        compiler_params=params(2),
        cost_estimate=LIGHT,
        name="spare_half",
    )(core_flag, first, second)


def merge_kernel(spans, core_flag, first, second, *refs):
    got, outs = refs[: len(spans)], refs[-2 * len(spans) :]

    def add(is_first):
        keep = first if is_first else second
        for part, span in enumerate(spans):
            held, own = outs[2 * part], outs[2 * part + 1]
            own[0] = keep[0, slice(*span)] + got[part][0]
            held[...] = keep[1:, slice(*span)] + got[part][1:]

    chosen(core_flag, add)


def merge(core_flag, first, second, got, spans, waits=()):
    blocks, _, width = first.shape
    outs = [pltpu.VMEM((count, high - low, width), BF16) for low, high in spans for count in (blocks - 1, 1)]
    return pl.pallas_call(
        functools.partial(merge_kernel, spans),
        out_shape=tuple(outs),
        in_specs=[VMEM] * (3 + len(got)) + [ANY] * len(waits),
        out_specs=tuple([VMEM] * len(outs)),
        compiler_params=params(8),
        cost_estimate=STEP,
        name="merge",
    )(core_flag, first, second, *got, *waits)


def rows_kernel(plan, name, core_flag, first, second, *refs):
    mine, theirs = refs[-2:]
    span, run = plan.spans[name], plan.micros * plan.tokens

    def copy(is_first):
        one, two = (first, second) if is_first else (second, first)
        mine[...] = one[:, :, span].reshape(run, plan.width)
        theirs[...] = two[:, :, span].reshape(run, plan.width)

    chosen(core_flag, copy)


def layer_rows(plan, name, core_flag, states, waits):
    shape = pltpu.VMEM((plan.micros * plan.tokens, plan.width), BF16)
    return pl.pallas_call(
        functools.partial(rows_kernel, plan, name),
        out_shape=(shape, shape),
        in_specs=[VMEM] * 3 + [ANY] * len(waits),
        out_specs=(VMEM, VMEM),
        compiler_params=params(2),
        cost_estimate=STEP,
        name="layer_rows",
    )(core_flag, *states, *waits)


def ring_add_kernel(sums, n_arrived, held, *refs):
    arrived, outs = refs[:n_arrived], refs[-len(sums) :]
    for (block, parts), out in zip(sums, outs):
        total = held[block].astype(F32)
        for part in parts:
            total = total + arrived[part][...].astype(F32)
        out[...] = total.astype(BF16)


def ring_add(held, arrived, sums, waits=()):
    return pl.pallas_call(
        functools.partial(ring_add_kernel, sums, len(arrived)),
        out_shape=tuple(pltpu.VMEM(held.shape[1:], BF16) for _ in sums),
        in_specs=[VMEM] * (1 + len(arrived)) + [ANY] * len(waits),
        out_specs=tuple([VMEM] * len(sums)),
        compiler_params=params(5),
        cost_estimate=STEP,
        name="ring_add",
    )(held, *arrived, *waits)


def normalise(values):
    center = values - jnp.mean(values, axis=-1, keepdims=True)
    spread = jnp.mean(center * center, axis=-1, keepdims=True)
    scale = lax.rsqrt(spread + 1e-05)
    return center * scale, scale


def norm_back(grad, gain, unit, scale):
    grad_unit = grad * gain
    mean_grad = jnp.mean(grad_unit, axis=-1, keepdims=True)
    mean_dot = jnp.mean(grad_unit * unit, axis=-1, keepdims=True)
    return scale * (grad_unit - mean_grad - unit * mean_dot)


def stack_heads(pair, low_lanes):
    zero = jnp.zeros_like(pair)
    return jnp.concatenate([jnp.where(low_lanes, pair, zero), jnp.where(low_lanes, zero, pair)], axis=0)


def load_source(slot, kind, refs, target, sem):
    if kind == "each":
        for micro, ref in enumerate(refs):

            @pl.when(slot == micro)
            def _():
                pltpu.make_async_copy(ref, target, sem).start()

    else:
        pltpu.make_async_copy(refs[0].at[slot] if kind == "slot" else refs[0], target, sem).start()


def for_slots(flag, micros, micro, work):
    @pl.when(jnp.max(flag[...]) > 0.5)
    def _():
        if micro is None:
            pl.loop(0, micros)(work)
        else:
            work(micro)


def forward_kernel(plan, micro, kind, count, has_state, n_waits, flag, *refs):
    sources, whole = refs[:count], micro is None
    bias_v, held = refs[count : count + 2]
    state, low_o, sem = refs[count + 2 + int(has_state) + n_waits :]
    tokens, width = plan.tokens, plan.width
    weight = lambda block: weight_block(held, width, block)

    def work(slot):
        value_of = lambda name: state.at[slot, :, plan.spans[name]]
        low_v = low_o.at[slot] if whole else low_o
        hidden_v, q_v, k_v, v_v, probs_v, mixed_v, middle_v, act_v, slope_v = (
            value_of(name) for name in ("hidden", "q", "k", "v", "probs", "mixed", "middle", "act", "slope")
        )
        load_source(slot, kind, sources, hidden_v, sem)
        small = small_rows(held, width)
        gain_one, shift_one, gain_two, shift_two, down_bias = (small[i : i + 1] for i in range(5))
        pltpu.make_async_copy(hidden_v, hidden_v, sem).wait()
        hidden = hidden_v[...].astype(F32)
        unit, _ = normalise(hidden)
        normed = (unit * gain_one + shift_one).astype(BF16)
        q_v[...] = (dot(normed, weight(0)) * HEAD_DIM**-0.5).astype(BF16)
        k_v[...] = dot(normed, weight(1)).astype(BF16)
        v_v[...] = dot(normed, weight(6)).astype(BF16)
        low_lanes = lax.broadcasted_iota(jnp.int32, (128, 128), 1) < HEAD_DIM
        for group in range(tokens // 128):
            rows = slice(group * 128, group * 128 + 128)
            bias = bias_v[slot, rows]
            bias = jnp.concatenate([bias, bias], axis=0)
            for pair in range(width // 128):
                lanes = slice(pair * 128, pair * 128 + 128)
                query = stack_heads(q_v[rows, lanes], low_lanes)
                scores = dot_rhs_t(query, k_v[rows, lanes]) + bias
                raised = jnp.exp(scores - jnp.max(scores, axis=-1, keepdims=True))
                probs = (raised * (1.0 / jnp.sum(raised, axis=-1, keepdims=True))).astype(BF16)
                probs_v[rows, pair * 256 : pair * 256 + 128] = probs[:128]
                probs_v[rows, pair * 256 + 128 : pair * 256 + 256] = probs[128:]
                mixed = dot(probs, v_v[rows, lanes])
                mixed_v[rows, lanes] = jnp.where(low_lanes, mixed[:128], mixed[128:]).astype(BF16)
        middle = hidden + dot(mixed_v[...], weight(7))
        high = middle.astype(BF16)
        middle_v[:, :width] = high
        middle_v[:, width:] = (middle - high.astype(F32)).astype(BF16)
        unit, _ = normalise(middle)
        normed = (unit * gain_two + shift_two).astype(BF16)
        total = middle + down_bias
        for block in range(plan.blocks):
            lanes = slice(block * width, (block + 1) * width)
            before = dot(normed, weight(2 + block)) + small[5 + block : 6 + block]
            square = before * before
            tanh = jnp.tanh(before * (0.7978845608028654 + 0.035677408136300125 * square))
            half = 0.5 * tanh + 0.5
            act = (before * half).astype(BF16)
            act_v[:, lanes] = act
            slope = half + before * (0.5 - 0.5 * (tanh * tanh)) * (0.7978845608028654 + 0.10703222440890037 * square)
            slope_v[:, lanes] = slope.astype(BF16)
            total = total + dot(act, weight(8 + block))
        low = total.astype(BF16)
        low_v[...] = low
        value_of("result")[...] = low

    for_slots(flag, plan.micros, micro, work)


def forward_call(plan, flag, micro, source, bias, held, state, waits=(), cost=LIGHT):
    kind, *given = source
    state = [] if state is None else [state]
    tokens, width = plan.tokens, plan.width
    low = ((plan.micros,) if micro is None else ()) + (tokens, width)
    return pl.pallas_call(
        functools.partial(forward_kernel, plan, micro, kind, len(given), bool(state), len(waits)),
        out_shape=(plan.state, pltpu.VMEM(low, BF16)),
        in_specs=[VMEM] + [ANY] * len(given) + [VMEM] * (2 + len(state)) + [ANY] * len(waits),
        out_specs=(VMEM, VMEM),
        input_output_aliases={3 + len(given): 0} if state else {},
        scratch_shapes=[pltpu.SemaphoreType.DMA],
        compiler_params=params(8),
        cost_estimate=cost,
        name="layer_forward",
    )(flag, *given, bias, held, *state, *waits)


def backward_kernel(plan, micro, kind, count, has_sums, n_waits, flag, *refs):
    sources, whole = refs[:count], micro is None
    held = refs[count]
    state, sums_o, low_o, grad_v, do_v, sem = refs[count + 2 + int(has_sums) + n_waits :]
    tokens, width = plan.tokens, plan.width
    weight = lambda block: weight_block(held, width, block)

    def work(slot):
        value_of = lambda name: state.at[slot, :, plan.spans[name]]
        low_v = low_o.at[slot] if whole else low_o
        upstream_v, hidden_v, q_v, k_v, v_v, probs_v, middle_v, du_v = (
            value_of(name) for name in ("upstream", "hidden", "q", "k", "v", "probs", "middle", "slope")
        )
        load_source(slot, kind, sources, upstream_v, sem)
        small = small_rows(held, width)
        gain_one, shift_one, gain_two, shift_two = (small[i : i + 1] for i in range(4))
        sums_v = sums_o.at[slot]
        sums_v[...] = jnp.zeros(sums_v.shape, F32)
        pltpu.make_async_copy(upstream_v, upstream_v, sem).wait()
        upstream_low = upstream_v[...]
        upstream = upstream_low.astype(F32)
        sums_v[4:5] = jnp.sum(upstream, axis=0, keepdims=True)
        da = jnp.zeros((tokens, width), F32)
        for block in range(plan.blocks):
            lanes = slice(block * width, (block + 1) * width)
            dz = dot_rhs_t(upstream_low, weight(8 + block))
            du = (dz * du_v[:, lanes].astype(F32)).astype(BF16)
            du_v[:, lanes] = du
            sums_v[5 + block : 6 + block] = jnp.sum(du.astype(F32), axis=0, keepdims=True)
            da = da + dot_rhs_t(du, weight(2 + block))
        unit, scale = normalise(middle_v[:, :width].astype(F32) + middle_v[:, width:].astype(F32))
        value_of("normed_two")[...] = (unit * gain_two + shift_two).astype(BF16)
        sums_v[2:3] = jnp.sum(da * unit, axis=0, keepdims=True)
        sums_v[3:4] = jnp.sum(da, axis=0, keepdims=True)
        grad_middle = upstream + norm_back(da, gain_two, unit, scale)
        grad_v[...] = grad_middle
        r1 = grad_middle.astype(BF16)
        value_of("r1")[...] = r1
        do_v[...] = dot_rhs_t(r1, weight(7)).astype(BF16)
        low_lanes = lax.broadcasted_iota(jnp.int32, (128, 128), 1) < HEAD_DIM
        for group in range(tokens // 128):
            rows = slice(group * 128, group * 128 + 128)
            for pair in range(width // 128):
                lanes = slice(pair * 128, pair * 128 + 128)
                query = stack_heads(q_v[rows, lanes], low_lanes)
                key = k_v[rows, lanes]
                grad_mixed = stack_heads(do_v[rows, lanes], low_lanes)
                probs = jnp.concatenate(
                    [probs_v[rows, pair * 256 : pair * 256 + 128], probs_v[rows, pair * 256 + 128 : pair * 256 + 256]], axis=0
                )
                grad_probs = dot_rhs_t(grad_mixed, v_v[rows, lanes])
                v_v[rows, lanes] = dot_lhs_t(probs, grad_mixed).astype(BF16)
                probs = probs.astype(F32)
                weighted = grad_probs * probs
                grad_scores = (weighted - probs * jnp.sum(weighted, axis=-1, keepdims=True)).astype(BF16)
                dq = dot(grad_scores, key) * HEAD_DIM**-0.5
                q_v[rows, lanes] = jnp.where(low_lanes, dq[:128], dq[128:]).astype(BF16)
                k_v[rows, lanes] = dot_lhs_t(grad_scores, query).astype(BF16)
        unit, scale = normalise(hidden_v[...].astype(F32))
        value_of("normed_one")[...] = (unit * gain_one + shift_one).astype(BF16)
        da = dot_rhs_t(q_v[...], weight(0)) + dot_rhs_t(k_v[...], weight(1)) + dot_rhs_t(v_v[...], weight(6))
        sums_v[0:1] = jnp.sum(da * unit, axis=0, keepdims=True)
        sums_v[1:2] = jnp.sum(da, axis=0, keepdims=True)
        low = (grad_v[...] + norm_back(da, gain_one, unit, scale)).astype(BF16)
        low_v[...] = low
        value_of("grad")[...] = low

    for_slots(flag, plan.micros, micro, work)


def backward_call(plan, flag, micro, source, held, state, sums, waits=()):
    kind, *given = source
    tokens, width = plan.tokens, plan.width
    sums = [] if sums is None else [sums]
    low = ((plan.micros,) if micro is None else ()) + (tokens, width)
    return pl.pallas_call(
        functools.partial(backward_kernel, plan, micro, kind, len(given), bool(sums), len(waits)),
        out_shape=(
            plan.state,
            pltpu.VMEM((plan.micros, SMALL_ROWS, width), F32),
            pltpu.VMEM(low, BF16),
        ),
        in_specs=[VMEM] + [ANY] * len(given) + [VMEM] * (2 + len(sums)) + [ANY] * len(waits),
        out_specs=(VMEM, VMEM, VMEM),
        input_output_aliases={2 + len(given) + i: i for i in range(1 + len(sums))},
        scratch_shapes=[pltpu.VMEM((tokens, width), F32), pltpu.VMEM((tokens, width), BF16), pltpu.SemaphoreType.DMA],
        compiler_params=params(8),
        cost_estimate=LIGHT,
        name="layer_backward",
    )(flag, *given, held, state, *sums, *waits)


def weight_kernel(plan, facts, sums, state, *refs):
    halves = refs[-2:]
    width, run = plan.width, plan.micros * plan.tokens
    part = width // GROUPS

    def value_of(name, block=0):
        at = plan.spans[name].start + block * width
        return state[:, :, at : at + width].reshape(run, width)

    def put(half, grad, groups, row, rows):
        grad = grad.astype(BF16)
        for index, group in enumerate(groups):
            source = grad[index * rows : (index + 1) * rows] if grad.shape[0] > rows else grad
            halves[half][facts[0, SPOT + group], row : row + rows] = source

    everyone = range(GROUPS)
    small = sums[0]
    for micro in range(1, plan.micros):
        small = small + sums[micro]
    for half in range(2):
        put(half, small, everyone, 6 * part, SMALL_ROWS)
    left = value_of("normed_one").T
    put(0, dot(left, value_of("q")), everyone, 0, part)
    put(0, dot(left, value_of("k")), everyone, part, part)
    put(1, dot(left, value_of("v")), everyone, 0, part)
    put(1, dot(value_of("mixed").T, value_of("r1")), everyone, part, part)
    left = value_of("normed_two").T
    for block in range(plan.blocks):
        put(0, dot(left, value_of("slope", block)), everyone, (2 + block) * part, part)
    right = value_of("upstream")
    of_block = GROUPS // plan.blocks
    for block in range(plan.blocks):
        groups = range(block * of_block, (block + 1) * of_block)
        put(1, dot(value_of("act", block).T, right), groups, 2 * part, 4 * part)


def weight_call(plan, facts, state, sums, waits=()):
    width = plan.width
    shape = (GROUPS, 6 * width // GROUPS + SMALL_ROWS, width)
    run = plan.micros * plan.tokens
    return pl.pallas_call(
        functools.partial(weight_kernel, plan),
        out_shape=(pltpu.VMEM(shape, BF16), pltpu.VMEM(shape, BF16)),
        in_specs=[SMEM, VMEM, VMEM] + [ANY] * len(waits),
        out_specs=(VMEM, VMEM),
        compiler_params=params(8),
        cost_estimate=LIGHT,
        name="weight_grads",
    )(facts, sums, state, *waits)


def halves_kernel(facts, *refs):
    inputs, outs, landed, (whole, sems) = refs[:10], refs[10:16], refs[16:26], refs[26:]
    copies = [pltpu.make_async_copy(source, target, sems.at[i]) for i, (source, target) in enumerate(zip(inputs, landed))]
    for copy in copies:
        copy.start()
    w_qkv, w_out, w_up, w_down, *vectors = landed
    part, width = w_out.shape[1:]
    for copy in copies[4:]:
        copy.wait()
    lane = lax.broadcasted_iota(jnp.int32, (1, width), 1)
    rows = []
    for vector in vectors:
        size = vector.shape[1]
        spread = jnp.concatenate([vector[...]] * (width // size), axis=1)
        for row in range(size * GROUPS // width):
            rows.append(jnp.where((lane + row * width) // size == facts[0, PLACE], spread, 0.0))
    rows.append(jnp.zeros((SMALL_ROWS - len(rows), width), F32))
    small = jnp.concatenate(rows, axis=0).astype(BF16)
    first, second = whole.at[0], whole.at[1]
    first[6 * part :] = small
    second[6 * part :] = small
    copies[0].wait()
    for i in range(2):
        first[i * part : (i + 1) * part] = w_qkv[0, :, i * width : (i + 1) * width].astype(BF16)
    second[:part] = w_qkv[0, :, 2 * width :].astype(BF16)
    copies[1].wait()
    second[part : 2 * part] = w_out[0].astype(BF16)
    copies[2].wait()
    for i in range(w_up.shape[2] // width):
        first[(2 + i) * part : (3 + i) * part] = w_up[0, :, i * width : (i + 1) * width].astype(BF16)
    copies[3].wait()
    second[2 * part : 6 * part] = w_down[0].astype(BF16)
    cut = outs[0].shape[0]
    for i, rows in enumerate((slice(0, cut), slice(cut, None))):
        outs[i][...] = first[rows]
        outs[2 + i][...] = second[rows]
        outs[4 + i][...] = whole[1 - facts[0, CORE], rows]


def halves_call(facts, matrices, vectors, cut):
    _, part, width = matrices[1].shape
    rows = 6 * part + SMALL_ROWS
    shapes = [pltpu.VMEM((size, width), BF16) for size in (cut, rows - cut)]
    inputs = (*matrices, *vectors)
    outs = pl.pallas_call(
        halves_kernel,
        out_shape=(*shapes, *shapes, *shapes),
        in_specs=[SMEM] + [ANY] * len(inputs),
        out_specs=tuple([VMEM] * 6),
        scratch_shapes=[pltpu.VMEM(value.shape, F32) for value in inputs]
        + [pltpu.VMEM((2, rows, width), BF16), pltpu.SemaphoreType.DMA((len(inputs),))],
        compiler_params=params(8),
        cost_estimate=LIGHT,
        name="round_shard",
    )(facts, *in_hbm(inputs))
    return outs[:2], outs[2:4], outs[4:]


def assemble_kernel(facts, mine, theirs, *refs):
    out, token, landed, wide, sems = refs[-5:]
    token[...] = jnp.zeros_like(token)
    copies = [pltpu.make_async_copy(source, landed.at[i], sems.at[i]) for i, source in enumerate((mine, theirs))]
    for copy in copies:
        copy.start()
    saves = []
    for i, copy in enumerate(copies):
        copy.wait()
        wide[i] = landed[i].astype(F32)
        half = facts[0, CORE] if i == 0 else 1 - facts[0, CORE]
        saves.append(pltpu.make_async_copy(wide.at[i], out.at[half], sems.at[2 + i]))
        saves[-1].start()
    for copy in saves:
        copy.wait()


def assemble(facts, mine, theirs, waits):
    rows, width = mine.shape
    return pl.pallas_call(
        assemble_kernel,
        out_shape=(pltpu.HBM((2, rows, width), F32), pltpu.VMEM((8, 128), F32)),
        in_specs=[SMEM] + [ANY] * (2 + len(waits)),
        out_specs=(ANY, VMEM),
        scratch_shapes=[
            pltpu.VMEM((2, rows, width), BF16),
            pltpu.VMEM((2, rows, width), F32),
            pltpu.SemaphoreType.DMA((4,)),
        ],
        compiler_params=params(6),
        cost_estimate=STEP,
        name="assemble",
    )(facts, mine, theirs, *waits)


def unpack_kernel(counts, facts, *refs):
    total = 4 * sum(counts)
    options, outs, (landed, sems) = refs[:total], refs[total : total + 10], refs[total + 10 :]
    grad_qkv, grad_out, grad_up, grad_down, *vectors = outs
    for section in range(4):

        @pl.when(facts[0, STAGE] * 2 + facts[0, CORE] == section)
        def _():
            for half, count in enumerate(counts):
                row = 0
                for i in range(count):
                    source = options[4 * (sum(counts[:half]) + i) + section]
                    target = landed.at[half, pl.ds(row, source.shape[0])]
                    pltpu.make_async_copy(source, target, sems.at[half]).start()
                    row += source.shape[0]

    for half in range(2):
        pltpu.make_async_copy(landed.at[half], landed.at[half], sems.at[half]).wait()
    part, width = grad_out.shape[1:]
    block = lambda half, first, count=1: landed[half, first * part : (first + count) * part].astype(F32)
    grad_qkv[0, :, :width] = block(0, 0)
    grad_qkv[0, :, width : 2 * width] = block(0, 1)
    grad_qkv[0, :, 2 * width :] = block(1, 0)
    grad_out[0] = block(1, 1)
    for i in range(grad_up.shape[2] // width):
        grad_up[0, :, i * width : (i + 1) * width] = block(0, 2 + i)
    grad_down[0] = block(1, 2, 4)
    small = landed[0, 6 * part :].astype(F32)
    for place in range(GROUPS):

        @pl.when(facts[0, PLACE] == place)
        def _():
            row = 0
            for vector in vectors:
                size = vector.shape[1]
                first = row * width + place * size
                lanes = first % width
                vector[...] = small[first // width : first // width + 1, lanes : lanes + size]
                row += size * GROUPS // width


def unpack(facts, first, second, shapes):
    given = [option for parts in (first, second) for options in parts for option in options]
    rows = sum(options[0].shape[0] for options in first)
    return pl.pallas_call(
        functools.partial(unpack_kernel, (len(first), len(second))),
        out_shape=tuple(jax.ShapeDtypeStruct(shape, F32) for shape in shapes),
        in_specs=[SMEM] + [ANY] * len(given),
        out_specs=tuple([VMEM] * len(shapes)),
        scratch_shapes=[pltpu.VMEM((2, rows, first[0][0].shape[1]), BF16), pltpu.SemaphoreType.DMA((2,))],
        compiler_params=params(8),
        cost_estimate=LIGHT,
        name="unpack",
    )(facts, *given)


CYCLE = (0, 2, 4, 6, 7, 5, 3, 1)
OFFSETS = (0, -1, 1, -2, 2, -3, 3, 4)


def send(value, pairs):
    return lax.ppermute(value, "section", pairs)


def to_core(value):
    return send(value, [(i, i ^ 1) for i in range(4)])


def onward(value):
    return send(value, [(0, 2), (1, 3)])


def backward(value):
    return send(value, [(2, 0), (3, 1)])


def along(value, by):
    size = len(CYCLE)
    return lax.ppermute(value, "dp", [(CYCLE[i], CYCLE[(i + by) % size]) for i in range(size)])


class Ring:
    def __init__(self, piece, low, high, cut):
        self.low, self.high, self.cut = low, high, cut
        self.arrived, self.places = [piece], [(0, low, high)]

    def level(self, *waits):
        if len(self.arrived) > 1:
            ahead, behind = self.arrived[-2:]
            ahead = after(ahead, behind, *waits)
            self.arrived[-2:] = [ahead, after(behind, ahead)]
        return (self.arrived * 2)[-2:]

    def step(self, *waits):
        ahead, behind = self.level(*waits)
        self.arrived += along(ahead, 1), along(behind, -1)
        self.places += [(len(self.places) + i, self.low, self.high) for i in range(2)]

    def last_step(self, *waits):
        ahead, behind = self.level(*waits)
        if self.cut == self.high:
            self.arrived.append(along(ahead, 1))
            self.places.append((7, self.low, self.high))
        else:
            self.arrived.append(along(behind, -1))
            self.places.append((7, self.low, self.high))


def advance(rings):
    ahead = ()
    for ring in rings:
        before = ring.arrived[-2:]
        ring.step(*ahead)
        ahead = (*ahead, *before)


class Gather:
    def __init__(self, facts, rings):
        self.facts, self.rings, self.done, self.held = facts, rings, 0, None

    def lay_out(self, count, *waits):
        span = slice(self.done, count)
        pieces = [piece for ring in self.rings for piece in ring.arrived[span]]
        places = tuple(place for ring in self.rings for place in ring.places[span])
        self.done = count
        self.held = gather_call(self.facts, places, pieces, [to_core(piece) for piece in pieces], self.held, waits)
        return self.held


class Scatter:
    def __init__(self, held, own, far_way):
        self.held, self.own, self.far_way, self.next, self.arrived = held, own, far_way, 4, {}

    def step(self, *waits):
        step, at = self.next, lambda offset: OFFSETS.index(offset) - 1
        if step == 4:
            ways = [(self.far_way, at(4))]
        elif step:
            ways = [(1, at(step)), (-1, at(-step))]
        else:
            ways = [(0, 0)]
        arrived = list(self.arrived.items())
        sums = tuple((block, tuple(i for i, (came, _) in enumerate(arrived) if not way or came == way)) for way, block in ways)
        parts = ring_add(self.held if step else self.own, [part for _, part in arrived], sums, waits)
        self.next -= 1
        if step:
            self.arrived = {way: along(part, way) for (way, _), part in zip(ways, parts)}
        else:
            self.total = parts[0]
        return parts[0]


def scatters(core_flag, halves, got, spans, token):
    merged = merge(core_flag, *halves, got, spans, (token,))
    parts = [Scatter(merged[2 * i], merged[2 * i + 1], far_way) for i, far_way in enumerate((1, -1))]
    token = merged[1]
    for each in parts:
        token = each.step(token)
    return parts, token


def facts_table(dp_count):
    ring = dp_count == len(CYCLE)
    table = np.zeros((4, dp_count, 1, FACTS), np.int32)
    for section in range(4):
        for place in range(dp_count):
            facts = table[section, place, 0]
            facts[[CORE, STAGE, PLACE]] = section % 2, section // 2, place
            for i, offset in enumerate(OFFSETS):
                owner = CYCLE[(CYCLE.index(place) + offset) % dp_count] if ring else i
                facts[ORDER + i], facts[SPOT + owner] = owner, i
    return table


def on_device(
    frames_in,
    segment_ids,
    cotangent,
    w_qkv,
    w_out,
    w_up,
    w_down,
    norm1_gain,
    norm1_shift,
    norm2_gain,
    norm2_shift,
    up_bias,
    down_bias,
):
    section = lax.axis_index("section")
    dp_index, dp_count = lax.axis_index("dp"), lax.axis_size("dp")
    rows, frame_count, width = frames_in.shape
    hidden_units = w_up.shape[2]
    own_rows = rows // 2
    tokens = own_rows * frame_count // MICRO
    ring = dp_count == len(CYCLE)
    part = w_qkv.shape[1]
    cut = 3 * width // GROUPS
    plan = Plan(MICRO, tokens, width, hidden_units)

    table = jnp.asarray(facts_table(dp_count))
    facts = lax.dynamic_slice(table, (section, dp_index, 0, 0), (1, 1) + table.shape[2:])[0, 0]

    segments = lax.dynamic_slice_in_dim(segment_ids, section % 2 * own_rows, own_rows, 0).reshape(-1, 128)
    spot = jnp.arange(128, dtype=jnp.int32)
    allowed = (spot[None, :] <= spot[:, None]) & (spot[None, :] // frame_count == spot[:, None] // frame_count)
    allowed = allowed[None] & (segments[:, :, None] == segments[:, None, :])
    bias = jnp.where(allowed, 0.0, -1e30).astype(F32).reshape(MICRO, tokens, 128)
    frames, last_grads = (
        lax.dynamic_slice_in_dim(value, section % 2 * own_rows, own_rows, 0).reshape(MICRO, tokens, width)
        for value in (frames_in, cotangent)
    )
    flags = [jnp.full((8, 128), flag, F32) for flag in (section < 2, section >= 2, section % 2 == 1)]

    matrices = (w_qkv, w_out, w_up, w_down)
    vectors = (norm1_gain, norm1_shift, norm2_gain, norm2_shift, down_bias, up_bias)
    if ring:
        height = 2 * cut + SMALL_ROWS
        one, two, spare = halves_call(facts, matrices, vectors, cut)
        near = [to_core(part_of) for part_of in spare]
        first_parts = [pick(facts, [(one[i], near[i]) * 2])[0] for i in range(2)]
        spans = ((0, cut), (cut, height))
        rings = [Ring(piece, *span, cut) for piece, span in zip(first_parts, spans)]
        second_parts = [pick(facts, [(near[i], two[i]) * 2])[0] for i in range(2)]
        besides = (frames, last_grads, bias, *flags, *second_parts)
        for step in range(3):
            for each in rings:
                each.step(*(besides if step == 1 else ()))
        for each in rings:
            each.last_step()
        last = [each.arrived[-1] for each in rings]
        second_rings = [Ring(after(piece, *last), *span, cut) for piece, span in zip(second_parts, spans)]
        for _ in range(3):
            for each in second_rings:
                each.step()
        gather = Gather(facts, rings)
        gather.lay_out(5)
        token = gather.lay_out(8)
        held = [gather.held]
    else:
        token = facts
        blocks = [w_qkv[0, :, :width], w_qkv[0, :, width : 2 * width]]
        blocks += [w_up[0, :, i * width : (i + 1) * width] for i in range(hidden_units // width)]
        blocks += [w_qkv[0, :, 2 * width :], w_out[0], w_down[0]]
        whole = jnp.concatenate([lax.all_gather(block.astype(BF16), "dp", axis=0, tiled=True) for block in blocks])
        flat = [lax.all_gather(vector[0].astype(BF16), "dp", axis=0, tiled=True) for vector in vectors]
        small = jnp.concatenate(flat + [jnp.zeros(((SMALL_ROWS - 5) * width - hidden_units,), BF16)])
        grouped = lambda low, count: jnp.swapaxes(
            whole[low * width : (low + count) * width].reshape(count, GROUPS, -1, width), 0, 1
        ).reshape(GROUPS, -1, width)
        small = jnp.pad(small.reshape(1, SMALL_ROWS, width), ((0, GROUPS - 1), (0, 0), (0, 0)))
        down = whole[8 * width :].reshape(GROUPS, -1, width)
        value = jnp.stack(
            [jnp.concatenate([grouped(0, 6), small], 1), jnp.concatenate([grouped(6, 2), down, small], 1)]
        )
        got = lax.all_gather(value, "section")
        held = [jnp.where(section < 2, got[i], got[i + 2]) for i in (0, 1)]

    states, sums = [None, None], [None, None]

    def whole_rows(name, token):
        mine, theirs = layer_rows(plan, name, flags[2], states, (token,))
        whole, token = assemble(facts, mine, to_core(theirs), (mine,))
        return whole.reshape(1, rows, frame_count, width), token


    def run_forward(layer, stage, micro, source, token, cost=LIGHT):
        states[layer], low = forward_call(
            plan, flags[stage], micro, source, bias, held[layer], states[layer], (token,), cost
        )
        return low

    def run_backward(layer, stage, micro, source, token):
        states[layer], sums[layer], low = backward_call(
            plan, flags[stage], micro, source, held[layer], states[layer], sums[layer], (token,)
        )
        return low

    token = stage_zero_low = run_forward(0, 0, None, ("slot", frames), token, HEAVY)
    if ring:
        for each in second_rings:
            each.last_step(token)
        gather = Gather(facts, second_rings)
        gather.lay_out(5, token)
        token = gather.lay_out(8)
        held.append(gather.held)
    hops = []
    for micro in range(MICRO):
        token = run_forward(1, 0, micro, ("slot", stage_zero_low), token)
        hops.append(onward(token))
    lows = []
    for micro in range(MICRO):
        token = run_forward(0, 1, micro, ("one", hops[micro]), token)
        lows.append(token)
    token = run_forward(1, 1, None, ("each", *lows), token)
    token = stage_one_back = run_backward(1, 1, None, ("slot", last_grads), token)
    hops = []
    for micro in range(MICRO):
        token = run_backward(0, 1, micro, ("slot", stage_one_back), token)
        hops.append(backward(token))
    lows = []
    for micro in range(MICRO):
        token = run_backward(1, 0, micro, ("one", hops[micro]), token)
        lows.append(token)

    halves = weight_call(plan, facts, states[1], sums[1], (token,))
    totals = [halves]
    if ring:
        give = spare_half(flags[2], *halves, spans)
        got = [to_core(part_of) for part_of in give]
        token = run_backward(0, 0, 0, ("one", lows[0]), give[1])
        second, token = scatters(flags[2], halves, got, spans, token)
        for micro in range(1, MICRO):
            token = run_backward(0, 0, micro, ("one", lows[micro]), token)
        for each in second:
            token = each.step(token)
        halves = weight_call(plan, facts, states[0], sums[0], (token,))
        token = halves[0]
        for each in second:
            token = each.step(token)
        give = spare_half(flags[2], *halves, spans)
        got = [to_core(after(part_of, token)) for part_of in give]
        first, token = scatters(flags[2], halves, got, spans, token)
        for each in second + first + second + first:
            token = each.step(token)
        input_grads, token = whole_rows("grad", token)
        for each in first:
            token = each.step(token)
        outputs, token = whole_rows("result", token)
        for each in first:
            token = each.step(token)
        mine = [(one.total, two.total) for one, two in zip(first, second)]
        is_first = section % 2 == 0
        theirs = [to_core(jnp.where(is_first, two, one)) for one, two in mine]
        grads = unpack(
            facts,
            [(one, other) * 2 for (one, _), other in zip(mine, theirs)],
            [(other, two) * 2 for (_, two), other in zip(mine, theirs)],
            [value.shape for value in matrices + vectors],
        )
        return (outputs, input_grads, *grads[:8], grads[9], grads[8])
    else:
        run_backward(0, 0, None, ("each", *lows), halves[0])
        totals.append(weight_call(plan, facts, states[0], sums[0]))
        (late_one, late_two), (early_one, early_two) = totals
        is_first = section % 2 == 0

        def to_layer(first, second):
            first, second = first.astype(F32), second.astype(F32)
            return jnp.where(is_first, first, second) + to_core(jnp.where(is_first, second, first))

        one, two = to_layer(early_one, late_one), to_layer(early_two, late_two)
        small = lax.psum(one[0, 6 * width // GROUPS :], "dp")
        block = width // GROUPS
        natural = lambda half, low, high: lax.psum_scatter(
            half[:, low * block : high * block].reshape(-1, width), "dp", scatter_dimension=0, tiled=True
        )
        first_grads = [natural(one, i, i + 1) for i in range(6)]
        second_grads = [natural(two, 0, 1), natural(two, 1, 2), natural(two, 2, 6)]
    grad_vectors = [lax.dynamic_slice_in_dim(small[i : i + 1].reshape(-1), dp_index * part, part) for i in range(5)]
    grad_vectors.append(
        lax.dynamic_slice_in_dim(small[5 : 5 + hidden_units // width].reshape(-1), dp_index * 4 * part, 4 * part)
    )
    grad_vectors = [vector[None].astype(F32) for vector in grad_vectors]

    outputs, input_grads = whole_rows("result", small)[0], whole_rows("grad", small)[0]
    return (
        outputs,
        input_grads,
        jnp.concatenate([first_grads[0], first_grads[1], second_grads[0]], axis=1)[None].astype(F32),
        second_grads[1][None].astype(F32),
        jnp.concatenate(first_grads[2:], axis=1)[None].astype(F32),
        second_grads[2][None].astype(F32),
        *grad_vectors[:4],
        grad_vectors[5],
        grad_vectors[4],
    )


def solution(mesh):
    rows = P("dp", None, None)
    matrix, vector = P("section", "dp", None), P("section", "dp")
    result = P("section", "dp", None, None)
    return jax.shard_map(
        on_device,
        mesh=mesh,
        in_specs=(rows, P("dp", None), rows) + (matrix,) * 4 + (vector,) * 6,
        out_specs=(result, result) + (matrix,) * 4 + (vector,) * 6,
        check_vma=False,
    )
```

```python
import functools

import jax
import jax.numpy as jnp
import numpy as np
from jax import lax
from jax.experimental import pallas as pl
from jax.experimental.pallas import tpu as pltpu
from jax.sharding import PartitionSpec as P

HEADS = 8
HEAD_DIM = 64
GROUPS = 8
SMALL_ROWS = 16
MICRO = 2
BF16 = jnp.bfloat16
F32 = jnp.float32
ANY = pl.BlockSpec(memory_space=pl.ANY)
SMEM = pl.BlockSpec(memory_space=pltpu.SMEM)
VMEM = pl.BlockSpec(memory_space=pltpu.VMEM)
LIGHT = pl.CostEstimate(flops=1, bytes_accessed=1, transcendentals=0)
STEP = pl.CostEstimate(flops=3 * 10**8, bytes_accessed=1, transcendentals=0)
TIE = pl.CostEstimate(flops=10**9, bytes_accessed=1, transcendentals=0)
HEAVY = pl.CostEstimate(flops=10**10, bytes_accessed=1, transcendentals=0)
CORE, STAGE, PLACE, ORDER, SPOT = 0, 1, 2, 4, 12
FACTS = 20


class Plan:
    def __init__(self, micros, tokens, width, hidden_units):
        self.micros, self.tokens, self.width, self.hidden_units = micros, tokens, width, hidden_units
        self.blocks = hidden_units // width
        self.spans, at = {}, 0
        sizes = dict(hidden=1, q=1, k=1, v=1, probs=HEADS * 128 // width, mixed=1, middle=2, act=self.blocks, slope=self.blocks,
                     result=1, upstream=1, normed_two=1, r1=1, normed_one=1, grad=1)
        for name, size in sizes.items():
            self.spans[name] = slice(at, at + size * width)
            at += size * width
        self.state = pltpu.VMEM((micros, tokens, at), BF16)


def dot(left, right):
    return lax.dot_general(left, right, (((1,), (0,)), ((), ())), preferred_element_type=F32)


def dot_rhs_t(left, right):
    return lax.dot_general(left, right, (((1,), (1,)), ((), ())), preferred_element_type=F32)


def dot_lhs_t(left, right):
    return lax.dot_general(left, right, (((0,), (0,)), ((), ())), preferred_element_type=F32)


def in_hbm(values):
    return [pltpu.with_memory_space_constraint(value, pltpu.HBM) for value in values]


def params(mebibytes):
    return pltpu.CompilerParams(vmem_limit_bytes=mebibytes << 20)


def after(value, *others):
    return pl.pallas_call(
        lambda *refs: None,
        out_shape=jax.ShapeDtypeStruct(value.shape, value.dtype),
        in_specs=[pl.BlockSpec(memory_space=pl.ANY)] * (1 + len(others)),
        out_specs=pl.BlockSpec(memory_space=pl.ANY),
        input_output_aliases={0: 0},
        compiler_params=params(1),
        cost_estimate=TIE,
        name="after",
    )(value, *others)


def gather_kernel(places, facts, *refs):
    held, count = refs[-1], len(places)
    for own, other, (place, low, high) in zip(refs[:count], refs[count : 2 * count], places):
        for ref, half in ((own, facts[0, CORE]), (other, 1 - facts[0, CORE])):
            held[half, facts[0, ORDER + place], low:high] = ref[...]


def gather_call(facts, places, own, other, held, waits=()):
    held = () if held is None else (held,)
    width = own[0].shape[1]
    rows = 6 * width // GROUPS + SMALL_ROWS
    return pl.pallas_call(
        functools.partial(gather_kernel, places),
        out_shape=pltpu.VMEM((2, GROUPS, rows, width), BF16),
        in_specs=[SMEM] + [VMEM] * (2 * len(own) + len(held)) + [ANY] * len(waits),
        out_specs=VMEM,
        input_output_aliases={1 + 2 * len(own): 0} if held else {},
        compiler_params=params(8),
        cost_estimate=LIGHT,
        name="lay_out_weights",
    )(facts, *own, *other, *held, *waits)


def weight_block(held, width, block):
    part = width // GROUPS
    if block < 6:
        return held[0, :, block * part : (block + 1) * part, :].reshape(width, width)
    if block < 8:
        return held[1, :, (block - 6) * part : (block - 5) * part, :].reshape(width, width)
    first = (block - 8) * 2
    return held[1, first : first + 2, 2 * part : 6 * part, :].reshape(width, width)


def small_rows(held, width):
    total = held[0, 0, 6 * width // GROUPS :].astype(F32)
    for group in range(1, GROUPS):
        total = total + held[0, group, 6 * width // GROUPS :].astype(F32)
    return total


def pick_kernel(parts, facts, *refs):
    outs, sems = refs[-1 - len(parts) : -1], refs[-1]
    options = refs[: 4 * sum(parts)]
    for section in range(4):

        @pl.when(facts[0, STAGE] * 2 + facts[0, CORE] == section)
        def _():
            copies, at = [], 0
            for out, count in zip(outs, parts):
                row = 0
                for i in range(count):
                    source = options[at + 4 * i + section]
                    copies.append(
                        pltpu.make_async_copy(source, out.at[pl.ds(row, source.shape[0])], sems.at[len(copies)])
                    )
                    row += source.shape[0]
                at += 4 * count
            for copy in copies:
                copy.start()
            for copy in copies:
                copy.wait()


def pick(facts, *choices, waits=()):
    shapes = [
        pltpu.VMEM((sum(options[0].shape[0] for options in parts), parts[0][0].shape[1]), BF16) for parts in choices
    ]
    given = [option for parts in choices for options in parts for option in options]
    return pl.pallas_call(
        functools.partial(pick_kernel, tuple(len(parts) for parts in choices)),
        out_shape=tuple(shapes),
        in_specs=[SMEM] + [ANY] * (len(given) + len(waits)),
        out_specs=tuple([VMEM] * len(choices)),
        scratch_shapes=[pltpu.SemaphoreType.DMA((sum(len(parts) for parts in choices),))],
        compiler_params=params(3),
        cost_estimate=LIGHT,
        name="pick",
    )(facts, *(in_hbm(given) if waits else given), *waits)


def split_kernel(first, second, low, high, sems):
    copies = [
        pltpu.make_async_copy(first.at[pl.ds(0, low.shape[0])], low, sems.at[0]),
        pltpu.make_async_copy(second.at[pl.ds(low.shape[0], high.shape[0])], high, sems.at[1]),
    ]
    for copy in copies:
        copy.start()
    for copy in copies:
        copy.wait()


def split(first, second, cut, *waits):
    rows, width = first.shape
    return pl.pallas_call(
        lambda *refs: split_kernel(*refs[:2], *refs[2 + len(waits) :]),
        out_shape=(pltpu.VMEM((cut, width), BF16), pltpu.VMEM((rows - cut, width), BF16)),
        in_specs=[ANY] * (2 + len(waits)),
        out_specs=(VMEM, VMEM),
        scratch_shapes=[pltpu.SemaphoreType.DMA((2,))],
        compiler_params=params(3),
        cost_estimate=LIGHT,
        name="split",
    )(first, second, *waits)


def chosen(core_flag, kernel):
    is_first = jnp.max(core_flag[...]) < 0.5
    pl.when(is_first)(functools.partial(kernel, True))
    pl.when(jnp.logical_not(is_first))(functools.partial(kernel, False))


def spare_kernel(spans, core_flag, first, second, *refs):
    def copy(is_first):
        for span, out in zip(spans, refs):
            out[...] = (second if is_first else first)[:, slice(*span)]

    chosen(core_flag, copy)


def spare_half(core_flag, first, second, spans):
    blocks, _, width = first.shape
    return pl.pallas_call(
        functools.partial(spare_kernel, spans),
        out_shape=tuple(pltpu.VMEM((blocks, high - low, width), BF16) for low, high in spans),
        in_specs=[VMEM] * 3,
        out_specs=tuple([VMEM] * len(spans)),
        compiler_params=params(2),
        cost_estimate=LIGHT,
        name="spare_half",
    )(core_flag, first, second)


def merge_kernel(spans, core_flag, first, second, *refs):
    got, outs = refs[: len(spans)], refs[-2 * len(spans) :]

    def add(is_first):
        keep = first if is_first else second
        for part, span in enumerate(spans):
            held, own = outs[2 * part], outs[2 * part + 1]
            own[0] = keep[0, slice(*span)] + got[part][0]
            held[...] = keep[1:, slice(*span)] + got[part][1:]

    chosen(core_flag, add)


def merge(core_flag, first, second, got, spans, waits=()):
    blocks, _, width = first.shape
    outs = [pltpu.VMEM((count, high - low, width), BF16) for low, high in spans for count in (blocks - 1, 1)]
    return pl.pallas_call(
        functools.partial(merge_kernel, spans),
        out_shape=tuple(outs),
        in_specs=[VMEM] * (3 + len(got)) + [ANY] * len(waits),
        out_specs=tuple([VMEM] * len(outs)),
        compiler_params=params(8),
        cost_estimate=STEP,
        name="merge",
    )(core_flag, first, second, *got, *waits)


def rows_kernel(plan, name, core_flag, first, second, *refs):
    mine, theirs = refs[-2:]
    span, run = plan.spans[name], plan.micros * plan.tokens

    def copy(is_first):
        one, two = (first, second) if is_first else (second, first)
        mine[...] = one[:, :, span].reshape(run, plan.width)
        theirs[...] = two[:, :, span].reshape(run, plan.width)

    chosen(core_flag, copy)


def layer_rows(plan, name, core_flag, states, waits):
    shape = pltpu.VMEM((plan.micros * plan.tokens, plan.width), BF16)
    return pl.pallas_call(
        functools.partial(rows_kernel, plan, name),
        out_shape=(shape, shape),
        in_specs=[VMEM] * 3 + [ANY] * len(waits),
        out_specs=(VMEM, VMEM),
        compiler_params=params(2),
        cost_estimate=STEP,
        name="layer_rows",
    )(core_flag, *states, *waits)


def ring_add_kernel(sums, n_arrived, held, *refs):
    arrived, outs = refs[:n_arrived], refs[-len(sums) :]
    for (block, parts), out in zip(sums, outs):
        total = held[block].astype(F32)
        for part in parts:
            total = total + arrived[part][...].astype(F32)
        out[...] = total.astype(BF16)


def ring_add(held, arrived, sums, waits=()):
    return pl.pallas_call(
        functools.partial(ring_add_kernel, sums, len(arrived)),
        out_shape=tuple(pltpu.VMEM(held.shape[1:], BF16) for _ in sums),
        in_specs=[VMEM] * (1 + len(arrived)) + [ANY] * len(waits),
        out_specs=tuple([VMEM] * len(sums)),
        compiler_params=params(5),
        cost_estimate=STEP,
        name="ring_add",
    )(held, *arrived, *waits)


def normalise(values):
    center = values - jnp.mean(values, axis=-1, keepdims=True)
    spread = jnp.mean(center * center, axis=-1, keepdims=True)
    scale = lax.rsqrt(spread + 1e-05)
    return center * scale, scale


def norm_back(grad, gain, unit, scale):
    grad_unit = grad * gain
    mean_grad = jnp.mean(grad_unit, axis=-1, keepdims=True)
    mean_dot = jnp.mean(grad_unit * unit, axis=-1, keepdims=True)
    return scale * (grad_unit - mean_grad - unit * mean_dot)


def stack_heads(pair, low_lanes):
    zero = jnp.zeros_like(pair)
    return jnp.concatenate([jnp.where(low_lanes, pair, zero), jnp.where(low_lanes, zero, pair)], axis=0)


def load_source(slot, kind, refs, target, sem):
    if kind == "each":
        for micro, ref in enumerate(refs):

            @pl.when(slot == micro)
            def _():
                pltpu.make_async_copy(ref, target, sem).start()

    else:
        pltpu.make_async_copy(refs[0].at[slot] if kind == "slot" else refs[0], target, sem).start()


def for_slots(flag, micros, micro, work):
    @pl.when(jnp.max(flag[...]) > 0.5)
    def _():
        if micro is None:
            pl.loop(0, micros)(work)
        else:
            work(micro)


def forward_kernel(plan, micro, kind, count, has_state, n_waits, flag, *refs):
    sources, whole = refs[:count], micro is None
    bias_v, held = refs[count : count + 2]
    state, low_o, sem = refs[count + 2 + int(has_state) + n_waits :]
    tokens, width = plan.tokens, plan.width
    weight = lambda block: weight_block(held, width, block)

    def work(slot):
        value_of = lambda name: state.at[slot, :, plan.spans[name]]
        low_v = low_o.at[slot] if whole else low_o
        hidden_v, q_v, k_v, v_v, probs_v, mixed_v, middle_v, act_v, slope_v = (
            value_of(name) for name in ("hidden", "q", "k", "v", "probs", "mixed", "middle", "act", "slope")
        )
        load_source(slot, kind, sources, hidden_v, sem)
        small = small_rows(held, width)
        gain_one, shift_one, gain_two, shift_two, down_bias = (small[i : i + 1] for i in range(5))
        pltpu.make_async_copy(hidden_v, hidden_v, sem).wait()
        hidden = hidden_v[...].astype(F32)
        unit, _ = normalise(hidden)
        normed = (unit * gain_one + shift_one).astype(BF16)
        q_v[...] = (dot(normed, weight(0)) * HEAD_DIM**-0.5).astype(BF16)
        k_v[...] = dot(normed, weight(1)).astype(BF16)
        v_v[...] = dot(normed, weight(6)).astype(BF16)
        low_lanes = lax.broadcasted_iota(jnp.int32, (128, 128), 1) < HEAD_DIM
        for group in range(tokens // 128):
            rows = slice(group * 128, group * 128 + 128)
            bias = bias_v[slot, rows]
            bias = jnp.concatenate([bias, bias], axis=0)
            for pair in range(width // 128):
                lanes = slice(pair * 128, pair * 128 + 128)
                query = stack_heads(q_v[rows, lanes], low_lanes)
                scores = dot_rhs_t(query, k_v[rows, lanes]) + bias
                raised = jnp.exp(scores - jnp.max(scores, axis=-1, keepdims=True))
                probs = (raised * (1.0 / jnp.sum(raised, axis=-1, keepdims=True))).astype(BF16)
                probs_v[rows, pair * 256 : pair * 256 + 128] = probs[:128]
                probs_v[rows, pair * 256 + 128 : pair * 256 + 256] = probs[128:]
                mixed = dot(probs, v_v[rows, lanes])
                mixed_v[rows, lanes] = jnp.where(low_lanes, mixed[:128], mixed[128:]).astype(BF16)
        middle = hidden + dot(mixed_v[...], weight(7))
        high = middle.astype(BF16)
        middle_v[:, :width] = high
        middle_v[:, width:] = (middle - high.astype(F32)).astype(BF16)
        unit, _ = normalise(middle)
        normed = (unit * gain_two + shift_two).astype(BF16)
        total = middle + down_bias
        for block in range(plan.blocks):
            lanes = slice(block * width, (block + 1) * width)
            before = dot(normed, weight(2 + block)) + small[5 + block : 6 + block]
            square = before * before
            tanh = jnp.tanh(before * (0.7978845608028654 + 0.035677408136300125 * square))
            half = 0.5 * tanh + 0.5
            act = (before * half).astype(BF16)
            act_v[:, lanes] = act
            slope = half + before * (0.5 - 0.5 * (tanh * tanh)) * (0.7978845608028654 + 0.10703222440890037 * square)
            slope_v[:, lanes] = slope.astype(BF16)
            total = total + dot(act, weight(8 + block))
        low = total.astype(BF16)
        low_v[...] = low
        value_of("result")[...] = low

    for_slots(flag, plan.micros, micro, work)


def forward_call(plan, flag, micro, source, bias, held, state, waits=(), cost=LIGHT):
    kind, *given = source
    state = [] if state is None else [state]
    tokens, width = plan.tokens, plan.width
    low = ((plan.micros,) if micro is None else ()) + (tokens, width)
    return pl.pallas_call(
        functools.partial(forward_kernel, plan, micro, kind, len(given), bool(state), len(waits)),
        out_shape=(plan.state, pltpu.VMEM(low, BF16)),
        in_specs=[VMEM] + [ANY] * len(given) + [VMEM] * (2 + len(state)) + [ANY] * len(waits),
        out_specs=(VMEM, VMEM),
        input_output_aliases={3 + len(given): 0} if state else {},
        scratch_shapes=[pltpu.SemaphoreType.DMA],
        compiler_params=params(8),
        cost_estimate=cost,
        name="layer_forward",
    )(flag, *given, bias, held, *state, *waits)


def backward_kernel(plan, micro, kind, count, has_sums, n_waits, flag, *refs):
    sources, whole = refs[:count], micro is None
    held = refs[count]
    state, sums_o, low_o, grad_v, do_v, sem = refs[count + 2 + int(has_sums) + n_waits :]
    tokens, width = plan.tokens, plan.width
    weight = lambda block: weight_block(held, width, block)

    def work(slot):
        value_of = lambda name: state.at[slot, :, plan.spans[name]]
        low_v = low_o.at[slot] if whole else low_o
        upstream_v, hidden_v, q_v, k_v, v_v, probs_v, middle_v, du_v = (
            value_of(name) for name in ("upstream", "hidden", "q", "k", "v", "probs", "middle", "slope")
        )
        load_source(slot, kind, sources, upstream_v, sem)
        small = small_rows(held, width)
        gain_one, shift_one, gain_two, shift_two = (small[i : i + 1] for i in range(4))
        sums_v = sums_o.at[slot]
        sums_v[...] = jnp.zeros(sums_v.shape, F32)
        pltpu.make_async_copy(upstream_v, upstream_v, sem).wait()
        upstream_low = upstream_v[...]
        upstream = upstream_low.astype(F32)
        sums_v[4:5] = jnp.sum(upstream, axis=0, keepdims=True)
        da = jnp.zeros((tokens, width), F32)
        for block in range(plan.blocks):
            lanes = slice(block * width, (block + 1) * width)
            dz = dot_rhs_t(upstream_low, weight(8 + block))
            du = (dz * du_v[:, lanes].astype(F32)).astype(BF16)
            du_v[:, lanes] = du
            sums_v[5 + block : 6 + block] = jnp.sum(du.astype(F32), axis=0, keepdims=True)
            da = da + dot_rhs_t(du, weight(2 + block))
        unit, scale = normalise(middle_v[:, :width].astype(F32) + middle_v[:, width:].astype(F32))
        value_of("normed_two")[...] = (unit * gain_two + shift_two).astype(BF16)
        sums_v[2:3] = jnp.sum(da * unit, axis=0, keepdims=True)
        sums_v[3:4] = jnp.sum(da, axis=0, keepdims=True)
        grad_middle = upstream + norm_back(da, gain_two, unit, scale)
        grad_v[...] = grad_middle
        r1 = grad_middle.astype(BF16)
        value_of("r1")[...] = r1
        do_v[...] = dot_rhs_t(r1, weight(7)).astype(BF16)
        low_lanes = lax.broadcasted_iota(jnp.int32, (128, 128), 1) < HEAD_DIM
        for group in range(tokens // 128):
            rows = slice(group * 128, group * 128 + 128)
            for pair in range(width // 128):
                lanes = slice(pair * 128, pair * 128 + 128)
                query = stack_heads(q_v[rows, lanes], low_lanes)
                key = k_v[rows, lanes]
                grad_mixed = stack_heads(do_v[rows, lanes], low_lanes)
                probs = jnp.concatenate(
                    [probs_v[rows, pair * 256 : pair * 256 + 128], probs_v[rows, pair * 256 + 128 : pair * 256 + 256]], axis=0
                )
                grad_probs = dot_rhs_t(grad_mixed, v_v[rows, lanes])
                v_v[rows, lanes] = dot_lhs_t(probs, grad_mixed).astype(BF16)
                probs = probs.astype(F32)
                weighted = grad_probs * probs
                grad_scores = (weighted - probs * jnp.sum(weighted, axis=-1, keepdims=True)).astype(BF16)
                dq = dot(grad_scores, key) * HEAD_DIM**-0.5
                q_v[rows, lanes] = jnp.where(low_lanes, dq[:128], dq[128:]).astype(BF16)
                k_v[rows, lanes] = dot_lhs_t(grad_scores, query).astype(BF16)
        unit, scale = normalise(hidden_v[...].astype(F32))
        value_of("normed_one")[...] = (unit * gain_one + shift_one).astype(BF16)
        da = dot_rhs_t(q_v[...], weight(0)) + dot_rhs_t(k_v[...], weight(1)) + dot_rhs_t(v_v[...], weight(6))
        sums_v[0:1] = jnp.sum(da * unit, axis=0, keepdims=True)
        sums_v[1:2] = jnp.sum(da, axis=0, keepdims=True)
        low = (grad_v[...] + norm_back(da, gain_one, unit, scale)).astype(BF16)
        low_v[...] = low
        value_of("grad")[...] = low

    for_slots(flag, plan.micros, micro, work)


def backward_call(plan, flag, micro, source, held, state, sums, waits=()):
    kind, *given = source
    tokens, width = plan.tokens, plan.width
    sums = [] if sums is None else [sums]
    low = ((plan.micros,) if micro is None else ()) + (tokens, width)
    return pl.pallas_call(
        functools.partial(backward_kernel, plan, micro, kind, len(given), bool(sums), len(waits)),
        out_shape=(
            plan.state,
            pltpu.VMEM((plan.micros, SMALL_ROWS, width), F32),
            pltpu.VMEM(low, BF16),
        ),
        in_specs=[VMEM] + [ANY] * len(given) + [VMEM] * (2 + len(sums)) + [ANY] * len(waits),
        out_specs=(VMEM, VMEM, VMEM),
        input_output_aliases={2 + len(given) + i: i for i in range(1 + len(sums))},
        scratch_shapes=[pltpu.VMEM((tokens, width), F32), pltpu.VMEM((tokens, width), BF16), pltpu.SemaphoreType.DMA],
        compiler_params=params(8),
        cost_estimate=LIGHT,
        name="layer_backward",
    )(flag, *given, held, state, *sums, *waits)


def weight_kernel(plan, facts, sums, state, *refs):
    halves = refs[-2:]
    width, run = plan.width, plan.micros * plan.tokens
    part = width // GROUPS

    def value_of(name, block=0):
        at = plan.spans[name].start + block * width
        return state[:, :, at : at + width].reshape(run, width)

    def put(half, grad, groups, row, rows):
        grad = grad.astype(BF16)
        for index, group in enumerate(groups):
            source = grad[index * rows : (index + 1) * rows] if grad.shape[0] > rows else grad
            halves[half][facts[0, SPOT + group], row : row + rows] = source

    everyone = range(GROUPS)
    small = sums[0]
    for micro in range(1, plan.micros):
        small = small + sums[micro]
    for half in range(2):
        put(half, small, everyone, 6 * part, SMALL_ROWS)
    left = value_of("normed_one").T
    put(0, dot(left, value_of("q")), everyone, 0, part)
    put(0, dot(left, value_of("k")), everyone, part, part)
    put(1, dot(left, value_of("v")), everyone, 0, part)
    put(1, dot(value_of("mixed").T, value_of("r1")), everyone, part, part)
    left = value_of("normed_two").T
    for block in range(plan.blocks):
        put(0, dot(left, value_of("slope", block)), everyone, (2 + block) * part, part)
    right = value_of("upstream")
    of_block = GROUPS // plan.blocks
    for block in range(plan.blocks):
        groups = range(block * of_block, (block + 1) * of_block)
        put(1, dot(value_of("act", block).T, right), groups, 2 * part, 4 * part)


def weight_call(plan, facts, state, sums, waits=()):
    width = plan.width
    shape = (GROUPS, 6 * width // GROUPS + SMALL_ROWS, width)
    run = plan.micros * plan.tokens
    return pl.pallas_call(
        functools.partial(weight_kernel, plan),
        out_shape=(pltpu.VMEM(shape, BF16), pltpu.VMEM(shape, BF16)),
        in_specs=[SMEM, VMEM, VMEM] + [ANY] * len(waits),
        out_specs=(VMEM, VMEM),
        compiler_params=params(8),
        cost_estimate=LIGHT,
        name="weight_grads",
    )(facts, sums, state, *waits)


def halves_kernel(facts, *refs):
    inputs, outs, landed, (whole, sems) = refs[:10], refs[10:16], refs[16:26], refs[26:]
    copies = [pltpu.make_async_copy(source, target, sems.at[i]) for i, (source, target) in enumerate(zip(inputs, landed))]
    for copy in copies:
        copy.start()
    w_qkv, w_out, w_up, w_down, *vectors = landed
    part, width = w_out.shape[1:]
    for copy in copies[4:]:
        copy.wait()
    lane = lax.broadcasted_iota(jnp.int32, (1, width), 1)
    rows = []
    for vector in vectors:
        size = vector.shape[1]
        spread = jnp.concatenate([vector[...]] * (width // size), axis=1)
        for row in range(size * GROUPS // width):
            rows.append(jnp.where((lane + row * width) // size == facts[0, PLACE], spread, 0.0))
    rows.append(jnp.zeros((SMALL_ROWS - len(rows), width), F32))
    small = jnp.concatenate(rows, axis=0).astype(BF16)
    first, second = whole.at[0], whole.at[1]
    first[6 * part :] = small
    second[6 * part :] = small
    copies[0].wait()
    for i in range(2):
        first[i * part : (i + 1) * part] = w_qkv[0, :, i * width : (i + 1) * width].astype(BF16)
    second[:part] = w_qkv[0, :, 2 * width :].astype(BF16)
    copies[1].wait()
    second[part : 2 * part] = w_out[0].astype(BF16)
    copies[2].wait()
    for i in range(w_up.shape[2] // width):
        first[(2 + i) * part : (3 + i) * part] = w_up[0, :, i * width : (i + 1) * width].astype(BF16)
    copies[3].wait()
    second[2 * part : 6 * part] = w_down[0].astype(BF16)
    cut = outs[0].shape[0]
    for i, rows in enumerate((slice(0, cut), slice(cut, None))):
        outs[i][...] = first[rows]
        outs[2 + i][...] = second[rows]
        outs[4 + i][...] = whole[1 - facts[0, CORE], rows]


def halves_call(facts, matrices, vectors, cut):
    _, part, width = matrices[1].shape
    rows = 6 * part + SMALL_ROWS
    shapes = [pltpu.VMEM((size, width), BF16) for size in (cut, rows - cut)]
    inputs = (*matrices, *vectors)
    outs = pl.pallas_call(
        halves_kernel,
        out_shape=(*shapes, *shapes, *shapes),
        in_specs=[SMEM] + [ANY] * len(inputs),
        out_specs=tuple([VMEM] * 6),
        scratch_shapes=[pltpu.VMEM(value.shape, F32) for value in inputs]
        + [pltpu.VMEM((2, rows, width), BF16), pltpu.SemaphoreType.DMA((len(inputs),))],
        compiler_params=params(8),
        cost_estimate=LIGHT,
        name="round_shard",
    )(facts, *in_hbm(inputs))
    return outs[:2], outs[2:4], outs[4:]


def assemble_kernel(facts, mine, theirs, *refs):
    out, token, landed, wide, sems = refs[-5:]
    token[...] = jnp.zeros_like(token)
    copies = [pltpu.make_async_copy(source, landed.at[i], sems.at[i]) for i, source in enumerate((mine, theirs))]
    for copy in copies:
        copy.start()
    saves = []
    for i, copy in enumerate(copies):
        copy.wait()
        wide[i] = landed[i].astype(F32)
        half = facts[0, CORE] if i == 0 else 1 - facts[0, CORE]
        saves.append(pltpu.make_async_copy(wide.at[i], out.at[half], sems.at[2 + i]))
        saves[-1].start()
    for copy in saves:
        copy.wait()


def assemble(facts, mine, theirs, waits):
    rows, width = mine.shape
    return pl.pallas_call(
        assemble_kernel,
        out_shape=(pltpu.HBM((2, rows, width), F32), pltpu.VMEM((8, 128), F32)),
        in_specs=[SMEM] + [ANY] * (2 + len(waits)),
        out_specs=(ANY, VMEM),
        scratch_shapes=[
            pltpu.VMEM((2, rows, width), BF16),
            pltpu.VMEM((2, rows, width), F32),
            pltpu.SemaphoreType.DMA((4,)),
        ],
        compiler_params=params(6),
        cost_estimate=STEP,
        name="assemble",
    )(facts, mine, theirs, *waits)


def unpack_kernel(counts, facts, *refs):
    total = 4 * sum(counts)
    options, outs, (landed, sems) = refs[:total], refs[total : total + 10], refs[total + 10 :]
    grad_qkv, grad_out, grad_up, grad_down, *vectors = outs
    for section in range(4):

        @pl.when(facts[0, STAGE] * 2 + facts[0, CORE] == section)
        def _():
            for half, count in enumerate(counts):
                row = 0
                for i in range(count):
                    source = options[4 * (sum(counts[:half]) + i) + section]
                    target = landed.at[half, pl.ds(row, source.shape[0])]
                    pltpu.make_async_copy(source, target, sems.at[half]).start()
                    row += source.shape[0]

    for half in range(2):
        pltpu.make_async_copy(landed.at[half], landed.at[half], sems.at[half]).wait()
    part, width = grad_out.shape[1:]
    block = lambda half, first, count=1: landed[half, first * part : (first + count) * part].astype(F32)
    grad_qkv[0, :, :width] = block(0, 0)
    grad_qkv[0, :, width : 2 * width] = block(0, 1)
    grad_qkv[0, :, 2 * width :] = block(1, 0)
    grad_out[0] = block(1, 1)
    for i in range(grad_up.shape[2] // width):
        grad_up[0, :, i * width : (i + 1) * width] = block(0, 2 + i)
    grad_down[0] = block(1, 2, 4)
    small = landed[0, 6 * part :].astype(F32)
    for place in range(GROUPS):

        @pl.when(facts[0, PLACE] == place)
        def _():
            row = 0
            for vector in vectors:
                size = vector.shape[1]
                first = row * width + place * size
                lanes = first % width
                vector[...] = small[first // width : first // width + 1, lanes : lanes + size]
                row += size * GROUPS // width


def unpack(facts, first, second, shapes):
    given = [option for parts in (first, second) for options in parts for option in options]
    rows = sum(options[0].shape[0] for options in first)
    return pl.pallas_call(
        functools.partial(unpack_kernel, (len(first), len(second))),
        out_shape=tuple(jax.ShapeDtypeStruct(shape, F32) for shape in shapes),
        in_specs=[SMEM] + [ANY] * len(given),
        out_specs=tuple([VMEM] * len(shapes)),
        scratch_shapes=[pltpu.VMEM((2, rows, first[0][0].shape[1]), BF16), pltpu.SemaphoreType.DMA((2,))],
        compiler_params=params(8),
        cost_estimate=LIGHT,
        name="unpack",
    )(facts, *given)


CYCLE = (0, 2, 4, 6, 7, 5, 3, 1)
OFFSETS = (0, -1, 1, -2, 2, -3, 3, 4)


def send(value, pairs):
    return lax.ppermute(value, "section", pairs)


def to_core(value):
    return send(value, [(i, i ^ 1) for i in range(4)])


def onward(value):
    return send(value, [(0, 2), (1, 3)])


def backward(value):
    return send(value, [(2, 0), (3, 1)])


def along(value, by):
    size = len(CYCLE)
    return lax.ppermute(value, "dp", [(CYCLE[i], CYCLE[(i + by) % size]) for i in range(size)])


class Ring:
    def __init__(self, piece, low, high, cut):
        self.low, self.high, self.cut = low, high, cut
        self.arrived, self.places = [piece], [(0, low, high)]

    def level(self, *waits):
        if len(self.arrived) > 1:
            ahead, behind = self.arrived[-2:]
            ahead = after(ahead, behind, *waits)
            self.arrived[-2:] = [ahead, after(behind, ahead)]
        return (self.arrived * 2)[-2:]

    def step(self, *waits):
        ahead, behind = self.level(*waits)
        self.arrived += along(ahead, 1), along(behind, -1)
        self.places += [(len(self.places) + i, self.low, self.high) for i in range(2)]

    def last_step(self, *waits):
        ahead, behind = self.level(*waits)
        if self.cut == self.high:
            self.arrived.append(along(ahead, 1))
            self.places.append((7, self.low, self.high))
        else:
            self.arrived.append(along(behind, -1))
            self.places.append((7, self.low, self.high))


def advance(rings):
    ahead = ()
    for ring in rings:
        before = ring.arrived[-2:]
        ring.step(*ahead)
        ahead = (*ahead, *before)


class Gather:
    def __init__(self, facts, rings):
        self.facts, self.rings, self.done, self.held = facts, rings, 0, None

    def lay_out(self, count, *waits):
        span = slice(self.done, count)
        pieces = [piece for ring in self.rings for piece in ring.arrived[span]]
        places = tuple(place for ring in self.rings for place in ring.places[span])
        self.done = count
        self.held = gather_call(self.facts, places, pieces, [to_core(piece) for piece in pieces], self.held, waits)
        return self.held


class Scatter:
    def __init__(self, held, own, far_way):
        self.held, self.own, self.far_way, self.next, self.arrived = held, own, far_way, 4, {}

    def step(self, *waits):
        step, at = self.next, lambda offset: OFFSETS.index(offset) - 1
        if step == 4:
            ways = [(self.far_way, at(4))]
        elif step:
            ways = [(1, at(step)), (-1, at(-step))]
        else:
            ways = [(0, 0)]
        arrived = list(self.arrived.items())
        sums = tuple((block, tuple(i for i, (came, _) in enumerate(arrived) if not way or came == way)) for way, block in ways)
        parts = ring_add(self.held if step else self.own, [part for _, part in arrived], sums, waits)
        self.next -= 1
        if step:
            self.arrived = {way: along(part, way) for (way, _), part in zip(ways, parts)}
        else:
            self.total = parts[0]
        return parts[0]


def scatters(core_flag, halves, got, spans, token):
    merged = merge(core_flag, *halves, got, spans, (token,))
    parts = [Scatter(merged[2 * i], merged[2 * i + 1], far_way) for i, far_way in enumerate((1, -1))]
    token = merged[1]
    for each in parts:
        token = each.step(token)
    return parts, token


def facts_table(dp_count):
    ring = dp_count == len(CYCLE)
    table = np.zeros((4, dp_count, 1, FACTS), np.int32)
    for section in range(4):
        for place in range(dp_count):
            facts = table[section, place, 0]
            facts[[CORE, STAGE, PLACE]] = section % 2, section // 2, place
            for i, offset in enumerate(OFFSETS):
                owner = CYCLE[(CYCLE.index(place) + offset) % dp_count] if ring else i
                facts[ORDER + i], facts[SPOT + owner] = owner, i
    return table


def on_device(
    frames_in,
    segment_ids,
    cotangent,
    w_qkv,
    w_out,
    w_up,
    w_down,
    norm1_gain,
    norm1_shift,
    norm2_gain,
    norm2_shift,
    up_bias,
    down_bias,
):
    section = lax.axis_index("section")
    dp_index, dp_count = lax.axis_index("dp"), lax.axis_size("dp")
    rows, frame_count, width = frames_in.shape
    hidden_units = w_up.shape[2]
    own_rows = rows // 2
    tokens = own_rows * frame_count // MICRO
    ring = dp_count == len(CYCLE)
    part = w_qkv.shape[1]
    cut = 3 * width // GROUPS
    plan = Plan(MICRO, tokens, width, hidden_units)

    table = jnp.asarray(facts_table(dp_count))
    facts = lax.dynamic_slice(table, (section, dp_index, 0, 0), (1, 1) + table.shape[2:])[0, 0]

    segments = lax.dynamic_slice_in_dim(segment_ids, section % 2 * own_rows, own_rows, 0).reshape(-1, 128)
    spot = jnp.arange(128, dtype=jnp.int32)
    allowed = (spot[None, :] <= spot[:, None]) & (spot[None, :] // frame_count == spot[:, None] // frame_count)
    allowed = allowed[None] & (segments[:, :, None] == segments[:, None, :])
    bias = jnp.where(allowed, 0.0, -1e30).astype(F32).reshape(MICRO, tokens, 128)
    frames, last_grads = (
        lax.dynamic_slice_in_dim(value, section % 2 * own_rows, own_rows, 0).reshape(MICRO, tokens, width)
        for value in (frames_in, cotangent)
    )
    flags = [jnp.full((8, 128), flag, F32) for flag in (section < 2, section >= 2, section % 2 == 1)]

    matrices = (w_qkv, w_out, w_up, w_down)
    vectors = (norm1_gain, norm1_shift, norm2_gain, norm2_shift, down_bias, up_bias)
    if ring:
        height = 2 * cut + SMALL_ROWS
        one, two, spare = halves_call(facts, matrices, vectors, cut)
        near = [to_core(part_of) for part_of in spare]
        first_parts = [pick(facts, [(one[i], near[i]) * 2])[0] for i in range(2)]
        spans = ((0, cut), (cut, height))
        rings = [Ring(piece, *span, cut) for piece, span in zip(first_parts, spans)]
        second_parts = [pick(facts, [(near[i], two[i]) * 2])[0] for i in range(2)]
        besides = (frames, last_grads, bias, *flags, *second_parts)
        for step in range(3):
            for each in rings:
                each.step(*(besides if step == 1 else ()))
        for each in rings:
            each.last_step()
        last = [each.arrived[-1] for each in rings]
        second_rings = [Ring(after(piece, *last), *span, cut) for piece, span in zip(second_parts, spans)]
        for _ in range(3):
            for each in second_rings:
                each.step()
        gather = Gather(facts, rings)
        gather.lay_out(5)
        token = gather.lay_out(8)
        held = [gather.held]
    else:
        token = facts
        blocks = [w_qkv[0, :, :width], w_qkv[0, :, width : 2 * width]]
        blocks += [w_up[0, :, i * width : (i + 1) * width] for i in range(hidden_units // width)]
        blocks += [w_qkv[0, :, 2 * width :], w_out[0], w_down[0]]
        whole = jnp.concatenate([lax.all_gather(block.astype(BF16), "dp", axis=0, tiled=True) for block in blocks])
        flat = [lax.all_gather(vector[0].astype(BF16), "dp", axis=0, tiled=True) for vector in vectors]
        small = jnp.concatenate(flat + [jnp.zeros(((SMALL_ROWS - 5) * width - hidden_units,), BF16)])
        grouped = lambda low, count: jnp.swapaxes(
            whole[low * width : (low + count) * width].reshape(count, GROUPS, -1, width), 0, 1
        ).reshape(GROUPS, -1, width)
        small = jnp.pad(small.reshape(1, SMALL_ROWS, width), ((0, GROUPS - 1), (0, 0), (0, 0)))
        down = whole[8 * width :].reshape(GROUPS, -1, width)
        value = jnp.stack(
            [jnp.concatenate([grouped(0, 6), small], 1), jnp.concatenate([grouped(6, 2), down, small], 1)]
        )
        got = lax.all_gather(value, "section")
        held = [jnp.where(section < 2, got[i], got[i + 2]) for i in (0, 1)]

    states, sums = [None, None], [None, None]

    def whole_rows(name, token):
        mine, theirs = layer_rows(plan, name, flags[2], states, (token,))
        whole, token = assemble(facts, mine, to_core(theirs), (mine,))
        return whole.reshape(1, rows, frame_count, width), token


    def run_forward(layer, stage, micro, source, token, cost=LIGHT):
        states[layer], low = forward_call(
            plan, flags[stage], micro, source, bias, held[layer], states[layer], (token,), cost
        )
        return low

    def run_backward(layer, stage, micro, source, token):
        states[layer], sums[layer], low = backward_call(
            plan, flags[stage], micro, source, held[layer], states[layer], sums[layer], (token,)
        )
        return low

    token = stage_zero_low = run_forward(0, 0, None, ("slot", frames), token, HEAVY)
    if ring:
        for each in second_rings:
            each.last_step(token)
        gather = Gather(facts, second_rings)
        gather.lay_out(5, token)
        token = gather.lay_out(8)
        held.append(gather.held)
    hops = []
    for micro in range(MICRO):
        token = run_forward(1, 0, micro, ("slot", stage_zero_low), token)
        hops.append(onward(token))
    lows = []
    for micro in range(MICRO):
        token = run_forward(0, 1, micro, ("one", hops[micro]), token)
        lows.append(token)
    token = run_forward(1, 1, None, ("each", *lows), token)
    token = stage_one_back = run_backward(1, 1, None, ("slot", last_grads), token)
    hops = []
    for micro in range(MICRO):
        token = run_backward(0, 1, micro, ("slot", stage_one_back), token)
        hops.append(backward(token))
    lows = []
    for micro in range(MICRO):
        token = run_backward(1, 0, micro, ("one", hops[micro]), token)
        lows.append(token)

    halves = weight_call(plan, facts, states[1], sums[1], (token,))
    totals = [halves]
    if ring:
        give = spare_half(flags[2], *halves, spans)
        got = [to_core(part_of) for part_of in give]
        token = run_backward(0, 0, 0, ("one", lows[0]), give[1])
        second, token = scatters(flags[2], halves, got, spans, token)
        for micro in range(1, MICRO):
            token = run_backward(0, 0, micro, ("one", lows[micro]), token)
        for each in second:
            token = each.step(token)
        halves = weight_call(plan, facts, states[0], sums[0], (token,))
        token = halves[0]
        for each in second:
            token = each.step(token)
        give = spare_half(flags[2], *halves, spans)
        got = [to_core(after(part_of, token)) for part_of in give]
        first, token = scatters(flags[2], halves, got, spans, token)
        for each in second + first + second + first:
            token = each.step(token)
        input_grads, token = whole_rows("grad", token)
        for each in first:
            token = each.step(token)
        outputs, token = whole_rows("result", token)
        for each in first:
            token = each.step(token)
        mine = [(one.total, two.total) for one, two in zip(first, second)]
        is_first = section % 2 == 0
        theirs = [to_core(jnp.where(is_first, two, one)) for one, two in mine]
        grads = unpack(
            facts,
            [(one, other) * 2 for (one, _), other in zip(mine, theirs)],
            [(other, two) * 2 for (_, two), other in zip(mine, theirs)],
            [value.shape for value in matrices + vectors],
        )
        return (outputs, input_grads, *grads[:8], grads[9], grads[8])
    else:
        run_backward(0, 0, None, ("each", *lows), halves[0])
        totals.append(weight_call(plan, facts, states[0], sums[0]))
        (late_one, late_two), (early_one, early_two) = totals
        is_first = section % 2 == 0

        def to_layer(first, second):
            first, second = first.astype(F32), second.astype(F32)
            return jnp.where(is_first, first, second) + to_core(jnp.where(is_first, second, first))

        one, two = to_layer(early_one, late_one), to_layer(early_two, late_two)
        small = lax.psum(one[0, 6 * width // GROUPS :], "dp")
        block = width // GROUPS
        natural = lambda half, low, high: lax.psum_scatter(
            half[:, low * block : high * block].reshape(-1, width), "dp", scatter_dimension=0, tiled=True
        )
        first_grads = [natural(one, i, i + 1) for i in range(6)]
        second_grads = [natural(two, 0, 1), natural(two, 1, 2), natural(two, 2, 6)]
    grad_vectors = [lax.dynamic_slice_in_dim(small[i : i + 1].reshape(-1), dp_index * part, part) for i in range(5)]
    grad_vectors.append(
        lax.dynamic_slice_in_dim(small[5 : 5 + hidden_units // width].reshape(-1), dp_index * 4 * part, 4 * part)
    )
    grad_vectors = [vector[None].astype(F32) for vector in grad_vectors]

    outputs, input_grads = whole_rows("result", small)[0], whole_rows("grad", small)[0]
    return (
        outputs,
        input_grads,
        jnp.concatenate([first_grads[0], first_grads[1], second_grads[0]], axis=1)[None].astype(F32),
        second_grads[1][None].astype(F32),
        jnp.concatenate(first_grads[2:], axis=1)[None].astype(F32),
        second_grads[2][None].astype(F32),
        *grad_vectors[:4],
        grad_vectors[5],
        grad_vectors[4],
    )


def solution(mesh):
    rows = P("dp", None, None)
    matrix, vector = P("section", "dp", None), P("section", "dp")
    result = P("section", "dp", None, None)
    return jax.shard_map(
        on_device,
        mesh=mesh,
        in_specs=(rows, P("dp", None), rows) + (matrix,) * 4 + (vector,) * 6,
        out_specs=(result, result) + (matrix,) * 4 + (vector,) * 6,
        check_vma=False,
    )
```
